128 devices in a mesh: gx: 8 (over z, core), gy: 16 (over y, x).
Axes of the slice: x: 4, y: 4, z: 4, core: 2. Of those that a mesh axis runs over, the one named last changes fastest.
Arguments:
- seed_grad: float32 [3, 64, 128, 128], P(None, 'gx', 'gy'), may hold values from -8 to 8
- modulus: float32 [64, 128, 128], P('gx', 'gy'), may hold values from 0.5 to 4
- lumped_mass: float32 [64, 128, 128], P('gx', 'gy'), may hold values from 0.3 to 3
- pair_dest: int32 [131072, 1], P(('gx', 'gy')), may hold values from 0 to 15; in each aligned block of 1024 rows (0 to 1023, 1024 to 2047, ...) at most 256 rows name the same one
- slave_nodes: int32 [4, 131072], P(None, ('gx', 'gy')), may hold values from 0 to 8191
- slave_weights: float32 [4, 131072], P(None, ('gx', 'gy')), may hold values from 0.2 to 1
- master_nodes: int32 [4, 131072], P(None, ('gx', 'gy')), may hold values from 0 to 8191
- master_weights: float32 [4, 131072], P(None, ('gx', 'gy')), may hold values from 0.2 to 1
- penalty: float32 [131072], P(('gx', 'gy')), may hold values from 0.5 to 4
Outputs:
- adjoint: float32 [3, 64, 128, 128], P(None, 'gx', 'gy')
- residual: float32 [3, 64, 128, 128], P(None, 'gx', 'gy')
The draws below stay inside these ranges and needn't reach their ends.
Inputs may be any that keep to these rules, and one draw needn't show every extreme that they name: `pair_dest`: in the rows of one device at most 256 segments name the same gy index, a bound that some block reaches of them.
All inputs are finite; a program needn't handle non-finite values.
Results may differ from the reference program's by a relative error of at most 0.00021.
Values sent between devices are 32-bit elements; how exact they have to be, the bound alone decides.
A program may use at most 192 MiB of HBM per device.

```python
import math
import jax
import jax.numpy as jnp
import numpy as np
from jax import lax

CX = 8
CY = 8
CZ = 128
SEG_DEV = 1024
ITERS = 2
CAP = 256
NX = 64
NY = 128
SEGMENTS = 131072
N_GX = 8
N_GY = 16


def draw_seed_grad(key, part):
    across = jnp.arange(NY, dtype=jnp.float32) / NY
    scaling = (0.6 + 1.2 * across)[None, None, :, None]
    random_part = jnp.clip(jax.random.normal(key, (3, NX, NY, CZ), jnp.float32), -4.0, 4.0)
    return random_part * scaling


def place_ends(values, key, smallest, largest):
    longest = values.shape.index(max(values.shape))
    spots = []
    for shift in (0, 1):
        where = [jax.random.randint(jax.random.fold_in(key, axis), (), 0, length) for axis, length in enumerate(values.shape)]
        where[longest] = (where[longest] + shift) % values.shape[longest]
        spots.append(tuple(where))
    return values.at[spots[0]].set(smallest).at[spots[1]].set(largest)


def steps_of(own_key, extent, cuts, smallest, largest):
    loudness = 1.0
    for dim, blocks in cuts:
        steps = jax.random.uniform(jax.random.fold_in(jax.random.fold_in(own_key, 6), dim), (blocks,), jnp.float32, smallest / len(cuts), largest / len(cuts))
        loudness = loudness * jnp.repeat(jnp.exp(steps), extent[dim] // blocks).reshape((-1,) + (1,) * (len(extent) - 1 - dim))
    return loudness


def assign_block(key, own, number, rows, count, top, reach, slope):
    sequence = jax.random.permutation(key, count)
    packed, ordinary = load_shares(count, rows * top, reach, slope, True), load_shares(count, rows * top, reach, slope, False)
    places = jnp.arange(count)

    def named(sizes, rotation):
        used = int((sizes > 0).sum())
        fixed = max(1, used // 4)
        passed = fixed + (places - fixed + rotation * (used - fixed)) % max(1, count - fixed)
        return jnp.zeros((count,), jnp.int32).at[sequence[jnp.where(places < fixed, places, passed)]].set(jnp.asarray(sizes, jnp.int32))

    sizes = jnp.where(number % 4 == 0, named(packed, number // 4), named(ordinary, number - number // 4 - 1))
    mixed = jax.random.permutation(jax.random.fold_in(own, 3), count)
    source_of, taker = mixed[0:count // 2 * 2:2], mixed[1:count // 2 * 2:2]
    margin = jnp.minimum(sizes[source_of] - 1, reach - sizes[taker]) // 2
    margin = jnp.where((source_of == sequence[0]) | (taker == sequence[0]) | (sizes[taker] == 0), 0, jnp.maximum(margin, 0))
    passed = jax.random.randint(jax.random.fold_in(own, 4), (count // 2,), 0, 1 << 20) % (margin + 1)
    sizes = sizes.at[source_of].add(-passed).at[taker].add(passed)
    labels = jnp.searchsorted(jnp.cumsum(sizes), jnp.arange(rows * top), side="right").astype(jnp.int32)
    grid = labels.reshape(top, rows).T
    grid = grid[jax.random.permutation(jax.random.fold_in(own, 1), rows)]
    rotation = jax.random.randint(jax.random.fold_in(own, 2), (rows, 1), 0, top)
    return jnp.take_along_axis(grid, (jnp.arange(top)[None, :] + rotation) % top, axis=1)


def load_shares(amount, total, reach, skew, full):
    loads = [(1 << 20) // math.isqrt(standing ** skew) + 1 for standing in range(1, amount + 1)]
    largest = reach if full else min(reach, max(-(-total // amount), total * loads[0] // sum(loads)))
    least = 1 if total - largest >= amount - 1 else 0
    given, spare = [largest] + [least] * (amount - 1), total - largest - least * (amount - 1)
    while spare > 0:
        movable = [i for i in range(1, amount) if given[i] < largest] or [i for i in range(1, amount) if given[i] < reach]
        mass, left = sum([loads[i] for i in movable]), spare
        for i in movable:
            addition = min(reach - given[i], max(1, left * loads[i] // mass), spare)
            given[i] = given[i] + addition
            spare = spare - addition
    return np.array(given)


def setup_inputs(seed: int = 0) -> dict:
    keys = jax.random.split(jax.random.key(seed), 10)
    seed_grad = draw_seed_grad(jax.random.fold_in(keys[9], 71), 0)
    modulus = jnp.clip(jnp.exp(math.log(4.0) - 2.0794415 * jax.random.uniform(keys[1], (NX, NY, CZ), jnp.float32) ** steps_of(keys[1], (NX, NY, CZ), ((0, 8), (1, 16)), -0.2, 0.2)), 0.5, 4.0)
    lumped_mass = jnp.clip(jnp.exp(math.log(3.0) - 2.3025851 * jax.random.uniform(keys[2], (NX, NY, CZ), jnp.float32) ** steps_of(keys[2], (NX, NY, CZ), ((0, 8), (1, 16)), -0.2, 0.2)), 0.3, 3.0)
    pair_dest_keys = jax.random.split(jax.random.fold_in(keys[3], 1), SEGMENTS // SEG_DEV)
    pair_dest_turns = jax.random.permutation(jax.random.fold_in(keys[3], 3), SEGMENTS // SEG_DEV)
    pair_dest = jax.vmap(lambda own, number: assign_block(jax.random.fold_in(keys[3], 2), own, number, SEG_DEV, N_GY, 1, CAP, 2))(pair_dest_keys, pair_dest_turns).reshape((SEGMENTS, 1))
    slave_nodes = place_ends(jax.random.randint(keys[4], (4, SEGMENTS), 0, CX * CY * CZ), jax.random.fold_in(keys[4], 1), 0, (CX * CY * CZ) - 1).astype(jnp.int32)
    slave_weights = jnp.clip(0.2 + 0.8 * jax.random.uniform(keys[5], (4, SEGMENTS), jnp.float32) ** steps_of(keys[5], (4, SEGMENTS), ((1, 128),), -0.2, 0.2), 0.2, 1.0)
    master_nodes = place_ends(jax.random.randint(keys[6], (4, SEGMENTS), 0, CX * CY * CZ), jax.random.fold_in(keys[6], 1), 0, (CX * CY * CZ) - 1).astype(jnp.int32)
    master_weights = jnp.clip(0.2 + 0.8 * jax.random.uniform(keys[7], (4, SEGMENTS), jnp.float32) ** steps_of(keys[7], (4, SEGMENTS), ((1, 128),), -0.2, 0.2), 0.2, 1.0)
    penalty = jnp.clip(jnp.exp(math.log(4.0) - 2.0794415 * jax.random.uniform(keys[8], (SEGMENTS,), jnp.float32) ** steps_of(keys[8], (SEGMENTS,), ((0, 128),), -0.2, 0.2)), 0.5, 4.0)
    return {"seed_grad": seed_grad, "modulus": modulus, "lumped_mass": lumped_mass, "pair_dest": pair_dest, "slave_nodes": slave_nodes, "slave_weights": slave_weights, "master_nodes": master_nodes, "master_weights": master_weights, "penalty": penalty}


shear_ratio = 1.0 / 2.6
lame_ratio = 0.3 / 0.52

def shape_tables():
    abscissa = 1.0 / math.sqrt(3.0)
    points = [(a, b, c) for a in (-abscissa, abscissa) for b in (-abscissa, abscissa) for c in (-abscissa, abscissa)]
    offsets = [(i, j, k) for i in range(3) for j in range(3) for k in range(3) if (i == 1) + (j == 1) + (k == 1) <= 1]
    corners = [(i, j, k) for i in (0, 2) for j in (0, 2) for k in (0, 2)]
    derivative = np.zeros((8, 3, 20))
    trilinear = np.zeros((8, 8))
    for g, location in enumerate(points):
        for n, offset in enumerate(offsets):
            natural = [offset[d] - 1 for d in range(3)]
            factors = [1.0 - location[d] ** 2 if natural[d] == 0 else 1.0 + location[d] * natural[d] for d in range(3)]
            slopes = [-2.0 * location[d] if natural[d] == 0 else float(natural[d]) for d in range(3)]
            linear = location[0] * natural[0] + location[1] * natural[1] + location[2] * natural[2] - 2.0
            for d in range(3):
                others = factors[(d + 1) % 3] * factors[(d + 2) % 3]
                if 0 in natural:
                    derivative[g, d, n] = slopes[d] * others / 4.0
                else:
                    derivative[g, d, n] = natural[d] * others * (linear + factors[d]) / 8.0
        for c, corner in enumerate(corners):
            weight = 1.0
            for d in range(3):
                weight = weight * (1.0 + location[d] * (corner[d] - 1)) / 2.0
            trilinear[g, c] = weight
    return (derivative, trilinear, offsets, corners)

def strided(first, count):
    return slice(first, first + 2 * count - 1, 2)

def gather_nodes(padded, counts, offsets):
    return jnp.stack([padded[:, strided(o[0], counts[0]), strided(o[1], counts[1]), strided(o[2], counts[2])] for o in offsets])

def spread_nodes(values, target_shape, counts, offsets):
    result = jnp.zeros(target_shape, jnp.float32)
    for n, offset in enumerate(offsets):
        result = result.at[:, strided(offset[0], counts[0]), strided(offset[1], counts[1]), strided(offset[2], counts[2])].add(values[n])
    return result

def gauss_moduli(padded_mod, counts, corners, trilinear):
    corner_values = jnp.stack([padded_mod[strided(c[0], counts[0]), strided(c[1], counts[1]), strided(c[2], counts[2])] for c in corners]).reshape(8, -1)
    moduli = jnp.einsum('gc,ce->ge', jnp.asarray(trilinear, jnp.float32), corner_values, precision=lax.Precision.HIGHEST)
    return (moduli * shear_ratio, moduli * lame_ratio)

def element_forces(padded, padded_mod, counts):
    derivative, trilinear, offsets, corners = shape_tables()
    slope_table = jnp.asarray(derivative, jnp.float32)
    shear_modulus, lame_lambda_modulus = gauss_moduli(padded_mod, counts, corners, trilinear)
    stacked = gather_nodes(padded, counts, offsets).reshape(20, -1)
    gradients = jnp.einsum('gan,nm->gam', slope_table, stacked, precision=lax.Precision.HIGHEST).reshape(8, 3, 3, -1)
    dilation = gradients[:, 0, 0] + gradients[:, 1, 1] + gradients[:, 2, 2]
    identity = jnp.eye(3, dtype=jnp.float32)[None, :, :, None]
    stress = shear_modulus[:, None, None] * (gradients + jnp.swapaxes(gradients, 1, 2)) + (lame_lambda_modulus * dilation)[:, None, None] * identity
    forces = jnp.einsum('gan,gam->nm', slope_table, stress.reshape(8, 3, -1), precision=lax.Precision.HIGHEST)
    return spread_nodes(forces.reshape((20, 3) + tuple(counts)), padded.shape, counts, offsets)

def element_diagonal(padded_mod, counts, target_shape):
    derivative, trilinear, offsets, corners = shape_tables()
    slope_table = jnp.asarray(derivative, jnp.float32)
    shear_modulus, lame_lambda_modulus = gauss_moduli(padded_mod, counts, corners, trilinear)
    squared_terms = slope_table * slope_table
    summed_squares = lax.optimization_barrier(jnp.sum(squared_terms, axis=1))
    first_part = jnp.einsum('gn,ge->ne', summed_squares, shear_modulus, precision=lax.Precision.HIGHEST)
    second_share = jnp.einsum('rtc,ry->cty', squared_terms, shear_modulus + lame_lambda_modulus, precision=lax.Precision.HIGHEST)
    values = first_part[:, None, :] + second_share
    return spread_nodes(values.reshape((20, 3) + tuple(counts)), target_shape, counts, offsets)

def reference(seed_grad, modulus, lumped_mass, pair_dest, slave_nodes, slave_weights, master_nodes, master_weights, penalty):
    row_count = NX // 2 + 1
    counts_row = (1, NY // 2 + 1, CZ // 2)
    padded_shape = (3, NX + 4, NY + 4, CZ + 1)
    slab_shape = (3, 3, NY + 4, CZ + 1)
    padded_mod = jnp.pad(modulus, ((2, 2), (2, 2), (0, 1)))
    anchor = jnp.int32(0)

    def over_rows(make_slab):

        def add_row(m, summed):
            row_start = (m * 2).astype(jnp.int32)
            current = lax.dynamic_slice(summed, (anchor, row_start, anchor, anchor), slab_shape)
            return lax.dynamic_update_slice(summed, current + make_slab(row_start), (anchor, row_start, anchor, anchor))
        summed = lax.fori_loop(0, row_count, add_row, jnp.zeros(padded_shape, jnp.float32))
        return summed[:, 2:2 + NX, 2:2 + NY, :CZ]

    def modulus_slab(row_start):
        return lax.dynamic_slice(padded_mod, (row_start, anchor, anchor), (3, NY + 4, CZ + 1))
    diagonal = over_rows(lambda row_start: element_diagonal(modulus_slab(row_start), counts_row, slab_shape)) + lumped_mass
    node_count = CX * CY * CZ
    owner_block = jnp.arange(SEGMENTS, dtype=jnp.int32) // SEG_DEV
    block_x = owner_block // N_GY
    slave_flat = owner_block[None, :] * node_count + slave_nodes
    master_flat = (block_x * N_GY + pair_dest[:, 0])[None, :] * node_count + master_nodes

    def to_blocks(field):
        return field.reshape(3, N_GX, CX, N_GY, CY, CZ).transpose(0, 1, 3, 2, 4, 5).reshape(3, -1)

    def from_blocks(flattened):
        return flattened.reshape(3, N_GX, N_GY, CX, CY, CZ).transpose(0, 1, 3, 2, 4, 5).reshape(3, NX, NY, CZ)

    def contact(field):
        flattened = to_blocks(field)
        slave_part = lax.optimization_barrier(jnp.sum(flattened[:, slave_flat] * slave_weights[None], axis=1))
        master_surface_share = lax.optimization_barrier(jnp.sum(flattened[:, master_flat] * master_weights[None], axis=1))
        contact_traction = penalty[None, :] * (slave_part - master_surface_share)
        result = jnp.zeros_like(flattened)
        result = result.at[:, slave_flat].add(slave_weights[None] * contact_traction[:, None, :])
        result = result.at[:, master_flat].add(-master_weights[None] * contact_traction[:, None, :])
        return from_blocks(result)

    def apply_matrix(field):
        padded_field = jnp.pad(field, ((0, 0), (2, 2), (2, 2), (0, 1)))
        elastic = over_rows(lambda row_start: element_forces(lax.dynamic_slice(padded_field, (anchor, row_start, anchor, anchor), slab_shape), modulus_slab(row_start), counts_row))
        return elastic + lumped_mass * field + contact(field)
    adjoint = jnp.zeros_like(seed_grad)
    residual = seed_grad
    precond = residual / diagonal
    direction = precond
    precond_dot = jnp.sum(residual * precond)
    for iteration in range(ITERS):
        applied = apply_matrix(direction)
        step_size = precond_dot / jnp.sum(direction * applied)
        adjoint = adjoint + step_size * direction
        residual = residual - step_size * applied
        if iteration + 1 < ITERS:
            precond = residual / diagonal
            new_dot = jnp.sum(residual * precond)
            direction = precond + new_dot / precond_dot * direction
            precond_dot = new_dot
    return (adjoint, residual)
```

```python
import functools
import math

import jax
import jax.numpy as jnp
import numpy as np
from jax import lax
from jax.experimental import pallas as pl
from jax.experimental.pallas import tpu as pltpu
from jax.sharding import PartitionSpec as P

CAP = 256
SHEAR = 1.0 / 2.6
LAME = 0.3 / 0.52
MESH = pl.DeviceIdType.MESH
F32 = jnp.float32
BF16 = jnp.bfloat16
VMEM = pl.BlockSpec(memory_space=pltpu.VMEM)
LIMIT = 40 * 1024 * 1024

WIDE = 72


def shape_tables():
    abscissa = 1.0 / math.sqrt(3.0)
    points = [
        (a, b, c)
        for a in (-abscissa, abscissa)
        for b in (-abscissa, abscissa)
        for c in (-abscissa, abscissa)
    ]
    offsets = [
        (i, j, k)
        for i in range(3)
        for j in range(3)
        for k in range(3)
        if (i == 1) + (j == 1) + (k == 1) <= 1
    ]
    derivative = np.zeros((8, 3, 20))
    for g, location in enumerate(points):
        for n, offset in enumerate(offsets):
            natural = [offset[d] - 1 for d in range(3)]
            factors = [
                1.0 - location[d] ** 2 if natural[d] == 0 else 1.0 + location[d] * natural[d]
                for d in range(3)
            ]
            slopes = [
                -2.0 * location[d] if natural[d] == 0 else float(natural[d]) for d in range(3)
            ]
            linear = sum(location[d] * natural[d] for d in range(3)) - 2.0
            for d in range(3):
                others = factors[(d + 1) % 3] * factors[(d + 2) % 3]
                if 0 in natural:
                    derivative[g, d, n] = slopes[d] * others / 4.0
                else:
                    derivative[g, d, n] = natural[d] * others * (linear + factors[d]) / 8.0
    return derivative, offsets


def signs(count, dims):
    table = np.ones((count, count))
    for t in range(count):
        for c in range(count):
            for d in range(dims):
                if t >> d & 1 and not c >> d & 1:
                    table[t, c] = -table[t, c]
    return table


def element_tables():
    derivative, offsets = shape_tables()
    eight, four = signs(8, 3), signs(4, 2)
    modal = np.einsum("sg,gan->asn", eight, derivative) / 8.0
    corner_at = [offsets.index((c >> 2 << 1, (c >> 1 & 1) << 1, (c & 1) << 1)) for c in range(8)]
    edge_at = []
    for d in range(3):
        row = []
        for c in range(4):
            offset = [(c >> 1) << 1, (c & 1) << 1]
            offset.insert(d, 1)
            row.append(offsets.index(tuple(offset)))
        edge_at.append(row)
    corner_terms = np.einsum("tn,asn->ast", eight, modal[:, :, corner_at]) / 8.0
    edge_terms = [np.einsum("tn,asn->ast", four, modal[:, :, edge_at[d]]) / 4.0 for d in range(3)]
    trilinear = np.array([(1.0 / math.sqrt(3.0)) ** bin(t).count("1") / 8.0 for t in range(8)])
    at_points = np.einsum("t,tg->gt", trilinear, eight)
    squares = derivative * derivative
    weight = np.einsum(
        "gt,gni->tni",
        at_points,
        SHEAR * squares.sum(axis=1)[:, :, None] + (LAME + SHEAR) * np.swapaxes(squares, 1, 2),
    )
    corner_diag = np.einsum("un,tni->uti", eight, weight[:, corner_at]) / 8.0
    edge_diag = [np.einsum("un,tni->uti", four, weight[:, edge_at[d]]) / 4.0 for d in range(3)]
    return corner_terms, edge_terms, trilinear, corner_diag, edge_diag


def split_sums(values):
    values = list(values)
    step = 1
    while step < len(values):
        for low in range(len(values)):
            if not low & step:
                a, b = values[low], values[low | step]
                values[low], values[low | step] = b + a, b - a
        step *= 2
    return values


def join_sums(values):
    values = list(values)
    step = 1
    while step < len(values):
        for low in range(len(values)):
            if not low & step:
                a, b = values[low], values[low | step]
                values[low], values[low | step] = a - b, a + b
        step *= 2
    return values


def combine(terms):
    total = None
    for factor, value in terms:
        if abs(factor) < 1e-12:
            continue
        term = value * np.float32(factor)
        total = term if total is None else total + term
    return total


def lanes(rows):
    return lax.broadcasted_iota(jnp.int32, (rows, 128), 1)


def shift_down(value):
    return jnp.where(lanes(value.shape[0]) == 63, 0.0, pltpu.roll(value, 127, 1))


def collect(low, middle, high):
    total = low + jnp.where(lanes(8) < 64, pltpu.roll(high, 1, 1), 0.0)
    if middle is not None:
        total = total + pltpu.roll(middle, 64, 1)
    return total


def corner_moduli(wide_mod, wide_mod_up, group):
    values = []
    for c in range(8):
        ref = wide_mod_up if c & 1 else wide_mod
        values.append(ref[pl.ds(8 * (group + (c >> 2)) + (c >> 1 & 1), 8), :])
    inside = lanes(8) < 64
    return split_sums([jnp.where(inside, value, 0.0) for value in values])


def edge_corner(d, c):
    where = [c >> 1, c & 1]
    where.insert(d, None)
    return where


def add_rows(ref, index, row, value):
    ref[index + (pl.ds(row, 8), slice(None))] += value


def scatter_forces(out, i, corner, edges, group):
    for xy in range(4):
        row = 8 * (group + (xy >> 1)) + (xy & 1)
        add_rows(out, (i, 0), row, collect(corner[2 * xy], edges[2][xy], corner[2 * xy + 1]))
    for y in range(2):
        add_rows(out, (i, 2), 8 * group + y, collect(edges[0][2 * y], None, edges[0][2 * y + 1]))
    for x in range(2):
        add_rows(
            out, (i, 1), 8 * (group + x), collect(edges[1][2 * x], None, edges[1][2 * x + 1])
        )


def diagonal_into(out, wide_mod, wide_mod_up):
    corner_diag, edge_diag = element_tables()[3:]
    out[...] = jnp.zeros_like(out)
    for group in range(7):
        moduli = corner_moduli(wide_mod, wide_mod_up, group)
        for i in range(3):
            corner = join_sums(
                [
                    combine([(corner_diag[u, t, i], moduli[t]) for t in range(8)])
                    for u in range(8)
                ]
            )
            edges = [
                join_sums(
                    [
                        combine([(edge_diag[d][u, t, i], moduli[t]) for t in range(8)])
                        for u in range(4)
                    ]
                )
                for d in range(3)
            ]
            scatter_forces(out, i, corner, edges, group)


def stiffness_into(out, wide, wide_up, wide_mid, wide_mod, wide_mod_up):
    corner_terms, edge_terms, trilinear = element_tables()[:3]
    out[...] = jnp.zeros_like(out)
    for group in range(1, 6):
        moduli = corner_moduli(wide_mod, wide_mod_up, group)
        points = join_sums([moduli[t] * np.float32(trilinear[t]) for t in range(8)])
        slopes = []
        for i in range(3):
            corner = []
            for c in range(8):
                ref = wide_up if c & 1 else wide
                corner.append(ref[i, 0, pl.ds(8 * (group + (c >> 2)) + (c >> 1 & 1), 8), :])
            corner = split_sums(corner)
            edges = []
            for d in range(3):
                values = []
                for c in range(4):
                    x, y, z = edge_corner(d, c)
                    row = 8 * (group + (x or 0)) + (y or 0)
                    parity = (2, 1, 0)[d]
                    if d == 2:
                        values.append(wide_mid[i, pl.ds(row, 8), :])
                    else:
                        values.append((wide_up if z else wide)[i, parity, pl.ds(row, 8), :])
                edges.append(split_sums(values))
            slopes.append(
                [
                    [
                        combine(
                            [(corner_terms[a, s, t], corner[t]) for t in range(8)]
                            + [
                                (edge_terms[d][a, s, t], edges[d][t])
                                for d in range(3)
                                for t in range(4)
                            ]
                        )
                        for s in range(8)
                    ]
                    for a in range(3)
                ]
            )

        def plus(a, b):
            return a if b is None else b if a is None else a + b

        zero = jnp.zeros((8, 128), F32)
        strain = {}
        for a in range(3):
            strain[a, a] = slopes[a][a]
            for b in range(a):
                strain[b, a] = [plus(p, q) for p, q in zip(slopes[a][b], slopes[b][a])]
        strain = {
            key: join_sums([zero if v is None else v for v in value])
            for key, value in strain.items()
        }
        stress = {key: [] for key in strain}
        for g in range(8):
            volume = (strain[0, 0][g] + strain[1, 1][g] + strain[2, 2][g]) * np.float32(LAME)
            for a in range(3):
                stress[a, a].append(
                    points[g] * (volume + strain[a, a][g] * np.float32(2.0 * SHEAR))
                )
            scaled = points[g] * np.float32(SHEAR)
            for key in ((0, 1), (0, 2), (1, 2)):
                stress[key].append(scaled * strain[key][g])
        stress = {key: split_sums(value) for key, value in stress.items()}
        for i in range(3):
            pairs = [
                (a, s, stress[min(a, i), max(a, i)][s]) for a in range(3) for s in range(8)
            ]
            corner = join_sums(
                [combine([(corner_terms[a, s, t], v) for a, s, v in pairs]) for t in range(8)]
            )
            edges = [
                join_sums(
                    [combine([(edge_terms[d][a, s, t], v) for a, s, v in pairs]) for t in range(4)]
                )
                for d in range(3)
            ]
            scatter_forces(out, i, corner, edges, group)


def lift(wide, wide_up, wide_mid):
    for i in range(3):
        for parity in range(3):
            wide_up[i, parity] = shift_down(wide[i, parity])
        wide_mid[i] = pltpu.roll(wide[i, 0], 64, 1)


def halo_plan(fields, with_modulus):
    plan, first = [], 0
    for dx in (-1, 0, 1):
        for dy in (-1, 0, 1):
            if dx == 0 and dy == 0:
                continue
            pieces = []

            def places(step, both):
                if step == 1:
                    return [(p, 3, 1) for p in ((0, 1) if both else (0,))]
                return [(0, 0, 6)]

            def strips(array, xs, ys):
                for px, ox, wx in xs:
                    for py, oy, wy in ys:
                        if ox is None:
                            pieces.append((array, px * 2 + py, oy, 4, 4, 8 * 2 + wy, 8))
                        elif oy is None:
                            pieces.append((array, px * 2 + py, 4 * ox, 4, 1, 8 * wx + 2, 1))
                        else:
                            pieces.append((array, px * 2 + py, 4 * ox + oy, 1, 1, 8 * wx + wy, 1))

            every = [(0, None, None), (1, None, None)]
            for array in range(fields):
                strips(
                    array,
                    every if dx == 0 else places(dx, True),
                    every if dy == 0 else places(dy, True),
                )
            if with_modulus:
                deep = {1: [(0, 3, 1), (0, 2, 0)], -1: [(0, 0, 6), (0, 1, 7)], 0: every[:1]}
                strips(fields, deep[dx], deep[dy])
            rows = sum(piece[3] for piece in pieces)
            plan.append((dx, dy, first, -(-rows // 8) * 8, pieces))
            first += plan[-1][3]
    return plan, first


FIRST_PLAN, FIRST_ROWS = halo_plan(4, True)
NEXT_PLAN, NEXT_ROWS = halo_plan(3, False)


def rows_of(start, count, stride):
    return pl.ds(start, count) if stride == 1 else pl.ds(start, count, stride=stride)


def pack_halo(plan, own, message):
    message[...] = jnp.zeros_like(message)
    for _, _, first, _, pieces in plan:
        at = first
        for array, parity, start, count, stride, _, _ in pieces:
            source = own[rows_of(array * 64 + parity * 16 + start, count, stride), :]
            message[pl.ds(at, count), :] = source
            at += count


def unpack_halo(plan, extents, message, store):
    gx, gy = lax.axis_index("gx"), lax.axis_index("gy")
    for dx, dy, first, _, pieces in plan:
        inside = None
        for step, at, extent in ((dx, gx, extents[0]), (dy, gy, extents[1])):
            if step:
                here = at > 0 if step == 1 else at < extent - 1
                inside = here if inside is None else jnp.logical_and(inside, here)
        keep = jnp.where(inside, 1.0, 0.0).astype(F32)
        at = first
        for array, parity, _, count, _, start, stride in pieces:
            store(array, parity, start, count, stride, message[pl.ds(at, count), :] * keep)
            at += count


def widen_own(own, array, wide, i):
    for parity in range(4):
        for x in range(4):
            wide[i, parity, pl.ds(8 * (x + 2) + 2, 4), :] = own[
                pl.ds(array * 64 + parity * 16 + 4 * x, 4), :
            ]


def narrow(wide, i, own, array):
    for parity in range(4):
        for x in range(4):
            own[pl.ds(array * 64 + parity * 16 + 4 * x, 4), :] = wide[
                i, parity, pl.ds(8 * (x + 2) + 2, 4), :
            ]


def in_two(value):
    head = value.astype(BF16)
    return head, (value - head.astype(F32)).astype(BF16)


def down_iota(rows, columns):
    return lax.broadcasted_iota(jnp.int32, (rows, columns), 0).astype(F32).astype(BF16)


def ones_where(rows, labels):
    columns = labels.shape[1]
    return jnp.where(
        down_iota(rows, columns) == labels.astype(BF16), jnp.ones((), BF16), jnp.zeros((), BF16)
    )


def dot(a, b, transposed=False):
    return lax.dot_general(
        a, b, (((1,), (1 if transposed else 0,)), ((), ())), preferred_element_type=F32
    )


def gather_chunk(table, row, lane, weight):
    picks = jnp.concatenate([ones_where(128, lane[j : j + 1]) for j in range(4)], axis=1)
    found = dot(table, jnp.concatenate([picks, picks], axis=0))
    down = lax.broadcasted_iota(jnp.int32, (64, 128), 0).astype(F32)
    factors = [jnp.where(down == row[j : j + 1], weight[j : j + 1], 0.0) for j in range(4)]
    result = []
    for i in range(3):
        total = sum(
            factors[j] * found[64 * i : 64 * (i + 1), 128 * j : 128 * (j + 1)] for j in range(4)
        )
        result.append(jnp.sum(total, axis=0, keepdims=True))
    return jnp.concatenate(result, axis=0)


def scatter_chunk(row, lane, weight, traction):
    picks = jnp.concatenate([ones_where(128, lane[j : j + 1]) for j in range(4)], axis=1)
    rows = [ones_where(64, row[j : j + 1]) for j in range(4)]
    left = []
    parts = [
        [in_two(weight[j : j + 1] * traction[i : i + 1]) for j in range(4)] for i in range(3)
    ]
    for part in range(2):
        for i in range(3):
            left.append(
                jnp.concatenate([rows[j] * parts[i][j][part] for j in range(4)], axis=1)
            )
    return dot(jnp.concatenate(left, axis=0), picks, True)


def table_of(value):
    head, tail = in_two(value)
    return jnp.concatenate([head, tail], axis=1)


def gather_all(table, segments, bundle, mine, theirs, places, group):
    mine[...] = jnp.zeros_like(mine)

    def slave(k, _):
        at = pl.ds(pl.multiple_of(k * 128, 128), 128)
        block = segments[:, at]
        mine[0:3, at] = gather_chunk(table, block[8:12], block[12:16], block[0:4])
        return _

    lax.fori_loop(0, segments.shape[1] // 128, slave, 0)
    head, tail = in_two(mine[...])
    both = jnp.concatenate([head, tail], axis=0)
    target = segments[5:6, :]
    left = jnp.concatenate(
        [jnp.where(target == t, 1.0, 0.0).astype(BF16) * both for t in range(group)], axis=0
    )
    placed = dot(left, places[...], True).reshape(group, 16, CAP)
    theirs[...] = placed[:, 0:8] + placed[:, 8:16]

    def master(source, _):
        for half in range(CAP // 128):
            at = slice(128 * half, 128 * (half + 1))
            block = bundle[source, :, at]

            @pl.when(jnp.max(block[4:5]) > 0.0)
            def _work():
                theirs[source, 3:6, at] = gather_chunk(
                    table, block[8:12], block[12:16], block[0:4]
                )

        return _

    lax.fori_loop(0, group, master, 0)


def scatter_all(total, segments, bundle, mine, sent, arrived, places, pulls, group):
    head, tail = in_two(arrived[...].reshape(group * 8, CAP))
    returned = dot(
        jnp.concatenate([head, tail], axis=1), jnp.concatenate([places[...], places[...]], axis=0)
    )
    target = segments[5:6, :]
    back = sum(
        jnp.where(target == t, 1.0, 0.0) * returned[8 * t : 8 * (t + 1)] for t in range(group)
    )
    pulls[0:3, :] = segments[4:5, :] * (mine[0:3, :] - back[3:6, :])
    total[...] = jnp.zeros_like(total)

    def slave(k, _):
        at = pl.ds(pl.multiple_of(k * 128, 128), 128)
        block = segments[:, at]
        total[...] += scatter_chunk(block[8:12], block[12:16], block[0:4], pulls[0:3, at])
        return _

    lax.fori_loop(0, segments.shape[1] // 128, slave, 0)

    def master(source, _):
        for half in range(CAP // 128):
            at = slice(128 * half, 128 * (half + 1))
            block = bundle[source, :, at]

            @pl.when(jnp.max(block[4:5]) > 0.0)
            def _work():
                traction = block[4:5] * (sent[source, 3:6, at] - arrived[source, 0:3, at])
                total[...] += scatter_chunk(block[8:12], block[12:16], block[0:4], traction)

        return _

    lax.fori_loop(0, group, master, 0)


def swap_lanes(forth):
    a = lax.broadcasted_iota(jnp.int32, (128, 128), 0 if forth else 1)
    b = lax.broadcasted_iota(jnp.int32, (128, 128), 1 if forth else 0)
    return jnp.where(b == (a % 2) * 64 + a // 2, 1.0, 0.0).astype(F32)


def exact_dot(a, b):
    return lax.dot_general(
        a,
        b,
        (((1,), (0,)), ((), ())),
        precision=lax.Precision.HIGHEST,
        preferred_element_type=F32,
    )


def prepare_kernel(
    group,
    seed,
    modulus,
    mass,
    pair,
    slave_nodes,
    slave_weights,
    master_nodes,
    master_weights,
    penalty,
    own,
    message,
    packed,
    segments,
    places,
    swapped,
):
    swap = swap_lanes(True)
    for i in range(3):
        swapped[i] = exact_dot(seed[i].reshape(64, 128), swap).reshape(8, 8, 128)
    swapped[3] = exact_dot(mass[...].reshape(64, 128), swap).reshape(8, 8, 128)
    swapped[4] = exact_dot(modulus[...].reshape(64, 128), swap).reshape(8, 8, 128)
    for array in range(5):
        for x in range(8):
            for py in range(2):
                row = array * 64 + (x % 2 * 2 + py) * 16 + x // 2 * 4
                own[pl.ds(row, 4), :] = swapped[array, x, pl.ds(py, 4, stride=2), :]
    pack_halo(FIRST_PLAN, own, message)

    def place_of(node):
        x, y, z = node // 1024, node // 128 % 8, node % 128
        row = (x % 2 * 2 + y % 2) * 16 + x // 2 * 4 + y // 2
        return row.astype(F32), (z % 2 * 64 + z // 2).astype(F32)

    slave_row, slave_lane = place_of(slave_nodes[...])
    master_row, master_lane = place_of(master_nodes[...])
    target = pair[...].astype(F32)
    count = target.shape[1]
    chosen = ones_where(group, target)
    a = lax.broadcasted_iota(jnp.int32, (128, 128), 0)
    b = lax.broadcasted_iota(jnp.int32, (128, 128), 1)
    before = jnp.where(a < b, 1.0, 0.0).astype(BF16)
    ranks, base = [], jnp.zeros((group, 1), F32)
    for k in range(count // 128):
        part = chosen[:, 128 * k : 128 * (k + 1)]
        wide = part.astype(F32)
        rank = dot(part, before) + base
        ranks.append(jnp.sum(rank * wide, axis=0, keepdims=True))
        base = base + jnp.sum(wide, axis=1, keepdims=True)
    position = jnp.concatenate(ranks, axis=1)
    segments[0:4, :] = slave_weights[...]
    segments[4:5, :] = penalty[...]
    segments[5:6, :] = target
    segments[6:7, :] = position
    segments[7:8, :] = jnp.zeros_like(position)
    segments[8:12, :] = slave_row
    segments[12:16, :] = slave_lane
    spots = ones_where(CAP, position)
    places[...] = spots
    nothing = jnp.zeros((3, count), F32)
    values = jnp.concatenate([master_weights[...], penalty[...], nothing], axis=0)
    head, tail = in_two(values)
    nodes = jnp.concatenate([master_row, master_lane], axis=0)
    sent = jnp.concatenate([head, tail, nodes.astype(BF16), jnp.zeros((8, count), BF16)], axis=0)
    left = jnp.concatenate(
        [jnp.where(target == t, 1.0, 0.0).astype(BF16) * sent for t in range(group)], axis=0
    )
    placed = dot(left, spots, True).reshape(group, 32, CAP)
    packed[:, 0:8] = placed[:, 0:8] + placed[:, 8:16]
    packed[:, 8:16] = placed[:, 16:24]


def start_kernel(
    extents,
    own,
    message,
    bundle,
    segments,
    places,
    kept,
    wide_mod,
    mine,
    theirs,
    wide,
    wide_up,
    wide_mid,
    wide_mod_up,
    mass,
    diag,
):
    wide[...] = jnp.zeros_like(wide)
    mass[...] = jnp.zeros_like(mass)
    wide_mod[...] = jnp.zeros_like(wide_mod)
    for i in range(3):
        widen_own(own, i, wide, i)
    widen_own(own, 3, mass, 0)
    for x in range(4):
        wide_mod[pl.ds(8 * (x + 2) + 2, 4), :] = own[pl.ds(4 * 64 + 4 * x, 4), :]

    def store(array, parity, start, count, stride, value):
        at = rows_of(start, count, stride)
        if array < 3:
            wide[array, parity, at, :] = value
        elif array == 3:
            mass[0, parity, at, :] = value
        else:
            wide_mod[at, :] = value

    unpack_halo(FIRST_PLAN, extents, message, store)
    wide_mod_up[...] = shift_down(wide_mod[...])
    diagonal_into(diag, wide_mod, wide_mod_up)
    for i in range(3):
        for parity in range(4):
            entry = diag[i, parity] + mass[0, parity]
            inverse = jnp.where(mass[0, parity] > 0.0, 1.0 / entry, 0.0)
            diag[i, parity] = inverse
            wide[i, parity] = wide[i, parity] * inverse
        narrow(wide, i, kept, i)
        narrow(diag, i, kept, 3 + i)
    table = table_of(kept[0:192, :])
    gather_all(table, segments, bundle, mine, theirs, places, extents[1])
    lift(wide, wide_up, wide_mid)
    stiffness_into(diag, wide, wide_up, wide_mid, wide_mod, wide_mod_up)
    for i in range(3):
        narrow(diag, i, kept, 6 + i)
        at = pl.ds(64 * (6 + i), 64)
        kept[at, :] += own[pl.ds(192, 64), :] * kept[pl.ds(64 * i, 64), :]


def middle_kernel(
    extents,
    kept,
    bundle,
    segments,
    places,
    mine,
    sent,
    arrived,
    fields,
    message,
    mine_next,
    theirs,
    total,
    pulls,
):
    group = extents[1]
    scatter_all(total, segments, bundle, mine, sent, arrived, places, pulls, group)
    applied = kept[384:576, :] + total[0:192, :] + total[192:384, :]
    scaled = applied * kept[192:384, :]
    fields[0:192, :] = scaled
    fields[192:384, :] = applied
    pack_halo(NEXT_PLAN, fields, message)
    gather_all(table_of(scaled), segments, bundle, mine_next, theirs, places, group)


def end_kernel(
    extents,
    own,
    kept,
    fields,
    message,
    wide_mod,
    bundle,
    segments,
    places,
    mine,
    sent,
    arrived,
    last,
    sums,
    total,
    pulls,
    wide,
    wide_up,
    wide_mid,
    wide_mod_up,
    out,
):
    wide[...] = jnp.zeros_like(wide)
    for i in range(3):
        widen_own(fields, i, wide, i)

    def store(array, parity, start, count, stride, value):
        wide[array, parity, rows_of(start, count, stride), :] = value

    unpack_halo(NEXT_PLAN, extents, message, store)
    wide_mod_up[...] = shift_down(wide_mod[...])
    lift(wide, wide_up, wide_mid)
    stiffness_into(out, wide, wide_up, wide_mid, wide_mod, wide_mod_up)
    for i in range(3):
        narrow(out, i, last, i)
    scatter_all(total, segments, bundle, mine, sent, arrived, places, pulls, extents[1])
    scaled, applied = fields[0:192, :], fields[192:384, :]
    mass = own[192:256, :]
    again = (
        last[...]
        + jnp.concatenate([mass, mass, mass], axis=0) * scaled
        + total[0:192, :]
        + total[192:384, :]
    )
    last[...] = again
    direction = kept[0:192, :]

    def inner(a, b):
        return jnp.sum(a * b, axis=0, keepdims=True)

    sums[0:1, :] = inner(own[0:192, :], direction)
    sums[1:2, :] = inner(direction, applied)
    sums[2:3, :] = inner(scaled, applied)
    sums[3:4, :] = inner(scaled, again)
    sums[4:8, :] = jnp.zeros((4, 128), F32)


def finish_kernel(own, kept, fields, last, sums, adjoint, residual):
    totals = jnp.sum(sums[...], axis=1, keepdims=True)
    first, second, third, fourth = (totals[k : k + 1] for k in range(4))
    step = first / second
    later = step * step * third - first
    ratio = later / first
    grown = 1.0 + ratio
    curved = grown * grown * second - 2.0 * step * grown * third + step * step * fourth
    step_next = later / curved
    along = step + step_next * grown
    across = step_next * step
    swap = swap_lanes(False)
    found = along * kept[0:192, :] - across * fields[0:192, :]
    left = own[0:192, :] - along * fields[192:384, :] + across * last[...]
    for value, ref in ((found, adjoint), (left, residual)):
        value = exact_dot(value, swap)
        for i in range(3):
            for x in range(8):
                for py in range(2):
                    row = i * 64 + (x % 2 * 2 + py) * 16 + x // 2 * 4
                    ref[i, x, pl.ds(py, 4, stride=2), :] = value[row : row + 4]


def exchange_kernel(plan, extents, *refs):
    if plan:
        message, blocks, message_out, blocks_out = refs[:4]
        sends, receives, halo_sends, halo_receives, here = refs[4:]
    else:
        blocks, blocks_out, sends, receives, here = refs
    gx, gy = lax.axis_index("gx"), lax.axis_index("gy")
    wide, group = extents

    def beside(dx, dy):
        return lax.rem(gx + dx + wide, wide), lax.rem(gy + dy + group, group)

    barrier = pltpu.get_barrier_semaphore()
    peers = [(0, k) for k in range(1, group)]
    peers += [(dx, dy) for dx, dy, _, _, _ in plan if dx]
    for dx, dy in peers:
        pl.semaphore_signal(barrier, inc=1, device_id=beside(dx, dy), device_id_type=MESH)
    own = pltpu.make_async_copy(blocks.at[gy], blocks_out.at[gy], here)
    own.start()
    pl.semaphore_wait(barrier, len(peers))
    copies = []
    for k, (dx, dy, first, rows, _) in enumerate(plan):
        at = pl.ds(first, rows)
        copies.append(
            pltpu.make_async_remote_copy(
                src_ref=message.at[at],
                dst_ref=message_out.at[at],
                send_sem=halo_sends.at[k],
                recv_sem=halo_receives.at[k],
                device_id=beside(dx, dy),
                device_id_type=MESH,
            )
        )
        copies[-1].start()
    for k in range(1, group):
        target = beside(0, k)
        copies.append(
            pltpu.make_async_remote_copy(
                src_ref=blocks.at[target[1]],
                dst_ref=blocks_out.at[gy],
                send_sem=sends.at[k],
                recv_sem=receives.at[k],
                device_id=target,
                device_id_type=MESH,
            )
        )
        copies[-1].start()
    own.wait()
    for copy in copies:
        copy.wait()


def exchange(plan, extents, collective, message, blocks):
    outs = [jax.ShapeDtypeStruct(blocks.shape, F32)]
    args = [blocks]
    dma = pltpu.SemaphoreType.DMA
    scratch = [dma((extents[1],)), dma((extents[1],))]
    if plan:
        outs.insert(0, jax.ShapeDtypeStruct(message.shape, F32))
        args.insert(0, message)
        scratch += [dma((len(plan),)), dma((len(plan),))]
    scratch.append(dma)
    return pl.pallas_call(
        functools.partial(exchange_kernel, plan, extents),
        out_shape=outs,
        in_specs=[VMEM] * len(args),
        out_specs=[VMEM] * len(outs),
        scratch_shapes=scratch,
        compiler_params=pltpu.CompilerParams(
            collective_id=collective, has_side_effects=True, vmem_limit_bytes=LIMIT
        ),
        name=f"exchange_{collective}",
    )(*args)


def sum_kernel(extents, tile, out, across, along, middle, sends, receives):
    gx, gy = lax.axis_index("gx"), lax.axis_index("gy")
    wide, group = extents
    barrier = pltpu.get_barrier_semaphore()
    rows = [(lax.rem(gx + k, wide), gy) for k in range(1, wide)]
    columns = [(gx, lax.rem(gy + k, group)) for k in range(1, group)]
    for device in rows + columns:
        pl.semaphore_signal(barrier, inc=1, device_id=device, device_id_type=MESH)
    across[gx] = tile[...]
    pl.semaphore_wait(barrier, len(rows) + len(columns))

    def send(source, slots, me, devices, first):
        copies = []
        for k, device in enumerate(devices):
            copies.append(
                pltpu.make_async_remote_copy(
                    src_ref=source,
                    dst_ref=slots.at[me],
                    send_sem=sends.at[first + k],
                    recv_sem=receives.at[first + k],
                    device_id=device,
                    device_id_type=MESH,
                )
            )
            copies[-1].start()
        for copy in copies:
            copy.wait()

    send(tile, across, gx, rows, 0)
    part = jnp.sum(across[...], axis=0)
    middle[...] = part
    along[gy] = part
    send(middle, along, gy, columns, len(rows))
    out[...] = jnp.sum(along[...], axis=0)


def global_sum(extents, collective, tile):
    count = sum(extents)
    return pl.pallas_call(
        functools.partial(sum_kernel, extents),
        out_shape=jax.ShapeDtypeStruct(tile.shape, F32),
        in_specs=[VMEM],
        out_specs=VMEM,
        scratch_shapes=[
            pltpu.VMEM((extents[0],) + tile.shape, F32),
            pltpu.VMEM((extents[1],) + tile.shape, F32),
            pltpu.VMEM(tile.shape, F32),
            pltpu.SemaphoreType.DMA((count,)),
            pltpu.SemaphoreType.DMA((count,)),
        ],
        compiler_params=pltpu.CompilerParams(collective_id=collective, has_side_effects=True),
        name="global_sum",
    )(tile)


def local(body, outs, scratch, args, name):
    return pl.pallas_call(
        body,
        out_shape=[jax.ShapeDtypeStruct(shape, dtype) for shape, dtype in outs],
        in_specs=[VMEM] * len(args),
        out_specs=[VMEM] * len(outs),
        scratch_shapes=[pltpu.VMEM(shape, F32) for shape in scratch],
        compiler_params=pltpu.CompilerParams(vmem_limit_bytes=LIMIT),
        name=name,
    )(*args)


def shards(
    seed_grad,
    modulus,
    lumped_mass,
    pair_dest,
    slave_nodes,
    slave_weights,
    master_nodes,
    master_weights,
    penalty,
):
    extents = (lax.axis_size("gx"), lax.axis_size("gy"))
    group, count = extents[1], penalty.shape[0]
    parts = ((group, 8, CAP), F32)
    field = (3, 4, WIDE, 128)
    own, message, packed, segments, places = local(
        functools.partial(prepare_kernel, group),
        [
            ((320, 128), F32),
            ((FIRST_ROWS, 128), F32),
            ((group, 16, CAP), F32),
            ((16, count), F32),
            ((CAP, count), BF16),
        ],
        [(5, 8, 8, 128)],
        (
            seed_grad,
            modulus,
            lumped_mass,
            pair_dest.reshape(1, count),
            slave_nodes,
            slave_weights,
            master_nodes,
            master_weights,
            penalty.reshape(1, count),
        ),
        "prepare",
    )
    message, bundle = exchange(FIRST_PLAN, extents, 1, message, packed)
    kept, wide_mod, mine, theirs = local(
        functools.partial(start_kernel, extents),
        [((576, 128), F32), ((WIDE, 128), F32), ((8, count), F32), parts],
        [field, (3, 3, WIDE, 128), (3, WIDE, 128), (WIDE, 128), (1, 4, WIDE, 128), field],
        (own, message, bundle, segments, places),
        "start",
    )
    (arrived,) = exchange([], extents, 2, None, theirs)
    fields, message, mine_next, theirs_next = local(
        functools.partial(middle_kernel, extents),
        [((384, 128), F32), ((NEXT_ROWS, 128), F32), ((8, count), F32), parts],
        [(384, 128), (8, count)],
        (kept, bundle, segments, places, mine, theirs, arrived),
        "middle",
    )
    message, arrived = exchange(NEXT_PLAN, extents, 3, message, theirs_next)
    last, sums = local(
        functools.partial(end_kernel, extents),
        [((192, 128), F32), ((8, 128), F32)],
        [
            (384, 128),
            (8, count),
            field,
            (3, 3, WIDE, 128),
            (3, WIDE, 128),
            (WIDE, 128),
            field,
        ],
        (
            own,
            kept,
            fields,
            message,
            wide_mod,
            bundle,
            segments,
            places,
            mine_next,
            theirs_next,
            arrived,
        ),
        "end",
    )
    sums = global_sum(extents, 4, sums)
    return tuple(
        local(
            finish_kernel,
            [(seed_grad.shape, F32), (seed_grad.shape, F32)],
            [],
            (own, kept, fields, last, sums),
            "finish",
        )
    )


def solution(mesh):
    placed = (
        P(None, "gx", "gy", None),
        P("gx", "gy", None),
        P("gx", "gy", None),
        P(("gx", "gy"), None),
        P(None, ("gx", "gy")),
        P(None, ("gx", "gy")),
        P(None, ("gx", "gy")),
        P(None, ("gx", "gy")),
        P(("gx", "gy")),
    )
    return jax.shard_map(
        shards,
        mesh=mesh,
        in_specs=placed,
        out_specs=(P(None, "gx", "gy", None), P(None, "gx", "gy", None)),
        check_vma=False,
    )
```

```python
import functools
import math

import jax
import jax.numpy as jnp
import numpy as np
from jax import lax
from jax.experimental import pallas as pl
from jax.experimental.pallas import tpu as pltpu
from jax.sharding import PartitionSpec as P

CAP = 256
SHEAR = 1.0 / 2.6
LAME = 0.3 / 0.52
MESH = pl.DeviceIdType.MESH
F32 = jnp.float32
BF16 = jnp.bfloat16
VMEM = pl.BlockSpec(memory_space=pltpu.VMEM)
LIMIT = 64 * 1024 * 1024

WIDE = 72


def shape_tables():
    abscissa = 1.0 / math.sqrt(3.0)
    points = [
        (a, b, c)
        for a in (-abscissa, abscissa)
        for b in (-abscissa, abscissa)
        for c in (-abscissa, abscissa)
    ]
    offsets = [
        (i, j, k)
        for i in range(3)
        for j in range(3)
        for k in range(3)
        if (i == 1) + (j == 1) + (k == 1) <= 1
    ]
    derivative = np.zeros((8, 3, 20))
    for g, location in enumerate(points):
        for n, offset in enumerate(offsets):
            natural = [offset[d] - 1 for d in range(3)]
            factors = [
                1.0 - location[d] ** 2 if natural[d] == 0 else 1.0 + location[d] * natural[d]
                for d in range(3)
            ]
            slopes = [
                -2.0 * location[d] if natural[d] == 0 else float(natural[d]) for d in range(3)
            ]
            linear = sum(location[d] * natural[d] for d in range(3)) - 2.0
            for d in range(3):
                others = factors[(d + 1) % 3] * factors[(d + 2) % 3]
                if 0 in natural:
                    derivative[g, d, n] = slopes[d] * others / 4.0
                else:
                    derivative[g, d, n] = natural[d] * others * (linear + factors[d]) / 8.0
    return derivative, offsets


def signs(count, dims):
    table = np.ones((count, count))
    for t in range(count):
        for c in range(count):
            for d in range(dims):
                if t >> d & 1 and not c >> d & 1:
                    table[t, c] = -table[t, c]
    return table


def element_tables():
    derivative, offsets = shape_tables()
    eight, four = signs(8, 3), signs(4, 2)
    modal = np.einsum("sg,gan->asn", eight, derivative) / 8.0
    corner_at = [offsets.index((c >> 2 << 1, (c >> 1 & 1) << 1, (c & 1) << 1)) for c in range(8)]
    edge_at = []
    for d in range(3):
        row = []
        for c in range(4):
            offset = [(c >> 1) << 1, (c & 1) << 1]
            offset.insert(d, 1)
            row.append(offsets.index(tuple(offset)))
        edge_at.append(row)
    corner_terms = np.einsum("tn,asn->ast", eight, modal[:, :, corner_at]) / 8.0
    edge_terms = [np.einsum("tn,asn->ast", four, modal[:, :, edge_at[d]]) / 4.0 for d in range(3)]
    trilinear = np.array([(1.0 / math.sqrt(3.0)) ** bin(t).count("1") / 8.0 for t in range(8)])
    at_points = np.einsum("t,tg->gt", trilinear, eight)
    squares = derivative * derivative
    weight = np.einsum(
        "gt,gni->tni",
        at_points,
        SHEAR * squares.sum(axis=1)[:, :, None] + (LAME + SHEAR) * np.swapaxes(squares, 1, 2),
    )
    corner_diag = np.einsum("un,tni->uti", eight, weight[:, corner_at]) / 8.0
    edge_diag = [np.einsum("un,tni->uti", four, weight[:, edge_at[d]]) / 4.0 for d in range(3)]
    return corner_terms, edge_terms, trilinear, corner_diag, edge_diag


def split_sums(values):
    values = list(values)
    step = 1
    while step < len(values):
        for low in range(len(values)):
            if not low & step:
                a, b = values[low], values[low | step]
                values[low], values[low | step] = b + a, b - a
        step *= 2
    return values


def join_sums(values):
    values = list(values)
    step = 1
    while step < len(values):
        for low in range(len(values)):
            if not low & step:
                a, b = values[low], values[low | step]
                values[low], values[low | step] = a - b, a + b
        step *= 2
    return values


def combine(terms):
    total = None
    for factor, value in terms:
        if abs(factor) < 1e-12:
            continue
        term = value * np.float32(factor)
        total = term if total is None else total + term
    return total


def lanes(rows):
    return lax.broadcasted_iota(jnp.int32, (rows, 128), 1)


def shift_down(value):
    return jnp.where(lanes(value.shape[0]) == 63, 0.0, pltpu.roll(value, 127, 1))


def collect(low, middle, high):
    total = low + jnp.where(lanes(8) < 64, pltpu.roll(high, 1, 1), 0.0)
    if middle is not None:
        total = total + pltpu.roll(middle, 64, 1)
    return total


def corner_moduli(wide_mod, wide_mod_up, group):
    values = []
    for c in range(8):
        ref = wide_mod_up if c & 1 else wide_mod
        values.append(ref[pl.ds(8 * (group + (c >> 2)) + (c >> 1 & 1), 8), :])
    inside = lanes(8) < 64
    return split_sums([jnp.where(inside, value, 0.0) for value in values])


def edge_corner(d, c):
    where = [c >> 1, c & 1]
    where.insert(d, None)
    return where


def add_rows(ref, index, row, value):
    ref[index + (pl.ds(row, 8), slice(None))] += value


def scatter_forces(out, i, corner, edges, group):
    for xy in range(4):
        row = 8 * (group + (xy >> 1)) + (xy & 1)
        add_rows(out, (i, 0), row, collect(corner[2 * xy], edges[2][xy], corner[2 * xy + 1]))
    for y in range(2):
        add_rows(out, (i, 2), 8 * group + y, collect(edges[0][2 * y], None, edges[0][2 * y + 1]))
    for x in range(2):
        add_rows(
            out, (i, 1), 8 * (group + x), collect(edges[1][2 * x], None, edges[1][2 * x + 1])
        )


def diagonal_into(out, wide_mod, wide_mod_up):
    corner_diag, edge_diag = element_tables()[3:]
    out[...] = jnp.zeros_like(out)
    for group in range(7):
        moduli = corner_moduli(wide_mod, wide_mod_up, group)
        for i in range(3):
            corner = join_sums(
                [
                    combine([(corner_diag[u, t, i], moduli[t]) for t in range(8)])
                    for u in range(8)
                ]
            )
            edges = [
                join_sums(
                    [
                        combine([(edge_diag[d][u, t, i], moduli[t]) for t in range(8)])
                        for u in range(4)
                    ]
                )
                for d in range(3)
            ]
            scatter_forces(out, i, corner, edges, group)


def stiffness_into(out, wide, wide_up, wide_mid, wide_mod, wide_mod_up):
    corner_terms, edge_terms, trilinear = element_tables()[:3]
    out[...] = jnp.zeros_like(out)
    for group in range(1, 6):
        moduli = corner_moduli(wide_mod, wide_mod_up, group)
        points = join_sums([moduli[t] * np.float32(trilinear[t]) for t in range(8)])
        slopes = []
        for i in range(3):
            corner = []
            for c in range(8):
                ref = wide_up if c & 1 else wide
                corner.append(ref[i, 0, pl.ds(8 * (group + (c >> 2)) + (c >> 1 & 1), 8), :])
            corner = split_sums(corner)
            edges = []
            for d in range(3):
                values = []
                for c in range(4):
                    x, y, z = edge_corner(d, c)
                    row = 8 * (group + (x or 0)) + (y or 0)
                    parity = (2, 1, 0)[d]
                    if d == 2:
                        values.append(wide_mid[i, pl.ds(row, 8), :])
                    else:
                        values.append((wide_up if z else wide)[i, parity, pl.ds(row, 8), :])
                edges.append(split_sums(values))
            slopes.append(
                [
                    [
                        combine(
                            [(corner_terms[a, s, t], corner[t]) for t in range(8)]
                            + [
                                (edge_terms[d][a, s, t], edges[d][t])
                                for d in range(3)
                                for t in range(4)
                            ]
                        )
                        for s in range(8)
                    ]
                    for a in range(3)
                ]
            )

        def plus(a, b):
            return a if b is None else b if a is None else a + b

        zero = jnp.zeros((8, 128), F32)
        strain = {}
        for a in range(3):
            strain[a, a] = slopes[a][a]
            for b in range(a):
                strain[b, a] = [plus(p, q) for p, q in zip(slopes[a][b], slopes[b][a])]
        strain = {
            key: join_sums([zero if v is None else v for v in value])
            for key, value in strain.items()
        }
        stress = {key: [] for key in strain}
        for g in range(8):
            volume = (strain[0, 0][g] + strain[1, 1][g] + strain[2, 2][g]) * np.float32(LAME)
            for a in range(3):
                stress[a, a].append(
                    points[g] * (volume + strain[a, a][g] * np.float32(2.0 * SHEAR))
                )
            scaled = points[g] * np.float32(SHEAR)
            for key in ((0, 1), (0, 2), (1, 2)):
                stress[key].append(scaled * strain[key][g])
        stress = {key: split_sums(value) for key, value in stress.items()}
        for i in range(3):
            pairs = [
                (a, s, stress[min(a, i), max(a, i)][s]) for a in range(3) for s in range(8)
            ]
            corner = join_sums(
                [combine([(corner_terms[a, s, t], v) for a, s, v in pairs]) for t in range(8)]
            )
            edges = [
                join_sums(
                    [combine([(edge_terms[d][a, s, t], v) for a, s, v in pairs]) for t in range(4)]
                )
                for d in range(3)
            ]
            scatter_forces(out, i, corner, edges, group)


def lift(wide, wide_up, wide_mid):
    for i in range(3):
        for parity in range(3):
            wide_up[i, parity] = shift_down(wide[i, parity])
        wide_mid[i] = pltpu.roll(wide[i, 0], 64, 1)


def halo_plan(fields, with_modulus):
    plan, first = [], 0
    for dx in (-1, 0, 1):
        for dy in (-1, 0, 1):
            if dx == 0 and dy == 0:
                continue
            pieces = []

            def places(step, both):
                if step == 1:
                    return [(p, 3, 1) for p in ((0, 1) if both else (0,))]
                return [(0, 0, 6)]

            def strips(array, xs, ys):
                for px, ox, wx in xs:
                    for py, oy, wy in ys:
                        if ox is None:
                            pieces.append((array, px * 2 + py, oy, 4, 4, 8 * 2 + wy, 8))
                        elif oy is None:
                            pieces.append((array, px * 2 + py, 4 * ox, 4, 1, 8 * wx + 2, 1))
                        else:
                            pieces.append((array, px * 2 + py, 4 * ox + oy, 1, 1, 8 * wx + wy, 1))

            every = [(0, None, None), (1, None, None)]
            for array in range(fields):
                strips(
                    array,
                    every if dx == 0 else places(dx, True),
                    every if dy == 0 else places(dy, True),
                )
            if with_modulus:
                deep = {1: [(0, 3, 1), (0, 2, 0)], -1: [(0, 0, 6), (0, 1, 7)], 0: every[:1]}
                strips(fields, deep[dx], deep[dy])
            rows = sum(piece[3] for piece in pieces)
            plan.append((dx, dy, first, -(-rows // 8) * 8, pieces))
            first += plan[-1][3]
    return plan, first


FIRST_PLAN, FIRST_ROWS = halo_plan(4, True)
NEXT_PLAN, NEXT_ROWS = halo_plan(3, False)


def rows_of(start, count, stride):
    return pl.ds(start, count) if stride == 1 else pl.ds(start, count, stride=stride)


def pack_halo(plan, own, message):
    message[...] = jnp.zeros_like(message)
    for _, _, first, _, pieces in plan:
        at = first
        for array, parity, start, count, stride, _, _ in pieces:
            source = own[rows_of(array * 64 + parity * 16 + start, count, stride), :]
            message[pl.ds(at, count), :] = source
            at += count


def unpack_halo(plan, extents, message, store):
    gx, gy = lax.axis_index("gx"), lax.axis_index("gy")
    for dx, dy, first, _, pieces in plan:
        inside = None
        for step, at, extent in ((dx, gx, extents[0]), (dy, gy, extents[1])):
            if step:
                here = at > 0 if step == 1 else at < extent - 1
                inside = here if inside is None else jnp.logical_and(inside, here)
        keep = jnp.where(inside, 1.0, 0.0).astype(F32)
        at = first
        for array, parity, _, count, _, start, stride in pieces:
            store(array, parity, start, count, stride, message[pl.ds(at, count), :] * keep)
            at += count


def widen_own(own, array, wide, i):
    for parity in range(4):
        for x in range(4):
            wide[i, parity, pl.ds(8 * (x + 2) + 2, 4), :] = own[
                pl.ds(array * 64 + parity * 16 + 4 * x, 4), :
            ]


def narrow(wide, i, own, array):
    for parity in range(4):
        for x in range(4):
            own[pl.ds(array * 64 + parity * 16 + 4 * x, 4), :] = wide[
                i, parity, pl.ds(8 * (x + 2) + 2, 4), :
            ]


def in_two(value):
    head = value.astype(BF16)
    return head, (value - head.astype(F32)).astype(BF16)


def down_iota(rows, columns):
    return lax.broadcasted_iota(jnp.int32, (rows, columns), 0).astype(F32).astype(BF16)


def ones_where(rows, labels):
    columns = labels.shape[1]
    return jnp.where(
        down_iota(rows, columns) == labels.astype(BF16), jnp.ones((), BF16), jnp.zeros((), BF16)
    )


def dot(a, b, transposed=False):
    return lax.dot_general(
        a, b, (((1,), (1 if transposed else 0,)), ((), ())), preferred_element_type=F32
    )


BLOCK = CAP


def picks_of(lane, extent):
    return jnp.concatenate([ones_where(extent, lane[j : j + 1]) for j in range(4)], axis=1)


def gather_block(table, block):
    count = block.shape[1]
    picks = picks_of(block[12:16], 128)
    found = dot(table, jnp.concatenate([picks, picks], axis=0))
    down = lax.broadcasted_iota(jnp.int32, (64, count), 0).astype(F32)
    factors = [
        jnp.where(down == block[8 + j : 9 + j], block[j : j + 1], 0.0) for j in range(4)
    ]
    result = []
    for i in range(3):
        total = sum(
            factors[j] * found[64 * i : 64 * (i + 1), count * j : count * (j + 1)]
            for j in range(4)
        )
        result.append(jnp.sum(total, axis=0, keepdims=True))
    return jnp.concatenate(result, axis=0)


def scatter_block(block, traction):
    upper = jnp.where(block[8:12] >= 32.0, 1.0, 0.0)
    row, lane = block[8:12] - 32.0 * upper, block[12:16] + 128.0 * upper
    rows = [ones_where(32, row[j : j + 1]) for j in range(4)]
    parts = [
        [in_two(block[j : j + 1] * traction[i : i + 1]) for j in range(4)] for i in range(3)
    ]
    left = [
        jnp.concatenate([rows[j] * parts[i][j][part] for j in range(4)], axis=1)
        for part in range(2)
        for i in range(3)
    ]
    return dot(jnp.concatenate(left, axis=0), picks_of(lane, 256), True)


def total_rows(total):
    value = total[0:96, :] + total[96:192, :]
    return jnp.concatenate(
        [
            value[32 * i : 32 * (i + 1), 128 * half : 128 * (half + 1)]
            for i in range(3)
            for half in range(2)
        ],
        axis=0,
    )


def table_of(value):
    head, tail = in_two(value)
    return jnp.concatenate([head, tail], axis=1)


def each(first, last, body, unroll):
    def step(k, carry):
        body(k)
        return carry

    lax.fori_loop(first, last, step, 0, unroll=unroll)


def gather_slaves(table, segments, mine, theirs, places, group):
    mine[...] = jnp.zeros_like(mine)

    def slave(k):
        at = pl.ds(pl.multiple_of(k * BLOCK, BLOCK), BLOCK)
        mine[0:3, at] = gather_block(table, segments[:, at])

    each(0, segments.shape[1] // BLOCK, slave, 4)
    head, tail = in_two(mine[...])
    both = jnp.concatenate([head, tail], axis=0)
    target = segments[5:6, :]
    left = jnp.concatenate(
        [jnp.where(target == t, 1.0, 0.0).astype(BF16) * both for t in range(group)], axis=0
    )
    placed = dot(left, places[...], True).reshape(group, 16, CAP)
    theirs[...] = placed[:, 0:8] + placed[:, 8:16]


def gather_masters(table, bundle, theirs, group):
    theirs[...] = jnp.zeros_like(theirs)

    def master(source):
        theirs[source, 0:3, :] = gather_block(table, bundle[source])

    each(0, group, master, 8)


def pull_slaves(segments, mine, returned, places, pulls, group):
    head, tail = in_two(returned[...].reshape(group * 8, CAP))
    found = dot(
        jnp.concatenate([head, tail], axis=1),
        jnp.concatenate([places[...], places[...]], axis=0),
    )
    target = segments[5:6, :]
    back = sum(jnp.where(target == t, 1.0, 0.0) * found[8 * t : 8 * (t + 1)] for t in range(group))
    gap = mine[0:3, :] - back[0:3, :]
    pulls[0:3, :] = segments[4:5, :] * gap
    return gap


def scatter_slaves(total, segments, pulls):
    def slave(k):
        at = pl.ds(pl.multiple_of(k * 2 * BLOCK, 2 * BLOCK), 2 * BLOCK)
        total[...] += scatter_block(segments[:, at], pulls[0:3, at])

    each(0, segments.shape[1] // (2 * BLOCK), slave, 2)


def scatter_masters(total, bundle, sent, arrived, first, last):
    def master(k):
        pair = [2 * k, 2 * k + 1]
        block = jnp.concatenate([bundle[source] for source in pair], axis=1)
        gap = [sent[source, 0:3, :] - arrived[source, 0:3, :] for source in pair]
        total[...] += scatter_block(block, block[4:5] * jnp.concatenate(gap, axis=1))

    each(first // 2, last // 2, master, 4)


def swap_lanes(forth):
    a = lax.broadcasted_iota(jnp.int32, (128, 128), 0 if forth else 1)
    b = lax.broadcasted_iota(jnp.int32, (128, 128), 1 if forth else 0)
    return jnp.where(b == (a % 2) * 64 + a // 2, 1.0, 0.0).astype(F32)


def reorder(value, forth):
    head = value.astype(BF16)
    rest = value - head.astype(F32)
    middle = rest.astype(BF16)
    tail = (rest - middle.astype(F32)).astype(BF16)
    swap = swap_lanes(forth).astype(BF16)
    return dot(
        jnp.concatenate([head, middle, tail], axis=1), jnp.concatenate([swap, swap, swap], axis=0)
    )


def lay_out(seed, modulus, mass, own, swapped):
    values = [seed[...].reshape(192, 128), mass[...].reshape(64, 128)]
    values.append(modulus[...].reshape(64, 128))
    swapped[...] = reorder(jnp.concatenate(values, axis=0), True).reshape(5, 8, 8, 128)
    for array in range(5):
        for x in range(8):
            for py in range(2):
                row = array * 64 + (x % 2 * 2 + py) * 16 + x // 2 * 4
                own[pl.ds(row, 4), :] = swapped[array, x, pl.ds(py, 4, stride=2), :]


def place_of(node):
    x, y, z = node // 1024, node // 128 % 8, node % 128
    row = (x % 2 * 2 + y % 2) * 16 + x // 2 * 4 + y // 2
    return row.astype(F32), (z % 2 * 64 + z // 2).astype(F32)


def place_segments(
    group,
    pair,
    slave_nodes,
    slave_weights,
    master_nodes,
    master_weights,
    penalty,
    packed,
    segments,
    places,
):
    slave_row, slave_lane = place_of(slave_nodes[...])
    master_row, master_lane = place_of(master_nodes[...])
    target = pair[...].astype(F32)
    count = target.shape[1]
    chosen = ones_where(group, target)
    a = lax.broadcasted_iota(jnp.int32, (128, 128), 0)
    b = lax.broadcasted_iota(jnp.int32, (128, 128), 1)
    before = jnp.where(a < b, 1.0, 0.0).astype(BF16)
    ranks, base = [], jnp.zeros((group, 1), F32)
    for k in range(count // 128):
        part = chosen[:, 128 * k : 128 * (k + 1)]
        wide = part.astype(F32)
        rank = dot(part, before) + base
        ranks.append(jnp.sum(rank * wide, axis=0, keepdims=True))
        base = base + jnp.sum(wide, axis=1, keepdims=True)
    position = jnp.concatenate(ranks, axis=1)
    segments[0:4, :] = slave_weights[...]
    segments[4:5, :] = penalty[...]
    segments[5:6, :] = target
    segments[6:7, :] = position
    segments[7:8, :] = jnp.zeros_like(position)
    segments[8:12, :] = slave_row
    segments[12:16, :] = slave_lane
    spots = ones_where(CAP, position)
    places[...] = spots
    nothing = jnp.zeros((3, count), F32)
    values = jnp.concatenate([master_weights[...], penalty[...], nothing], axis=0)
    head, tail = in_two(values)
    nodes = jnp.concatenate([master_row, master_lane], axis=0)
    sent = jnp.concatenate([head, tail, nodes.astype(BF16), jnp.zeros((8, count), BF16)], axis=0)
    left = jnp.concatenate(
        [jnp.where(target == t, 1.0, 0.0).astype(BF16) * sent for t in range(group)], axis=0
    )
    placed = dot(left, spots, True).reshape(group, 32, CAP)
    packed[:, 0:8] = placed[:, 0:8] + placed[:, 8:16]
    packed[:, 8:16] = placed[:, 16:24]


def inner(a, b):
    return jnp.sum(a * b, axis=0, keepdims=True)


INPUTS = (
    "seed",
    "modulus",
    "mass",
    "pair",
    "slave_nodes",
    "slave_weights",
    "master_nodes",
    "master_weights",
    "penalty",
)


def scratch_of(extents, args):
    group, count = extents[1], args[-1].shape[-1]
    dma, parts, field = pltpu.SemaphoreType.DMA, (group, 8, CAP), (3, 4, WIDE, 128)
    room = {name: pltpu.VMEM(arg.shape, arg.dtype) for name, arg in zip(INPUTS, args)}
    shapes = {
        "own": (320, 128),
        "swapped": (5, 8, 8, 128),
        "segments": (16, count),
        "packed": (group, 16, CAP),
        "bundle": (group, 16, CAP),
        "halo_out": (FIRST_ROWS, 128),
        "halo_in": (FIRST_ROWS, 128),
        "halo_out_next": (NEXT_ROWS, 128),
        "halo_in_next": (NEXT_ROWS, 128),
        "mine": (8, count),
        "mine_next": (8, count),
        "slaves_out": parts,
        "slaves_in": parts,
        "masters_out": parts,
        "masters_in": parts,
        "slaves_out_next": parts,
        "slaves_in_next": parts,
        "masters_out_next": parts,
        "masters_in_next": parts,
        "kept": (576, 128),
        "fields": (384, 128),
        "last": (192, 128),
        "wide_mod": (WIDE, 128),
        "wide_mod_up": (WIDE, 128),
        "mass_wide": (1, 4, WIDE, 128),
        "wide": field,
        "wide_up": (3, 3, WIDE, 128),
        "wide_mid": (3, WIDE, 128),
        "out": field,
        "total": (192, 256),
        "pulls": (8, count),
        "tile": (8, 128),
        "middle": (8, 128),
        "across": (extents[0], 8, 128),
        "along": (group, 8, 128),
    }
    room.update({name: pltpu.VMEM(shape, F32) for name, shape in shapes.items()})
    room["places"] = pltpu.VMEM((CAP, count), BF16)
    room["loads"] = dma((len(INPUTS),))
    for name in ("halo", "halo_next"):
        room[name + "_sends"] = room[name + "_receives"] = dma((len(FIRST_PLAN),))
    for name in ("packed", "slaves", "masters", "slaves_next", "masters_next", "sum_along"):
        room[name + "_sends"] = room[name + "_receives"] = dma((group,))
    room["sum_across_sends"] = room["sum_across_receives"] = dma((extents[0],))
    return room


class Refs:
    def __init__(self, names, refs):
        self.__dict__.update(zip(names, refs))


def whole_kernel(extents, names, *refs):
    inputs, (adjoint, residual) = refs[: len(INPUTS)], refs[len(INPUTS) : len(INPUTS) + 2]
    r = Refs(names, refs[len(INPUTS) + 2 :])
    wide, group = extents
    gx, gy = lax.axis_index("gx"), lax.axis_index("gy")
    loads = [
        pltpu.make_async_copy(ref, getattr(r, name), r.loads.at[k])
        for k, (name, ref) in enumerate(zip(INPUTS, inputs))
    ]
    for load in loads:
        load.start()

    def beside(dx, dy):
        return lax.rem(gx + dx + wide, wide), lax.rem(gy + dy + group, group)

    barrier = pltpu.get_barrier_semaphore()
    peers = [(0, k) for k in range(1, group)] + [(k, 0) for k in range(1, wide)]
    peers += [(dx, dy) for dx, dy, _, _, _ in FIRST_PLAN if dx and dy]
    for dx, dy in peers:
        pl.semaphore_signal(barrier, inc=1, device_id=beside(dx, dy), device_id_type=MESH)

    def send(source, target, kind, k, device):
        copy = pltpu.make_async_remote_copy(
            src_ref=source,
            dst_ref=target,
            send_sem=getattr(r, kind + "_sends").at[k],
            recv_sem=getattr(r, kind + "_receives").at[k],
            device_id=device,
            device_id_type=MESH,
        )
        copy.start()
        return copy

    def send_halo(plan, source, target, kind):
        return [
            send(source.at[pl.ds(at, rows)], target.at[pl.ds(at, rows)], kind, k, beside(dx, dy))
            for k, (dx, dy, at, rows, _) in enumerate(plan)
        ]

    def send_blocks(source, target, kind):
        copies = []
        for k in range(1, group):
            device = beside(0, k)
            copies.append(send(source.at[device[1]], target.at[gy], kind, k, device))
        target[gy] = source[gy]
        return copies

    def receive(copies):
        for copy in copies:
            copy.wait_recv()

    for load in loads[:3]:
        load.wait()
    lay_out(r.seed, r.modulus, r.mass, r.own, r.swapped)
    pack_halo(FIRST_PLAN, r.own, r.halo_out)
    pl.semaphore_wait(barrier, len(peers))
    halo = send_halo(FIRST_PLAN, r.halo_out, r.halo_in, "halo")
    for load in loads[3:]:
        load.wait()
    place_segments(
        group,
        r.pair,
        r.slave_nodes,
        r.slave_weights,
        r.master_nodes,
        r.master_weights,
        r.penalty,
        r.packed,
        r.segments,
        r.places,
    )
    bundles = send_blocks(r.packed, r.bundle, "packed")

    r.wide[...] = jnp.zeros_like(r.wide)
    r.mass_wide[...] = jnp.zeros_like(r.mass_wide)
    r.wide_mod[...] = jnp.zeros_like(r.wide_mod)
    for i in range(3):
        widen_own(r.own, i, r.wide, i)
    widen_own(r.own, 3, r.mass_wide, 0)
    for x in range(4):
        r.wide_mod[pl.ds(8 * (x + 2) + 2, 4), :] = r.own[pl.ds(4 * 64 + 4 * x, 4), :]

    def store(array, parity, start, count, stride, value):
        at = rows_of(start, count, stride)
        if array < 3:
            r.wide[array, parity, at, :] = value
        elif array == 3:
            r.mass_wide[0, parity, at, :] = value
        else:
            r.wide_mod[at, :] = value

    receive(halo)
    unpack_halo(FIRST_PLAN, extents, r.halo_in, store)
    r.wide_mod_up[...] = shift_down(r.wide_mod[...])
    diagonal_into(r.out, r.wide_mod, r.wide_mod_up)
    for i in range(3):
        for parity in range(4):
            mass = r.mass_wide[0, parity]
            inverse = jnp.where(mass > 0.0, 1.0 / (r.out[i, parity] + mass), 0.0)
            r.out[i, parity] = inverse
            r.wide[i, parity] = r.wide[i, parity] * inverse
        narrow(r.wide, i, r.kept, i)
        narrow(r.out, i, r.kept, 3 + i)
    table = table_of(r.kept[0:192, :])
    gather_slaves(table, r.segments, r.mine, r.slaves_out, r.places, group)
    slaves = send_blocks(r.slaves_out, r.slaves_in, "slaves")
    receive(bundles)
    gather_masters(table, r.bundle, r.masters_out, group)
    masters = send_blocks(r.masters_out, r.masters_in, "masters")

    def stiffness():
        lift(r.wide, r.wide_up, r.wide_mid)
        stiffness_into(r.out, r.wide, r.wide_up, r.wide_mid, r.wide_mod, r.wide_mod_up)

    stiffness()
    for i in range(3):
        narrow(r.out, i, r.kept, 6 + i)
        at = pl.ds(64 * (6 + i), 64)
        r.kept[at, :] += r.own[pl.ds(192, 64), :] * r.kept[pl.ds(64 * i, 64), :]

    receive(slaves)
    r.total[...] = jnp.zeros_like(r.total)
    scatter_masters(r.total, r.bundle, r.masters_out, r.slaves_in, 0, group)
    receive(masters)
    pull_slaves(r.segments, r.mine, r.masters_in, r.places, r.pulls, group)
    scatter_slaves(r.total, r.segments, r.pulls)
    applied = r.kept[384:576, :] + total_rows(r.total)
    scaled = applied * r.kept[192:384, :]
    r.fields[0:192, :] = scaled
    r.fields[192:384, :] = applied
    pack_halo(NEXT_PLAN, r.fields, r.halo_out_next)
    halo_next = send_halo(NEXT_PLAN, r.halo_out_next, r.halo_in_next, "halo_next")
    table = table_of(scaled)
    gather_slaves(table, r.segments, r.mine_next, r.slaves_out_next, r.places, group)
    slaves_next = send_blocks(r.slaves_out_next, r.slaves_in_next, "slaves_next")
    gather_masters(table, r.bundle, r.masters_out_next, group)
    masters_next = send_blocks(r.masters_out_next, r.masters_in_next, "masters_next")

    r.wide[...] = jnp.zeros_like(r.wide)
    for i in range(3):
        widen_own(r.fields, i, r.wide, i)

    def store_next(array, parity, start, count, stride, value):
        r.wide[array, parity, rows_of(start, count, stride), :] = value

    receive(halo_next)
    unpack_halo(NEXT_PLAN, extents, r.halo_in_next, store_next)
    stiffness()
    for i in range(3):
        narrow(r.out, i, r.last, i)
    seed, direction = r.own[0:192, :], r.kept[0:192, :]
    scaled, applied = r.fields[0:192, :], r.fields[192:384, :]
    mass = r.own[192:256, :]
    smooth = r.last[...] + jnp.concatenate([mass, mass, mass], axis=0) * scaled
    r.last[...] = smooth
    r.tile[0:1, :] = inner(seed, direction)
    r.tile[1:2, :] = inner(direction, applied)
    r.tile[2:3, :] = inner(scaled, applied)
    r.tile[4:8, :] = jnp.zeros((4, 128), F32)

    def masters_from(first, last):
        scatter_masters(r.total, r.bundle, r.masters_out_next, r.slaves_in_next, first, last)

    receive(slaves_next)
    r.total[...] = jnp.zeros_like(r.total)
    masters_from(0, group // 4)
    receive(masters_next)
    gap = pull_slaves(r.segments, r.mine_next, r.masters_in_next, r.places, r.pulls, group)
    pressed = inner(gap, r.pulls[0:3, :])
    energy = inner(scaled, smooth)
    for k in range(pressed.shape[1] // 128):
        energy = energy + pressed[:, 128 * k : 128 * (k + 1)]
    r.tile[3:4, :] = energy
    across = [
        send(r.tile, r.across.at[gx], "sum_across", k, beside(k, 0)) for k in range(1, wide)
    ]
    r.across[gx] = r.tile[...]
    scatter_slaves(r.total, r.segments, r.pulls)
    masters_from(group // 4, group // 2)
    receive(across)
    part = jnp.sum(r.across[...], axis=0)
    r.middle[...] = part
    along = [
        send(r.middle, r.along.at[gy], "sum_along", k, beside(0, k)) for k in range(1, group)
    ]
    r.along[gy] = part
    masters_from(group // 2, group)
    again = r.last[...] + total_rows(r.total)
    receive(along)
    totals = jnp.sum(jnp.sum(r.along[...], axis=0), axis=1, keepdims=True)
    first, second, third, fourth = (totals[k : k + 1] for k in range(4))
    step = first / second
    later = step * step * third - first
    grown = 1.0 + later / first
    curved = grown * grown * second - 2.0 * step * grown * third + step * step * fourth
    step_next = later / curved
    forward = step + step_next * grown
    aside = step_next * step
    adjoint[...] = forward * direction - aside * scaled
    residual[...] = seed - forward * applied + aside * again
    sends = halo + bundles + slaves + masters + halo_next + slaves_next + masters_next
    for copy in sends + across + along:
        copy.wait_send()


def finish_kernel(found, left, adjoint, residual):
    for source, ref in ((found, adjoint), (left, residual)):
        value = reorder(source[...], False)
        for i in range(3):
            for x in range(8):
                for py in range(2):
                    row = i * 64 + (x % 2 * 2 + py) * 16 + x // 2 * 4
                    ref[i, x, pl.ds(py, 4, stride=2), :] = value[row : row + 4]


def shards(
    seed_grad,
    modulus,
    lumped_mass,
    pair_dest,
    slave_nodes,
    slave_weights,
    master_nodes,
    master_weights,
    penalty,
):
    extents = (lax.axis_size("gx"), lax.axis_size("gy"))
    count = penalty.shape[0]
    args = (
        seed_grad,
        modulus,
        lumped_mass,
        pair_dest.reshape(1, count),
        slave_nodes,
        slave_weights,
        master_nodes,
        master_weights,
        penalty.reshape(1, count),
    )
    scratch = scratch_of(extents, args)
    own = jax.ShapeDtypeStruct((192, 128), F32)
    found, left = pl.pallas_call(
        functools.partial(whole_kernel, extents, tuple(scratch)),
        out_shape=[own, own],
        in_specs=[pl.BlockSpec(memory_space=pl.ANY)] * len(args),
        out_specs=[VMEM, VMEM],
        scratch_shapes=list(scratch.values()),
        compiler_params=pltpu.CompilerParams(
            collective_id=1, has_side_effects=True, vmem_limit_bytes=LIMIT
        ),
        name="conjugate_gradients",
    )(*args)
    field = jax.ShapeDtypeStruct(seed_grad.shape, F32)
    return tuple(
        pl.pallas_call(
            finish_kernel,
            out_shape=[field, field],
            in_specs=[VMEM, VMEM],
            out_specs=[VMEM, VMEM],
            compiler_params=pltpu.CompilerParams(vmem_limit_bytes=LIMIT),
            name="finish",
        )(found, left)
    )


def solution(mesh):
    placed = (
        P(None, "gx", "gy", None),
        P("gx", "gy", None),
        P("gx", "gy", None),
        P(("gx", "gy"), None),
        P(None, ("gx", "gy")),
        P(None, ("gx", "gy")),
        P(None, ("gx", "gy")),
        P(None, ("gx", "gy")),
        P(("gx", "gy")),
    )
    return jax.shard_map(
        shards,
        mesh=mesh,
        in_specs=placed,
        out_specs=(P(None, "gx", "gy", None), P(None, "gx", "gy", None)),
        check_vma=False,
    )
```

```python
import functools
import math

import jax
import jax.numpy as jnp
import numpy as np
from jax import lax
from jax.experimental import pallas as pl
from jax.experimental.pallas import tpu as pltpu
from jax.sharding import PartitionSpec as P

CAP = 256
SHEAR = 1.0 / 2.6
LAME = 0.3 / 0.52
MESH = pl.DeviceIdType.MESH
F32 = jnp.float32
BF16 = jnp.bfloat16
VMEM = pl.BlockSpec(memory_space=pltpu.VMEM)
LIMIT = 64 * 1024 * 1024

WIDE = 72


def shape_tables():
    abscissa = 1.0 / math.sqrt(3.0)
    points = [
        (a, b, c)
        for a in (-abscissa, abscissa)
        for b in (-abscissa, abscissa)
        for c in (-abscissa, abscissa)
    ]
    offsets = [
        (i, j, k)
        for i in range(3)
        for j in range(3)
        for k in range(3)
        if (i == 1) + (j == 1) + (k == 1) <= 1
    ]
    derivative = np.zeros((8, 3, 20))
    for g, location in enumerate(points):
        for n, offset in enumerate(offsets):
            natural = [offset[d] - 1 for d in range(3)]
            factors = [
                1.0 - location[d] ** 2 if natural[d] == 0 else 1.0 + location[d] * natural[d]
                for d in range(3)
            ]
            slopes = [
                -2.0 * location[d] if natural[d] == 0 else float(natural[d]) for d in range(3)
            ]
            linear = sum(location[d] * natural[d] for d in range(3)) - 2.0
            for d in range(3):
                others = factors[(d + 1) % 3] * factors[(d + 2) % 3]
                if 0 in natural:
                    derivative[g, d, n] = slopes[d] * others / 4.0
                else:
                    derivative[g, d, n] = natural[d] * others * (linear + factors[d]) / 8.0
    return derivative, offsets


def signs(count, dims):
    table = np.ones((count, count))
    for t in range(count):
        for c in range(count):
            for d in range(dims):
                if t >> d & 1 and not c >> d & 1:
                    table[t, c] = -table[t, c]
    return table


def element_tables():
    derivative, offsets = shape_tables()
    eight, four = signs(8, 3), signs(4, 2)
    modal = np.einsum("sg,gan->asn", eight, derivative) / 8.0
    corner_at = [offsets.index((c >> 2 << 1, (c >> 1 & 1) << 1, (c & 1) << 1)) for c in range(8)]
    edge_at = []
    for d in range(3):
        row = []
        for c in range(4):
            offset = [(c >> 1) << 1, (c & 1) << 1]
            offset.insert(d, 1)
            row.append(offsets.index(tuple(offset)))
        edge_at.append(row)
    corner_terms = np.einsum("tn,asn->ast", eight, modal[:, :, corner_at]) / 8.0
    edge_terms = [np.einsum("tn,asn->ast", four, modal[:, :, edge_at[d]]) / 4.0 for d in range(3)]
    trilinear = np.array([(1.0 / math.sqrt(3.0)) ** bin(t).count("1") / 8.0 for t in range(8)])
    at_points = np.einsum("t,tg->gt", trilinear, eight)
    squares = derivative * derivative
    weight = np.einsum(
        "gt,gni->tni",
        at_points,
        SHEAR * squares.sum(axis=1)[:, :, None] + (LAME + SHEAR) * np.swapaxes(squares, 1, 2),
    )
    corner_diag = np.einsum("un,tni->uti", eight, weight[:, corner_at]) / 8.0
    edge_diag = [np.einsum("un,tni->uti", four, weight[:, edge_at[d]]) / 4.0 for d in range(3)]
    return corner_terms, edge_terms, trilinear, corner_diag, edge_diag


def split_sums(values):
    values = list(values)
    step = 1
    while step < len(values):
        for low in range(len(values)):
            if not low & step:
                a, b = values[low], values[low | step]
                values[low], values[low | step] = b + a, b - a
        step *= 2
    return values


def join_sums(values):
    values = list(values)
    step = 1
    while step < len(values):
        for low in range(len(values)):
            if not low & step:
                a, b = values[low], values[low | step]
                values[low], values[low | step] = a - b, a + b
        step *= 2
    return values


def combine(terms):
    total = None
    for factor, value in terms:
        if abs(factor) < 1e-12:
            continue
        term = value * np.float32(factor)
        total = term if total is None else total + term
    return total


def lanes(rows):
    return lax.broadcasted_iota(jnp.int32, (rows, 128), 1)


def shift_down(value):
    return jnp.where(lanes(value.shape[0]) == 63, 0.0, pltpu.roll(value, 127, 1))


def collect(low, middle, high):
    total = low + jnp.where(lanes(8) < 64, pltpu.roll(high, 1, 1), 0.0)
    if middle is not None:
        total = total + pltpu.roll(middle, 64, 1)
    return total


def corner_moduli(wide_mod, wide_mod_up, group):
    values = []
    for c in range(8):
        ref = wide_mod_up if c & 1 else wide_mod
        values.append(ref[pl.ds(8 * (group + (c >> 2)) + (c >> 1 & 1), 8), :])
    inside = lanes(8) < 64
    return split_sums([jnp.where(inside, value, 0.0) for value in values])


def edge_corner(d, c):
    where = [c >> 1, c & 1]
    where.insert(d, None)
    return where


def add_rows(ref, index, row, value):
    ref[index + (pl.ds(row, 8), slice(None))] += value


def scatter_forces(out, i, corner, edges, group):
    for xy in range(4):
        row = 8 * (group + (xy >> 1)) + (xy & 1)
        add_rows(out, (i, 0), row, collect(corner[2 * xy], edges[2][xy], corner[2 * xy + 1]))
    for y in range(2):
        add_rows(out, (i, 2), 8 * group + y, collect(edges[0][2 * y], None, edges[0][2 * y + 1]))
    for x in range(2):
        add_rows(
            out, (i, 1), 8 * (group + x), collect(edges[1][2 * x], None, edges[1][2 * x + 1])
        )


def diagonal_into(out, wide_mod, wide_mod_up):
    corner_diag, edge_diag = element_tables()[3:]
    out[...] = jnp.zeros_like(out)
    for group in range(7):
        moduli = corner_moduli(wide_mod, wide_mod_up, group)
        for i in range(3):
            corner = join_sums(
                [
                    combine([(corner_diag[u, t, i], moduli[t]) for t in range(8)])
                    for u in range(8)
                ]
            )
            edges = [
                join_sums(
                    [
                        combine([(edge_diag[d][u, t, i], moduli[t]) for t in range(8)])
                        for u in range(4)
                    ]
                )
                for d in range(3)
            ]
            scatter_forces(out, i, corner, edges, group)


def stiffness_into(out, wide, wide_up, wide_mid, wide_mod, wide_mod_up):
    corner_terms, edge_terms, trilinear = element_tables()[:3]
    out[...] = jnp.zeros_like(out)
    for group in range(1, 6):
        moduli = corner_moduli(wide_mod, wide_mod_up, group)
        points = join_sums([moduli[t] * np.float32(trilinear[t]) for t in range(8)])
        slopes = []
        for i in range(3):
            corner = []
            for c in range(8):
                ref = wide_up if c & 1 else wide
                corner.append(ref[i, 0, pl.ds(8 * (group + (c >> 2)) + (c >> 1 & 1), 8), :])
            corner = split_sums(corner)
            edges = []
            for d in range(3):
                values = []
                for c in range(4):
                    x, y, z = edge_corner(d, c)
                    row = 8 * (group + (x or 0)) + (y or 0)
                    parity = (2, 1, 0)[d]
                    if d == 2:
                        values.append(wide_mid[i, pl.ds(row, 8), :])
                    else:
                        values.append((wide_up if z else wide)[i, parity, pl.ds(row, 8), :])
                edges.append(split_sums(values))
            slopes.append(
                [
                    [
                        combine(
                            [(corner_terms[a, s, t], corner[t]) for t in range(8)]
                            + [
                                (edge_terms[d][a, s, t], edges[d][t])
                                for d in range(3)
                                for t in range(4)
                            ]
                        )
                        for s in range(8)
                    ]
                    for a in range(3)
                ]
            )

        def plus(a, b):
            return a if b is None else b if a is None else a + b

        zero = jnp.zeros((8, 128), F32)
        strain = {}
        for a in range(3):
            strain[a, a] = slopes[a][a]
            for b in range(a):
                strain[b, a] = [plus(p, q) for p, q in zip(slopes[a][b], slopes[b][a])]
        strain = {
            key: join_sums([zero if v is None else v for v in value])
            for key, value in strain.items()
        }
        stress = {key: [] for key in strain}
        for g in range(8):
            volume = (strain[0, 0][g] + strain[1, 1][g] + strain[2, 2][g]) * np.float32(LAME)
            for a in range(3):
                stress[a, a].append(
                    points[g] * (volume + strain[a, a][g] * np.float32(2.0 * SHEAR))
                )
            scaled = points[g] * np.float32(SHEAR)
            for key in ((0, 1), (0, 2), (1, 2)):
                stress[key].append(scaled * strain[key][g])
        stress = {key: split_sums(value) for key, value in stress.items()}
        for i in range(3):
            pairs = [
                (a, s, stress[min(a, i), max(a, i)][s]) for a in range(3) for s in range(8)
            ]
            corner = join_sums(
                [combine([(corner_terms[a, s, t], v) for a, s, v in pairs]) for t in range(8)]
            )
            edges = [
                join_sums(
                    [combine([(edge_terms[d][a, s, t], v) for a, s, v in pairs]) for t in range(4)]
                )
                for d in range(3)
            ]
            scatter_forces(out, i, corner, edges, group)


def lift(wide, wide_up, wide_mid):
    for i in range(3):
        for parity in range(3):
            wide_up[i, parity] = shift_down(wide[i, parity])
        wide_mid[i] = pltpu.roll(wide[i, 0], 64, 1)


def halo_plan(fields, modulus=None):
    plan, first = [], 0
    for dx in (-1, 0, 1):
        for dy in (-1, 0, 1):
            if dx == 0 and dy == 0:
                continue
            pieces = []

            def places(step, both):
                if step == 1:
                    return [(p, 3, 1) for p in ((0, 1) if both else (0,))]
                return [(0, 0, 6)]

            def strips(array, xs, ys):
                for px, ox, wx in xs:
                    for py, oy, wy in ys:
                        if ox is None:
                            pieces.append((array, px * 2 + py, oy, 4, 4, 8 * 2 + wy, 8))
                        elif oy is None:
                            pieces.append((array, px * 2 + py, 4 * ox, 4, 1, 8 * wx + 2, 1))
                        else:
                            pieces.append((array, px * 2 + py, 4 * ox + oy, 1, 1, 8 * wx + wy, 1))

            every = [(0, None, None), (1, None, None)]
            for array in range(fields):
                strips(
                    array,
                    every if dx == 0 else places(dx, True),
                    every if dy == 0 else places(dy, True),
                )
            if modulus is not None:
                deep = {1: [(0, 3, 1), (0, 2, 0)], -1: [(0, 0, 6), (0, 1, 7)], 0: every[:1]}
                strips(modulus, deep[dx], deep[dy])
            rows = sum(piece[3] for piece in pieces)
            plan.append((dx, dy, first, -(-rows // 8) * 8, pieces))
            first += plan[-1][3]
    return plan, first


MODULUS_PLAN, MODULUS_ROWS = halo_plan(0, 4)
FIRST_PLAN, FIRST_ROWS = halo_plan(4)
NEXT_PLAN, NEXT_ROWS = halo_plan(3)


def rows_of(start, count, stride):
    return pl.ds(start, count) if stride == 1 else pl.ds(start, count, stride=stride)


def pack_halo(plan, own, message):
    message[...] = jnp.zeros_like(message)
    for _, _, first, _, pieces in plan:
        at = first
        for array, parity, start, count, stride, _, _ in pieces:
            source = own[rows_of(array * 64 + parity * 16 + start, count, stride), :]
            message[pl.ds(at, count), :] = source
            at += count


def unpack_halo(plan, extents, message, store):
    gx, gy = lax.axis_index("gx"), lax.axis_index("gy")
    for dx, dy, first, _, pieces in plan:
        inside = None
        for step, at, extent in ((dx, gx, extents[0]), (dy, gy, extents[1])):
            if step:
                here = at > 0 if step == 1 else at < extent - 1
                inside = here if inside is None else jnp.logical_and(inside, here)
        keep = jnp.where(inside, 1.0, 0.0).astype(F32)
        at = first
        for array, parity, _, count, _, start, stride in pieces:
            store(array, parity, start, count, stride, message[pl.ds(at, count), :] * keep)
            at += count


def widen_own(own, array, wide, i):
    for parity in range(4):
        for x in range(4):
            wide[i, parity, pl.ds(8 * (x + 2) + 2, 4), :] = own[
                pl.ds(array * 64 + parity * 16 + 4 * x, 4), :
            ]


def narrow(wide, i, own, array):
    for parity in range(4):
        for x in range(4):
            own[pl.ds(array * 64 + parity * 16 + 4 * x, 4), :] = wide[
                i, parity, pl.ds(8 * (x + 2) + 2, 4), :
            ]


def in_two(value):
    head = value.astype(BF16)
    return head, (value - head.astype(F32)).astype(BF16)


def down_iota(rows, columns):
    return lax.broadcasted_iota(jnp.int32, (rows, columns), 0).astype(F32).astype(BF16)


def ones_where(rows, labels):
    columns = labels.shape[1]
    return jnp.where(
        down_iota(rows, columns) == labels.astype(BF16), jnp.ones((), BF16), jnp.zeros((), BF16)
    )


def dot(a, b, transposed=False):
    return lax.dot_general(
        a, b, (((1,), (1 if transposed else 0,)), ((), ())), preferred_element_type=F32
    )


BLOCK = CAP


def picks_of(lane, extent):
    return jnp.concatenate([ones_where(extent, lane[j : j + 1]) for j in range(4)], axis=1)


def gather_block(table, block):
    count = block.shape[1]
    picks = picks_of(block[12:16], 128)
    found = dot(table, jnp.concatenate([picks, picks], axis=0))
    down = lax.broadcasted_iota(jnp.int32, (64, count), 0).astype(F32)
    factors = [
        jnp.where(down == block[8 + j : 9 + j], block[j : j + 1], 0.0) for j in range(4)
    ]
    result = []
    for i in range(3):
        total = sum(
            factors[j] * found[64 * i : 64 * (i + 1), count * j : count * (j + 1)]
            for j in range(4)
        )
        result.append(jnp.sum(total, axis=0, keepdims=True))
    return jnp.concatenate(result, axis=0)


def scatter_block(block, traction):
    upper = jnp.where(block[8:12] >= 32.0, 1.0, 0.0)
    row, lane = block[8:12] - 32.0 * upper, block[12:16] + 128.0 * upper
    rows = [ones_where(32, row[j : j + 1]) for j in range(4)]
    parts = [
        [in_two(block[j : j + 1] * traction[i : i + 1]) for j in range(4)] for i in range(3)
    ]
    left = [
        jnp.concatenate([rows[j] * parts[i][j][part] for j in range(4)], axis=1)
        for part in range(2)
        for i in range(3)
    ]
    return dot(jnp.concatenate(left, axis=0), picks_of(lane, 256), True)


def total_rows(total):
    value = total[0:96, :] + total[96:192, :]
    return jnp.concatenate(
        [
            value[32 * i : 32 * (i + 1), 128 * half : 128 * (half + 1)]
            for i in range(3)
            for half in range(2)
        ],
        axis=0,
    )


def table_of(value):
    head, tail = in_two(value)
    return jnp.concatenate([head, tail], axis=1)


def each(first, last, body, unroll):
    def step(k, carry):
        body(k)
        return carry

    lax.fori_loop(first, last, step, 0, unroll=unroll)


def gather_slaves(table, segments, mine, theirs, places, group):
    mine[...] = jnp.zeros_like(mine)

    def slave(k):
        at = pl.ds(pl.multiple_of(k * BLOCK, BLOCK), BLOCK)
        mine[0:3, at] = gather_block(table, segments[:, at])

    each(0, segments.shape[1] // BLOCK, slave, 4)
    head, tail = in_two(mine[...])
    both = jnp.concatenate([head, tail], axis=0)
    target = segments[5:6, :]
    left = jnp.concatenate(
        [jnp.where(target == t, 1.0, 0.0).astype(BF16) * both for t in range(group)], axis=0
    )
    placed = dot(left, places[...], True).reshape(group, 16, CAP)
    theirs[...] = placed[:, 0:4] + placed[:, 8:12]


def gather_masters(table, bundle, theirs, group, me, first, last):
    def master(k):
        source = lax.rem(me + k, group)
        theirs[source, 0:3, :] = gather_block(table, bundle[source])

    each(first, last, master, 8)


def pull_slaves(segments, mine, returned, places, pulls, group):
    nothing = jnp.zeros((4, CAP), F32)
    slots = jnp.concatenate([v for t in range(group) for v in (returned[t], nothing)], axis=0)
    head, tail = in_two(slots)
    found = dot(
        jnp.concatenate([head, tail], axis=1),
        jnp.concatenate([places[...], places[...]], axis=0),
    )
    target = segments[5:6, :]
    back = sum(jnp.where(target == t, 1.0, 0.0) * found[8 * t : 8 * (t + 1)] for t in range(group))
    pulls[0:3, :] = segments[4:5, :] * (mine[0:3, :] - back[0:3, :])


def scatter_slaves(total, segments, pulls):
    def slave(k):
        at = pl.ds(pl.multiple_of(k * 2 * BLOCK, 2 * BLOCK), 2 * BLOCK)
        total[...] += scatter_block(segments[:, at], pulls[0:3, at])

    each(0, segments.shape[1] // (2 * BLOCK), slave, 2)


def scatter_masters(total, bundle, sent, arrived, first, last):
    def master(k):
        pair = [2 * k, 2 * k + 1]
        block = jnp.concatenate([bundle[source] for source in pair], axis=1)
        gap = [sent[source, 0:3, :] - arrived[source, 0:3, :] for source in pair]
        total[...] += scatter_block(block, block[4:5] * jnp.concatenate(gap, axis=1))

    each(first // 2, last // 2, master, 4)


def swap_lanes(forth):
    a = lax.broadcasted_iota(jnp.int32, (128, 128), 0 if forth else 1)
    b = lax.broadcasted_iota(jnp.int32, (128, 128), 1 if forth else 0)
    return jnp.where(b == (a % 2) * 64 + a // 2, 1.0, 0.0).astype(F32)


def reorder(value, forth):
    head = value.astype(BF16)
    rest = value - head.astype(F32)
    middle = rest.astype(BF16)
    tail = (rest - middle.astype(F32)).astype(BF16)
    swap = swap_lanes(forth).astype(BF16)
    return dot(
        jnp.concatenate([head, middle, tail], axis=1), jnp.concatenate([swap, swap, swap], axis=0)
    )


def lay_out(fields, first, own, swapped):
    values = [field[...].reshape(-1, 128) for field in fields]
    value = reorder(values[0] if len(values) == 1 else jnp.concatenate(values, axis=0), True)
    count = value.shape[0] // 64
    swapped[pl.ds(first, count)] = value.reshape(count, 8, 8, 128)
    for array in range(first, first + count):
        for x in range(8):
            for py in range(2):
                row = array * 64 + (x % 2 * 2 + py) * 16 + x // 2 * 4
                own[pl.ds(row, 4), :] = swapped[array, x, pl.ds(py, 4, stride=2), :]


def place_of(node):
    x, y, z = node // 1024, node // 128 % 8, node % 128
    row = (x % 2 * 2 + y % 2) * 16 + x // 2 * 4 + y // 2
    return row.astype(F32), (z % 2 * 64 + z // 2).astype(F32)


def place_segments(
    group,
    pair,
    slave_nodes,
    slave_weights,
    master_nodes,
    master_weights,
    penalty,
    packed,
    segments,
    places,
):
    slave_row, slave_lane = place_of(slave_nodes[...])
    master_row, master_lane = place_of(master_nodes[...])
    target = pair[...].astype(F32)
    count = target.shape[1]
    chosen = ones_where(group, target)
    a = lax.broadcasted_iota(jnp.int32, (128, 128), 0)
    b = lax.broadcasted_iota(jnp.int32, (128, 128), 1)
    before = jnp.where(a < b, 1.0, 0.0).astype(BF16)
    ranks, base = [], jnp.zeros((group, 1), F32)
    for k in range(count // 128):
        part = chosen[:, 128 * k : 128 * (k + 1)]
        wide = part.astype(F32)
        rank = dot(part, before) + base
        ranks.append(jnp.sum(rank * wide, axis=0, keepdims=True))
        base = base + jnp.sum(wide, axis=1, keepdims=True)
    position = jnp.concatenate(ranks, axis=1)
    segments[0:4, :] = slave_weights[...]
    segments[4:5, :] = penalty[...]
    segments[5:6, :] = target
    segments[6:7, :] = position
    segments[7:8, :] = jnp.zeros_like(position)
    segments[8:12, :] = slave_row
    segments[12:16, :] = slave_lane
    spots = ones_where(CAP, position)
    places[...] = spots
    nothing = jnp.zeros((3, count), F32)
    values = jnp.concatenate([master_weights[...], penalty[...], nothing], axis=0)
    head, tail = in_two(values)
    nodes = jnp.concatenate([master_row, master_lane], axis=0)
    sent = jnp.concatenate([head, tail, nodes.astype(BF16), jnp.zeros((8, count), BF16)], axis=0)
    left = jnp.concatenate(
        [jnp.where(target == t, 1.0, 0.0).astype(BF16) * sent for t in range(group)], axis=0
    )
    placed = dot(left, spots, True).reshape(group, 32, CAP)
    packed[:, 0:8] = placed[:, 0:8] + placed[:, 8:16]
    packed[:, 8:16] = placed[:, 16:24]


def inner(a, b):
    return jnp.sum(a * b, axis=0, keepdims=True)


INPUTS = (
    "seed",
    "modulus",
    "mass",
    "pair",
    "slave_nodes",
    "slave_weights",
    "master_nodes",
    "master_weights",
    "penalty",
)


KINDS = (
    "modulus",
    "halo",
    "packed",
    "slaves",
    "masters",
    "halo_next",
    "slaves_next",
    "masters_next",
    "across",
    "along",
)


def scratch_of(extents, args):
    group, count = extents[1], args[-1].shape[-1]
    dma, parts, field = pltpu.SemaphoreType.DMA, (group, 4, CAP), (3, 4, WIDE, 128)
    room = {name: pltpu.VMEM(arg.shape, arg.dtype) for name, arg in zip(INPUTS, args)}
    shapes = {
        "own": (320, 128),
        "swapped": (5, 8, 8, 128),
        "segments": (16, count),
        "packed": (group, 16, CAP),
        "bundle": (group, 16, CAP),
        "modulus_out": (MODULUS_ROWS, 128),
        "modulus_in": (MODULUS_ROWS, 128),
        "halo_out": (FIRST_ROWS, 128),
        "halo_in": (FIRST_ROWS, 128),
        "halo_out_next": (NEXT_ROWS, 128),
        "halo_in_next": (NEXT_ROWS, 128),
        "mine": (8, count),
        "mine_next": (8, count),
        "slaves_out": parts,
        "slaves_in": parts,
        "masters_out": parts,
        "masters_in": parts,
        "slaves_out_next": parts,
        "slaves_in_next": parts,
        "masters_out_next": parts,
        "masters_in_next": parts,
        "kept": (576, 128),
        "fields": (384, 128),
        "last": (192, 128),
        "wide_mod": (WIDE, 128),
        "wide_mod_up": (WIDE, 128),
        "mass_wide": (1, 4, WIDE, 128),
        "wide": field,
        "wide_up": (3, 3, WIDE, 128),
        "wide_mid": (3, WIDE, 128),
        "out": field,
        "total": (192, 256),
        "pulls": (8, count),
        "tile": (8, 128),
        "middle": (8, 128),
        "across": (extents[0], 8, 128),
        "along": (group, 8, 128),
    }
    room.update({name: pltpu.VMEM(shape, F32) for name, shape in shapes.items()})
    room["places"] = pltpu.VMEM((CAP, count), BF16)
    room["loads"] = dma((len(INPUTS),))
    room["sends"] = dma((len(KINDS),))
    room["receives"] = dma((len(KINDS),))
    return room


class Refs:
    def __init__(self, names, refs):
        self.__dict__.update(zip(names, refs))


def whole_kernel(extents, names, *refs):
    inputs, (adjoint, residual) = refs[: len(INPUTS)], refs[len(INPUTS) : len(INPUTS) + 2]
    r = Refs(names, refs[len(INPUTS) + 2 :])
    wide, group = extents
    gx, gy = lax.axis_index("gx"), lax.axis_index("gy")
    loads = {
        name: pltpu.make_async_copy(ref, getattr(r, name), r.loads.at[k])
        for k, (name, ref) in enumerate(zip(INPUTS, inputs))
    }
    for name in sorted(loads, key=lambda name: name != "modulus"):
        loads[name].start()

    def beside(dx, dy):
        return lax.rem(gx + dx + wide, wide), lax.rem(gy + dy + group, group)

    barrier = pltpu.get_barrier_semaphore()
    peers = [(dx, dy) for dx, dy, _, _, _ in FIRST_PLAN]
    peers += [(k, 0) for k in range(2, wide - 1)] + [(0, k) for k in range(2, group - 1)]
    for dx, dy in peers:
        pl.semaphore_signal(barrier, inc=1, device_id=beside(dx, dy), device_id_type=MESH)

    def copy_of(kind, source, target, device):
        k = KINDS.index(kind)
        return pltpu.make_async_remote_copy(
            src_ref=source,
            dst_ref=target,
            send_sem=r.sends.at[k],
            recv_sem=r.receives.at[k],
            device_id=device,
            device_id_type=MESH,
        )

    def all_of(kind, buffer, count=None):
        part = buffer if count is None else buffer.at[pl.ds(0, count)]
        return copy_of(kind, part, part, beside(0, 1))

    whole = {
        "modulus": all_of("modulus", r.modulus_in),
        "halo": all_of("halo", r.halo_in),
        "packed": all_of("packed", r.bundle, group - 1),
        "slaves": all_of("slaves", r.slaves_in, group - 1),
        "masters": all_of("masters", r.masters_in, group - 1),
        "halo_next": all_of("halo_next", r.halo_in_next),
        "slaves_next": all_of("slaves_next", r.slaves_in_next, group - 1),
        "masters_next": all_of("masters_next", r.masters_in_next, group - 1),
        "across": all_of("across", r.across, wide - 1),
        "along": all_of("along", r.along, group - 1),
    }

    def receive(kind):
        whole[kind].wait_recv()

    def send_halo(plan, source, target, kind):
        for dx, dy, at, rows, _ in plan:
            part = pl.ds(at, rows)
            copy_of(kind, source.at[part], target.at[part], beside(dx, dy)).start()

    def send_blocks(source, target, kind, first=1, last=group):
        for k in range(first, last):
            device = beside(0, k)
            copy_of(kind, source.at[device[1]], target.at[gy], device).start()
        if first == 1:
            target[gy] = source[gy]

    loads["modulus"].wait()
    lay_out([r.modulus], 4, r.own, r.swapped)
    pack_halo(MODULUS_PLAN, r.own, r.modulus_out)
    pl.semaphore_wait(barrier, len(peers))
    send_halo(MODULUS_PLAN, r.modulus_out, r.modulus_in, "modulus")
    loads["seed"].wait()
    loads["mass"].wait()
    lay_out([r.seed, r.mass], 0, r.own, r.swapped)
    pack_halo(FIRST_PLAN, r.own, r.halo_out)
    send_halo(FIRST_PLAN, r.halo_out, r.halo_in, "halo")
    for name in INPUTS[3:]:
        loads[name].wait()
    place_segments(
        group,
        r.pair,
        r.slave_nodes,
        r.slave_weights,
        r.master_nodes,
        r.master_weights,
        r.penalty,
        r.packed,
        r.segments,
        r.places,
    )
    send_blocks(r.packed, r.bundle, "packed")

    r.wide[...] = jnp.zeros_like(r.wide)
    r.mass_wide[...] = jnp.zeros_like(r.mass_wide)
    r.wide_mod[...] = jnp.zeros_like(r.wide_mod)
    for i in range(3):
        widen_own(r.own, i, r.wide, i)
    widen_own(r.own, 3, r.mass_wide, 0)
    for x in range(4):
        r.wide_mod[pl.ds(8 * (x + 2) + 2, 4), :] = r.own[pl.ds(4 * 64 + 4 * x, 4), :]
    for buffer in (r.masters_out, r.masters_out_next):
        buffer[...] = jnp.zeros_like(buffer)

    def store_modulus(array, parity, start, count, stride, value):
        r.wide_mod[rows_of(start, count, stride), :] = value

    receive("modulus")
    unpack_halo(MODULUS_PLAN, extents, r.modulus_in, store_modulus)
    r.wide_mod_up[...] = shift_down(r.wide_mod[...])
    diagonal_into(r.out, r.wide_mod, r.wide_mod_up)
    for i in range(3):
        narrow(r.out, i, r.kept, 3 + i)
    mass = r.own[192:256, :]
    masses = jnp.concatenate([mass, mass, mass], axis=0)
    r.kept[192:384, :] = 1.0 / (r.kept[192:384, :] + masses)
    r.kept[0:192, :] = r.own[0:192, :] * r.kept[192:384, :]
    table = table_of(r.kept[0:192, :])
    gather_slaves(table, r.segments, r.mine, r.slaves_out, r.places, group)
    send_blocks(r.slaves_out, r.slaves_in, "slaves")
    receive("packed")
    gather_masters(table, r.bundle, r.masters_out, group, gy, 0, group // 2)
    send_blocks(r.masters_out, r.masters_in, "masters", 1, group // 2)
    gather_masters(table, r.bundle, r.masters_out, group, gy, group // 2, group)
    send_blocks(r.masters_out, r.masters_in, "masters", group // 2, group)

    def store(array, parity, start, count, stride, value):
        at = rows_of(start, count, stride)
        if array < 3:
            r.wide[array, parity, at, :] = value
        else:
            r.mass_wide[0, parity, at, :] = value

    receive("halo")
    unpack_halo(FIRST_PLAN, extents, r.halo_in, store)
    for i in range(3):
        for parity in range(4):
            wide_mass = r.mass_wide[0, parity]
            inverse = jnp.where(wide_mass > 0.0, 1.0 / (r.out[i, parity] + wide_mass), 0.0)
            r.wide[i, parity] = r.wide[i, parity] * inverse

    def stiffness():
        lift(r.wide, r.wide_up, r.wide_mid)
        stiffness_into(r.out, r.wide, r.wide_up, r.wide_mid, r.wide_mod, r.wide_mod_up)

    stiffness()
    for i in range(3):
        narrow(r.out, i, r.kept, 6 + i)
    r.kept[384:576, :] += masses * r.kept[0:192, :]

    receive("slaves")
    r.total[...] = jnp.zeros_like(r.total)
    scatter_masters(r.total, r.bundle, r.masters_out, r.slaves_in, 0, group)
    receive("masters")
    pull_slaves(r.segments, r.mine, r.masters_in, r.places, r.pulls, group)
    scatter_slaves(r.total, r.segments, r.pulls)
    applied = r.kept[384:576, :] + total_rows(r.total)
    scaled = applied * r.kept[192:384, :]
    r.fields[0:192, :] = scaled
    r.fields[192:384, :] = applied
    pack_halo(NEXT_PLAN, r.fields, r.halo_out_next)
    send_halo(NEXT_PLAN, r.halo_out_next, r.halo_in_next, "halo_next")
    table = table_of(scaled)
    gather_slaves(table, r.segments, r.mine_next, r.slaves_out_next, r.places, group)
    send_blocks(r.slaves_out_next, r.slaves_in_next, "slaves_next")
    gather_masters(table, r.bundle, r.masters_out_next, group, gy, 0, group // 2)
    send_blocks(r.masters_out_next, r.masters_in_next, "masters_next", 1, group // 2)
    gather_masters(table, r.bundle, r.masters_out_next, group, gy, group // 2, group)
    send_blocks(r.masters_out_next, r.masters_in_next, "masters_next", group // 2, group)

    r.wide[...] = jnp.zeros_like(r.wide)
    for i in range(3):
        widen_own(r.fields, i, r.wide, i)

    def store_next(array, parity, start, count, stride, value):
        r.wide[array, parity, rows_of(start, count, stride), :] = value

    receive("halo_next")
    unpack_halo(NEXT_PLAN, extents, r.halo_in_next, store_next)
    stiffness()
    for i in range(3):
        narrow(r.out, i, r.last, i)
    seed, direction = r.own[0:192, :], r.kept[0:192, :]
    scaled, applied = r.fields[0:192, :], r.fields[192:384, :]
    smooth = r.last[...] + masses * scaled
    r.last[...] = smooth
    r.tile[0:1, :] = inner(seed, direction)
    r.tile[1:2, :] = inner(direction, applied)
    r.tile[2:3, :] = inner(scaled, applied)
    r.tile[4:8, :] = jnp.zeros((4, 128), F32)
    receive("slaves_next")
    pressed = jnp.zeros((3, CAP), F32)
    for source in range(group):
        gap = r.masters_out_next[source, 0:3, :] - r.slaves_in_next[source, 0:3, :]
        pressed = pressed + r.bundle[source, 4:5, :] * gap * gap
    pressed = jnp.sum(pressed, axis=0, keepdims=True)
    energy = inner(scaled, smooth)
    for k in range(CAP // 128):
        energy = energy + pressed[:, 128 * k : 128 * (k + 1)]
    r.tile[3:4, :] = energy
    for k in range(1, wide):
        copy_of("across", r.tile, r.across.at[gx], beside(k, 0)).start()
    r.across[gx] = r.tile[...]

    def masters_from(first, last):
        scatter_masters(r.total, r.bundle, r.masters_out_next, r.slaves_in_next, first, last)

    r.total[...] = jnp.zeros_like(r.total)
    masters_from(0, group // 2)
    receive("across")
    part = jnp.sum(r.across[...], axis=0)
    r.middle[...] = part
    for k in range(1, group):
        copy_of("along", r.middle, r.along.at[gy], beside(0, k)).start()
    r.along[gy] = part
    masters_from(group // 2, group)
    receive("masters_next")
    pull_slaves(r.segments, r.mine_next, r.masters_in_next, r.places, r.pulls, group)
    scatter_slaves(r.total, r.segments, r.pulls)
    again = r.last[...] + total_rows(r.total)
    receive("along")
    totals = jnp.sum(jnp.sum(r.along[...], axis=0), axis=1, keepdims=True)
    first, second, third, fourth = (totals[k : k + 1] for k in range(4))
    step = first / second
    later = step * step * third - first
    grown = 1.0 + later / first
    curved = grown * grown * second - 2.0 * step * grown * third + step * step * fourth
    step_next = later / curved
    forward = step + step_next * grown
    aside = step_next * step
    adjoint[...] = forward * direction - aside * scaled
    residual[...] = seed - forward * applied + aside * again
    for kind in KINDS:
        whole[kind].wait_send()


def finish_kernel(found, left, adjoint, residual):
    for source, ref in ((found, adjoint), (left, residual)):
        value = reorder(source[...], False)
        for i in range(3):
            for x in range(8):
                for py in range(2):
                    row = i * 64 + (x % 2 * 2 + py) * 16 + x // 2 * 4
                    ref[i, x, pl.ds(py, 4, stride=2), :] = value[row : row + 4]


def shards(
    seed_grad,
    modulus,
    lumped_mass,
    pair_dest,
    slave_nodes,
    slave_weights,
    master_nodes,
    master_weights,
    penalty,
):
    extents = (lax.axis_size("gx"), lax.axis_size("gy"))
    count = penalty.shape[0]
    args = (
        seed_grad,
        modulus,
        lumped_mass,
        pair_dest.reshape(1, count),
        slave_nodes,
        slave_weights,
        master_nodes,
        master_weights,
        penalty.reshape(1, count),
    )
    scratch = scratch_of(extents, args)
    own = jax.ShapeDtypeStruct((192, 128), F32)
    found, left = pl.pallas_call(
        functools.partial(whole_kernel, extents, tuple(scratch)),
        out_shape=[own, own],
        in_specs=[pl.BlockSpec(memory_space=pl.ANY)] * len(args),
        out_specs=[VMEM, VMEM],
        scratch_shapes=list(scratch.values()),
        compiler_params=pltpu.CompilerParams(
            collective_id=1, has_side_effects=True, vmem_limit_bytes=LIMIT
        ),
        name="conjugate_gradients",
    )(*args)
    field = jax.ShapeDtypeStruct(seed_grad.shape, F32)
    return tuple(
        pl.pallas_call(
            finish_kernel,
            out_shape=[field, field],
            in_specs=[VMEM, VMEM],
            out_specs=[VMEM, VMEM],
            compiler_params=pltpu.CompilerParams(vmem_limit_bytes=LIMIT),
            name="finish",
        )(found, left)
    )


def solution(mesh):
    placed = (
        P(None, "gx", "gy", None),
        P("gx", "gy", None),
        P("gx", "gy", None),
        P(("gx", "gy"), None),
        P(None, ("gx", "gy")),
        P(None, ("gx", "gy")),
        P(None, ("gx", "gy")),
        P(None, ("gx", "gy")),
        P(("gx", "gy")),
    )
    return jax.shard_map(
        shards,
        mesh=mesh,
        in_specs=placed,
        out_specs=(P(None, "gx", "gy", None), P(None, "gx", "gy", None)),
        check_vma=False,
    )
```

```python
import functools
import math

import jax
import jax.numpy as jnp
import numpy as np
from jax import lax
from jax.experimental import pallas as pl
from jax.experimental.pallas import tpu as pltpu
from jax.sharding import PartitionSpec as P

CAP = 256
SHEAR = 1.0 / 2.6
LAME = 0.3 / 0.52
MESH = pl.DeviceIdType.MESH
F32 = jnp.float32
BF16 = jnp.bfloat16
VMEM = pl.BlockSpec(memory_space=pltpu.VMEM)
LIMIT = 64 * 1024 * 1024

WIDE = 72


def shape_tables():
    abscissa = 1.0 / math.sqrt(3.0)
    points = [
        (a, b, c)
        for a in (-abscissa, abscissa)
        for b in (-abscissa, abscissa)
        for c in (-abscissa, abscissa)
    ]
    offsets = [
        (i, j, k)
        for i in range(3)
        for j in range(3)
        for k in range(3)
        if (i == 1) + (j == 1) + (k == 1) <= 1
    ]
    derivative = np.zeros((8, 3, 20))
    for g, location in enumerate(points):
        for n, offset in enumerate(offsets):
            natural = [offset[d] - 1 for d in range(3)]
            factors = [
                1.0 - location[d] ** 2 if natural[d] == 0 else 1.0 + location[d] * natural[d]
                for d in range(3)
            ]
            slopes = [
                -2.0 * location[d] if natural[d] == 0 else float(natural[d]) for d in range(3)
            ]
            linear = sum(location[d] * natural[d] for d in range(3)) - 2.0
            for d in range(3):
                others = factors[(d + 1) % 3] * factors[(d + 2) % 3]
                if 0 in natural:
                    derivative[g, d, n] = slopes[d] * others / 4.0
                else:
                    derivative[g, d, n] = natural[d] * others * (linear + factors[d]) / 8.0
    return derivative, offsets


def signs(count, dims):
    table = np.ones((count, count))
    for t in range(count):
        for c in range(count):
            for d in range(dims):
                if t >> d & 1 and not c >> d & 1:
                    table[t, c] = -table[t, c]
    return table


def element_tables():
    derivative, offsets = shape_tables()
    eight, four = signs(8, 3), signs(4, 2)
    modal = np.einsum("sg,gan->asn", eight, derivative) / 8.0
    corner_at = [offsets.index((c >> 2 << 1, (c >> 1 & 1) << 1, (c & 1) << 1)) for c in range(8)]
    edge_at = []
    for d in range(3):
        row = []
        for c in range(4):
            offset = [(c >> 1) << 1, (c & 1) << 1]
            offset.insert(d, 1)
            row.append(offsets.index(tuple(offset)))
        edge_at.append(row)
    corner_terms = np.einsum("tn,asn->ast", eight, modal[:, :, corner_at]) / 8.0
    edge_terms = [np.einsum("tn,asn->ast", four, modal[:, :, edge_at[d]]) / 4.0 for d in range(3)]
    trilinear = np.array([(1.0 / math.sqrt(3.0)) ** bin(t).count("1") / 8.0 for t in range(8)])
    at_points = np.einsum("t,tg->gt", trilinear, eight)
    squares = derivative * derivative
    weight = np.einsum(
        "gt,gni->tni",
        at_points,
        SHEAR * squares.sum(axis=1)[:, :, None] + (LAME + SHEAR) * np.swapaxes(squares, 1, 2),
    )
    corner_diag = np.einsum("un,tni->uti", eight, weight[:, corner_at]) / 8.0
    edge_diag = [np.einsum("un,tni->uti", four, weight[:, edge_at[d]]) / 4.0 for d in range(3)]
    return corner_terms, edge_terms, trilinear, corner_diag, edge_diag


def split_sums(values):
    values = list(values)
    step = 1
    while step < len(values):
        for low in range(len(values)):
            if not low & step:
                a, b = values[low], values[low | step]
                values[low], values[low | step] = b + a, b - a
        step *= 2
    return values


def join_sums(values):
    values = list(values)
    step = 1
    while step < len(values):
        for low in range(len(values)):
            if not low & step:
                a, b = values[low], values[low | step]
                values[low], values[low | step] = a - b, a + b
        step *= 2
    return values


def combine(terms):
    total = None
    for factor, value in terms:
        if abs(factor) < 1e-12:
            continue
        term = value * np.float32(factor)
        total = term if total is None else total + term
    return total


def rows_at(group, shift):
    return pl.ds(pl.multiple_of(8 * group, 8) + shift, 8)


def lanes(rows):
    return lax.broadcasted_iota(jnp.int32, (rows, 128), 1)


def shift_down(value):
    return jnp.where(lanes(value.shape[0]) == 63, 0.0, pltpu.roll(value, 127, 1))


def collect(low, middle, high):
    total = low + jnp.where(lanes(8) < 64, pltpu.roll(high, 1, 1), 0.0)
    if middle is not None:
        total = total + pltpu.roll(middle, 64, 1)
    return total


def corner_moduli(wide_mod, wide_mod_up, group):
    values = []
    for c in range(8):
        ref = wide_mod_up if c & 1 else wide_mod
        values.append(ref[rows_at(group + (c >> 2), c >> 1 & 1), :])
    inside = lanes(8) < 64
    return split_sums([jnp.where(inside, value, 0.0) for value in values])


def edge_corner(d, c):
    where = [c >> 1, c & 1]
    where.insert(d, None)
    return where


def add_rows(ref, index, row, value):
    ref[index + (row, slice(None))] += value


def scatter_forces(out, i, corner, edges, group):
    for xy in range(4):
        row = rows_at(group + (xy >> 1), xy & 1)
        add_rows(out, (i, 0), row, collect(corner[2 * xy], edges[2][xy], corner[2 * xy + 1]))
    for y in range(2):
        add_rows(
            out, (i, 2), rows_at(group, y), collect(edges[0][2 * y], None, edges[0][2 * y + 1])
        )
    for x in range(2):
        add_rows(
            out, (i, 1), rows_at(group + x, 0), collect(edges[1][2 * x], None, edges[1][2 * x + 1])
        )


def diagonal_into(out, wide_mod, wide_mod_up):
    corner_diag, edge_diag = element_tables()[3:]
    out[...] = jnp.zeros_like(out)

    def step(group, carry):
        moduli = corner_moduli(wide_mod, wide_mod_up, group)
        for i in range(3):
            corner = join_sums(
                [
                    combine([(corner_diag[u, t, i], moduli[t]) for t in range(8)])
                    for u in range(8)
                ]
            )
            edges = [
                join_sums(
                    [
                        combine([(edge_diag[d][u, t, i], moduli[t]) for t in range(8)])
                        for u in range(4)
                    ]
                )
                for d in range(3)
            ]
            scatter_forces(out, i, corner, edges, group)
        return carry

    lax.fori_loop(0, 7, step, 0, unroll=7)


def stiffness_into(out, wide, wide_up, wide_mid, wide_mod, wide_mod_up):
    corner_terms, edge_terms, trilinear = element_tables()[:3]
    out[...] = jnp.zeros_like(out)

    def step(group, carry):
        moduli = corner_moduli(wide_mod, wide_mod_up, group)
        points = join_sums([moduli[t] * np.float32(trilinear[t]) for t in range(8)])
        slopes = []
        for i in range(3):
            corner = []
            for c in range(8):
                ref = wide_up if c & 1 else wide
                corner.append(ref[i, 0, rows_at(group + (c >> 2), c >> 1 & 1), :])
            corner = split_sums(corner)
            edges = []
            for d in range(3):
                values = []
                for c in range(4):
                    x, y, z = edge_corner(d, c)
                    row = rows_at(group + (x or 0), y or 0)
                    parity = (2, 1, 0)[d]
                    if d == 2:
                        values.append(wide_mid[i, row, :])
                    else:
                        values.append((wide_up if z else wide)[i, parity, row, :])
                edges.append(split_sums(values))
            slopes.append(
                [
                    [
                        combine(
                            [(corner_terms[a, s, t], corner[t]) for t in range(8)]
                            + [
                                (edge_terms[d][a, s, t], edges[d][t])
                                for d in range(3)
                                for t in range(4)
                            ]
                        )
                        for s in range(8)
                    ]
                    for a in range(3)
                ]
            )

        def plus(a, b):
            return a if b is None else b if a is None else a + b

        zero = jnp.zeros((8, 128), F32)
        strain = {}
        for a in range(3):
            strain[a, a] = slopes[a][a]
            for b in range(a):
                strain[b, a] = [plus(p, q) for p, q in zip(slopes[a][b], slopes[b][a])]
        strain = {
            key: join_sums([zero if v is None else v for v in value])
            for key, value in strain.items()
        }
        stress = {key: [] for key in strain}
        for g in range(8):
            volume = (strain[0, 0][g] + strain[1, 1][g] + strain[2, 2][g]) * np.float32(LAME)
            for a in range(3):
                stress[a, a].append(
                    points[g] * (volume + strain[a, a][g] * np.float32(2.0 * SHEAR))
                )
            scaled = points[g] * np.float32(SHEAR)
            for key in ((0, 1), (0, 2), (1, 2)):
                stress[key].append(scaled * strain[key][g])
        stress = {key: split_sums(value) for key, value in stress.items()}
        for i in range(3):
            pairs = [
                (a, s, stress[min(a, i), max(a, i)][s]) for a in range(3) for s in range(8)
            ]
            corner = join_sums(
                [combine([(corner_terms[a, s, t], v) for a, s, v in pairs]) for t in range(8)]
            )
            edges = [
                join_sums(
                    [combine([(edge_terms[d][a, s, t], v) for a, s, v in pairs]) for t in range(4)]
                )
                for d in range(3)
            ]
            scatter_forces(out, i, corner, edges, group)
        return carry

    lax.fori_loop(1, 6, step, 0, unroll=5)


def lift(wide, wide_up, wide_mid):
    for i in range(3):
        for parity in range(3):
            wide_up[i, parity] = shift_down(wide[i, parity])
        wide_mid[i] = pltpu.roll(wide[i, 0], 64, 1)


def halo_plan(fields, modulus=None):
    plan, first = [], 0
    for dx in (-1, 0, 1):
        for dy in (-1, 0, 1):
            if dx == 0 and dy == 0:
                continue
            pieces = []

            def places(step, both):
                if step == 1:
                    return [(p, 3, 1) for p in ((0, 1) if both else (0,))]
                return [(0, 0, 6)]

            def strips(array, xs, ys):
                for px, ox, wx in xs:
                    for py, oy, wy in ys:
                        if ox is None:
                            pieces.append((array, px * 2 + py, oy, 4, 4, 8 * 2 + wy, 8))
                        elif oy is None:
                            pieces.append((array, px * 2 + py, 4 * ox, 4, 1, 8 * wx + 2, 1))
                        else:
                            pieces.append((array, px * 2 + py, 4 * ox + oy, 1, 1, 8 * wx + wy, 1))

            every = [(0, None, None), (1, None, None)]
            for array in range(fields):
                strips(
                    array,
                    every if dx == 0 else places(dx, True),
                    every if dy == 0 else places(dy, True),
                )
            if modulus is not None:
                deep = {1: [(0, 3, 1), (0, 2, 0)], -1: [(0, 0, 6), (0, 1, 7)], 0: every[:1]}
                strips(modulus, deep[dx], deep[dy])
            rows = sum(piece[3] for piece in pieces)
            plan.append((dx, dy, first, -(-rows // 8) * 8, pieces))
            first += plan[-1][3]
    return plan, first


MODULUS_PLAN, MODULUS_ROWS = halo_plan(0, 4)
FIRST_PLAN, FIRST_ROWS = halo_plan(4)
NEXT_PLAN, NEXT_ROWS = halo_plan(3)


def rows_of(start, count, stride):
    return pl.ds(start, count) if stride == 1 else pl.ds(start, count, stride=stride)


def pack_halo(plan, own, message):
    message[...] = jnp.zeros_like(message)
    for _, _, first, _, pieces in plan:
        at = first
        for array, parity, start, count, stride, _, _ in pieces:
            source = own[rows_of(array * 64 + parity * 16 + start, count, stride), :]
            message[pl.ds(at, count), :] = source
            at += count


def unpack_halo(plan, extents, message, store):
    gx, gy = lax.axis_index("gx"), lax.axis_index("gy")
    for dx, dy, first, _, pieces in plan:
        inside = None
        for step, at, extent in ((dx, gx, extents[0]), (dy, gy, extents[1])):
            if step:
                here = at > 0 if step == 1 else at < extent - 1
                inside = here if inside is None else jnp.logical_and(inside, here)
        keep = jnp.where(inside, 1.0, 0.0).astype(F32)
        at = first
        for array, parity, _, count, _, start, stride in pieces:
            store(array, parity, start, count, stride, message[pl.ds(at, count), :] * keep)
            at += count


def widen_own(own, array, wide, i):
    for parity in range(4):
        for x in range(4):
            wide[i, parity, pl.ds(8 * (x + 2) + 2, 4), :] = own[
                pl.ds(array * 64 + parity * 16 + 4 * x, 4), :
            ]


def narrow(wide, i, own, array):
    for parity in range(4):
        for x in range(4):
            own[pl.ds(array * 64 + parity * 16 + 4 * x, 4), :] = wide[
                i, parity, pl.ds(8 * (x + 2) + 2, 4), :
            ]


def in_two(value):
    head = value.astype(BF16)
    return head, (value - head.astype(F32)).astype(BF16)


def down_iota(rows, columns):
    return lax.broadcasted_iota(jnp.int32, (rows, columns), 0).astype(F32).astype(BF16)


def ones_where(rows, labels):
    columns = labels.shape[1]
    return jnp.where(
        down_iota(rows, columns) == labels.astype(BF16), jnp.ones((), BF16), jnp.zeros((), BF16)
    )


def dot(a, b, transposed=False):
    return lax.dot_general(
        a, b, (((1,), (1 if transposed else 0,)), ((), ())), preferred_element_type=F32
    )


BLOCK = CAP
GATHER_UNROLL = 8
SCATTER_UNROLL = 4


def picks_of(lane, extent):
    return jnp.concatenate([ones_where(extent, lane[j : j + 1]) for j in range(4)], axis=1)


def gather_block(table, block):
    count = block.shape[1]
    picks = picks_of(block[12:16], 128)
    found = dot(table, jnp.concatenate([picks, picks], axis=0))
    down = lax.broadcasted_iota(jnp.int32, (64, count), 0).astype(F32)
    factors = [
        jnp.where(down == block[8 + j : 9 + j], block[j : j + 1], 0.0) for j in range(4)
    ]
    result = []
    for i in range(3):
        total = sum(
            factors[j] * found[64 * i : 64 * (i + 1), count * j : count * (j + 1)]
            for j in range(4)
        )
        result.append(jnp.sum(total, axis=0, keepdims=True))
    return jnp.concatenate(result, axis=0)


def scatter_block(block, traction):
    upper = jnp.where(block[8:12] >= 32.0, 1.0, 0.0)
    row, lane = block[8:12] - 32.0 * upper, block[12:16] + 128.0 * upper
    rows = [ones_where(32, row[j : j + 1]) for j in range(4)]
    parts = [
        [in_two(block[j : j + 1] * traction[i : i + 1]) for j in range(4)] for i in range(3)
    ]
    left = [
        jnp.concatenate([rows[j] * parts[i][j][part] for j in range(4)], axis=1)
        for part in range(2)
        for i in range(3)
    ]
    return dot(jnp.concatenate(left, axis=0), picks_of(lane, 256), True)


def total_rows(total):
    value = total[0:96, :] + total[96:192, :]
    return jnp.concatenate(
        [
            value[32 * i : 32 * (i + 1), 128 * half : 128 * (half + 1)]
            for i in range(3)
            for half in range(2)
        ],
        axis=0,
    )


def table_of(value):
    head, tail = in_two(value)
    return jnp.concatenate([head, tail], axis=1)


def each(first, last, body, unroll):
    def step(k, carry):
        body(k)
        return carry

    lax.fori_loop(first, last, step, 0, unroll=unroll)


def gather_slaves(table, segments, mine, theirs, places, group):
    mine[...] = jnp.zeros_like(mine)

    def slave(k):
        at = pl.ds(pl.multiple_of(k * BLOCK, BLOCK), BLOCK)
        mine[0:3, at] = gather_block(table, segments[:, at])

    each(0, segments.shape[1] // BLOCK, slave, 4)
    head, tail = in_two(mine[...])
    both = jnp.concatenate([head, tail], axis=0)
    target = segments[5:6, :]
    left = jnp.concatenate(
        [jnp.where(target == t, 1.0, 0.0).astype(BF16) * both for t in range(group)], axis=0
    )
    placed = dot(left, places[...], True).reshape(group, 16, CAP)
    theirs[...] = placed[:, 0:4] + placed[:, 8:12]


def gather_masters(table, bundle, theirs, group, first, count):
    def master(k):
        source = lax.rem(first + k, group)
        theirs[source, 0:3, :] = gather_block(table, bundle[source])

    each(0, count, master, GATHER_UNROLL)


def pull_slaves(segments, mine, returned, places, pulls, group):
    nothing = jnp.zeros((4, CAP), F32)
    slots = jnp.concatenate([v for t in range(group) for v in (returned[t], nothing)], axis=0)
    head, tail = in_two(slots)
    found = dot(
        jnp.concatenate([head, tail], axis=1),
        jnp.concatenate([places[...], places[...]], axis=0),
    )
    target = segments[5:6, :]
    back = sum(jnp.where(target == t, 1.0, 0.0) * found[8 * t : 8 * (t + 1)] for t in range(group))
    pulls[0:3, :] = segments[4:5, :] * (mine[0:3, :] - back[0:3, :])


def scatter_slaves(total, segments, pulls):
    def slave(k):
        at = pl.ds(pl.multiple_of(k * 2 * BLOCK, 2 * BLOCK), 2 * BLOCK)
        total[...] += scatter_block(segments[:, at], pulls[0:3, at])

    each(0, segments.shape[1] // (2 * BLOCK), slave, 2)


def scatter_masters(total, bundle, sent, arrived, first, count):
    def master(k):
        pair = [first + 2 * k, first + 2 * k + 1]
        block = jnp.concatenate([bundle[source] for source in pair], axis=1)
        gap = [sent[source, 0:3, :] - arrived[source, 0:3, :] for source in pair]
        total[...] += scatter_block(block, block[4:5] * jnp.concatenate(gap, axis=1))

    each(0, count // 2, master, SCATTER_UNROLL)


def swap_lanes(forth):
    a = lax.broadcasted_iota(jnp.int32, (128, 128), 0 if forth else 1)
    b = lax.broadcasted_iota(jnp.int32, (128, 128), 1 if forth else 0)
    return jnp.where(b == (a % 2) * 64 + a // 2, 1.0, 0.0).astype(F32)


def reorder(value, forth):
    head = value.astype(BF16)
    rest = value - head.astype(F32)
    middle = rest.astype(BF16)
    tail = (rest - middle.astype(F32)).astype(BF16)
    swap = swap_lanes(forth).astype(BF16)
    return dot(
        jnp.concatenate([head, middle, tail], axis=1), jnp.concatenate([swap, swap, swap], axis=0)
    )


def lay_out(fields, first, own, swapped):
    values = [field[...].reshape(-1, 128) for field in fields]
    value = reorder(values[0] if len(values) == 1 else jnp.concatenate(values, axis=0), True)
    count = value.shape[0] // 64
    swapped[pl.ds(first, count)] = value.reshape(count, 8, 8, 128)
    for array in range(first, first + count):
        for x in range(8):
            for py in range(2):
                row = array * 64 + (x % 2 * 2 + py) * 16 + x // 2 * 4
                own[pl.ds(row, 4), :] = swapped[array, x, pl.ds(py, 4, stride=2), :]


def place_of(node):
    x, y, z = node // 1024, node // 128 % 8, node % 128
    row = (x % 2 * 2 + y % 2) * 16 + x // 2 * 4 + y // 2
    return row.astype(F32), (z % 2 * 64 + z // 2).astype(F32)


def place_segments(
    group,
    pair,
    slave_nodes,
    slave_weights,
    master_nodes,
    master_weights,
    penalty,
    packed,
    segments,
    places,
):
    slave_row, slave_lane = place_of(slave_nodes[...])
    master_row, master_lane = place_of(master_nodes[...])
    target = pair[...].astype(F32)
    count = target.shape[1]
    chosen = ones_where(group, target)
    a = lax.broadcasted_iota(jnp.int32, (128, 128), 0)
    b = lax.broadcasted_iota(jnp.int32, (128, 128), 1)
    before = jnp.where(a < b, 1.0, 0.0).astype(BF16)
    ranks, base = [], jnp.zeros((group, 1), F32)
    for k in range(count // 128):
        part = chosen[:, 128 * k : 128 * (k + 1)]
        wide = part.astype(F32)
        rank = dot(part, before) + base
        ranks.append(jnp.sum(rank * wide, axis=0, keepdims=True))
        base = base + jnp.sum(wide, axis=1, keepdims=True)
    position = jnp.concatenate(ranks, axis=1)
    segments[0:4, :] = slave_weights[...]
    segments[4:5, :] = penalty[...]
    segments[5:6, :] = target
    segments[6:7, :] = position
    segments[7:8, :] = jnp.zeros_like(position)
    segments[8:12, :] = slave_row
    segments[12:16, :] = slave_lane
    spots = ones_where(CAP, position)
    places[...] = spots
    nothing = jnp.zeros((3, count), F32)
    values = jnp.concatenate([master_weights[...], penalty[...], nothing], axis=0)
    head, tail = in_two(values)
    nodes = jnp.concatenate([master_row, master_lane], axis=0)
    sent = jnp.concatenate([head, tail, nodes.astype(BF16), jnp.zeros((8, count), BF16)], axis=0)
    left = jnp.concatenate(
        [jnp.where(target == t, 1.0, 0.0).astype(BF16) * sent for t in range(group)], axis=0
    )
    placed = dot(left, spots, True).reshape(group, 32, CAP)
    packed[:, 0:8] = placed[:, 0:8] + placed[:, 8:16]
    packed[:, 8:16] = placed[:, 16:24]


def inner(a, b):
    return jnp.sum(a * b, axis=0, keepdims=True)


INPUTS = (
    "seed",
    "modulus",
    "mass",
    "pair",
    "slave_nodes",
    "slave_weights",
    "master_nodes",
    "master_weights",
    "penalty",
)


KINDS = {
    "modulus": 0,
    "halo": 1,
    "packed": 2,
    "slaves": 3,
    "masters": 5,
    "halo_next": 7,
    "across": 8,
    "along": 9,
}


def scratch_of(extents, args):
    group, count = extents[1], args[-1].shape[-1]
    dma, parts, field = pltpu.SemaphoreType.DMA, (group, 4, CAP), (3, 4, WIDE, 128)
    room = {name: pltpu.VMEM(arg.shape, arg.dtype) for name, arg in zip(INPUTS, args)}
    shapes = {
        "own": (320, 128),
        "swapped": (5, 8, 8, 128),
        "segments": (16, count),
        "packed": (group, 16, CAP),
        "bundle": (group, 16, CAP),
        "modulus_out": (MODULUS_ROWS, 128),
        "modulus_in": (MODULUS_ROWS, 128),
        "halo_out": (FIRST_ROWS, 128),
        "halo_in": (FIRST_ROWS, 128),
        "halo_out_next": (NEXT_ROWS, 128),
        "halo_in_next": (NEXT_ROWS, 128),
        "mine": (2, 8, count),
        "slaves_out": (2,) + parts,
        "slaves_in": (2,) + parts,
        "masters_out": (2,) + parts,
        "masters_in": (2,) + parts,
        "vectors": (2, 192, 128),
        "applied": (2, 192, 128),
        "inverse": (192, 128),
        "wide_mod": (WIDE, 128),
        "wide_mod_up": (WIDE, 128),
        "mass_wide": (1, 4, WIDE, 128),
        "wide": field,
        "wide_up": (3, 3, WIDE, 128),
        "wide_mid": (3, WIDE, 128),
        "out": field,
        "total": (192, 256),
        "pulls": (8, count),
        "tile": (8, 128),
        "middle": (8, 128),
        "across": (extents[0], 8, 128),
        "along": (group, 8, 128),
    }
    room.update({name: pltpu.VMEM(shape, F32) for name, shape in shapes.items()})
    room["places"] = pltpu.VMEM((CAP, count), BF16)
    room["loads"] = dma((len(INPUTS),))
    room["sends"] = dma((10,))
    room["receives"] = dma((10,))
    return room


class Refs:
    def __init__(self, names, refs):
        self.__dict__.update(zip(names, refs))


def whole_kernel(extents, names, *refs):
    inputs, (adjoint, residual) = refs[: len(INPUTS)], refs[len(INPUTS) : len(INPUTS) + 2]
    r = Refs(names, refs[len(INPUTS) + 2 :])
    wide, group = extents
    gx, gy = lax.axis_index("gx"), lax.axis_index("gy")
    loads = {
        name: pltpu.make_async_copy(ref, getattr(r, name), r.loads.at[k])
        for k, (name, ref) in enumerate(zip(INPUTS, inputs))
    }
    for name in sorted(loads, key=lambda name: name != "modulus"):
        loads[name].start()

    def beside(dx, dy):
        return lax.rem(gx + dx + wide, wide), lax.rem(gy + dy + group, group)

    barrier = pltpu.get_barrier_semaphore()
    peers = [(dx, dy) for dx, dy, _, _, _ in FIRST_PLAN]
    peers += [(k, 0) for k in range(2, wide - 1)] + [(0, k) for k in range(2, group - 1)]
    for dx, dy in peers:
        pl.semaphore_signal(barrier, inc=1, device_id=beside(dx, dy), device_id_type=MESH)

    def copy_of(kind, source, target, device, turn=0):
        k = KINDS[kind] + turn
        return pltpu.make_async_remote_copy(
            src_ref=source,
            dst_ref=target,
            send_sem=r.sends.at[k],
            recv_sem=r.receives.at[k],
            device_id=device,
            device_id_type=MESH,
        )

    def all_of(kind, turn=0):
        buffers = {"modulus": r.modulus_in, "halo": r.halo_in, "halo_next": r.halo_in_next}
        if kind in buffers:
            part = buffers[kind]
        elif kind in ("slaves", "masters"):
            part = (r.slaves_in if kind == "slaves" else r.masters_in).at[turn]
            part = part.at[pl.ds(0, group - 1)]
        elif kind == "across":
            part = r.across.at[pl.ds(0, wide - 1)]
        else:
            part = (r.bundle if kind == "packed" else r.along).at[pl.ds(0, group - 1)]
        return copy_of(kind, part, part, beside(0, 1), turn)

    def receive(kind, turn=0):
        all_of(kind, turn).wait_recv()

    def send_halo(plan, source, target, kind):
        for dx, dy, at, rows, _ in plan:
            part = pl.ds(at, rows)
            copy_of(kind, source.at[part], target.at[part], beside(dx, dy)).start()

    def send_block(source, target, kind, k, turn):
        device = beside(0, k)
        copy_of(kind, source.at[device[1]], target.at[gy], device, turn).start()

    def send_blocks(source, target, kind, turn=0):
        for k in range(1, group):
            send_block(source, target, kind, k, turn)
        target[gy] = source[gy]

    loads["modulus"].wait()
    lay_out([r.modulus], 4, r.own, r.swapped)
    pack_halo(MODULUS_PLAN, r.own, r.modulus_out)
    pl.semaphore_wait(barrier, len(peers))
    send_halo(MODULUS_PLAN, r.modulus_out, r.modulus_in, "modulus")
    loads["seed"].wait()
    loads["mass"].wait()
    lay_out([r.seed, r.mass], 0, r.own, r.swapped)
    pack_halo(FIRST_PLAN, r.own, r.halo_out)
    send_halo(FIRST_PLAN, r.halo_out, r.halo_in, "halo")
    for name in INPUTS[3:]:
        loads[name].wait()
    place_segments(
        group,
        r.pair,
        r.slave_nodes,
        r.slave_weights,
        r.master_nodes,
        r.master_weights,
        r.penalty,
        r.packed,
        r.segments,
        r.places,
    )
    send_blocks(r.packed, r.bundle, "packed")

    r.wide[...] = jnp.zeros_like(r.wide)
    r.mass_wide[...] = jnp.zeros_like(r.mass_wide)
    r.wide_mod[...] = jnp.zeros_like(r.wide_mod)
    for i in range(3):
        widen_own(r.own, i, r.wide, i)
    widen_own(r.own, 3, r.mass_wide, 0)
    for x in range(4):
        r.wide_mod[pl.ds(8 * (x + 2) + 2, 4), :] = r.own[pl.ds(4 * 64 + 4 * x, 4), :]
    r.masters_out[...] = jnp.zeros_like(r.masters_out)

    def store_modulus(array, parity, start, count, stride, value):
        r.wide_mod[rows_of(start, count, stride), :] = value

    receive("modulus")
    unpack_halo(MODULUS_PLAN, extents, r.modulus_in, store_modulus)
    r.wide_mod_up[...] = shift_down(r.wide_mod[...])
    diagonal_into(r.out, r.wide_mod, r.wide_mod_up)
    for i in range(3):
        narrow(r.out, i, r.inverse, i)
    mass = r.own[192:256, :]
    r.inverse[...] = 1.0 / (r.inverse[...] + jnp.concatenate([mass, mass, mass], axis=0))
    r.vectors[0] = r.own[0:192, :] * r.inverse[...]

    def store(array, parity, start, count, stride, value):
        at = rows_of(start, count, stride)
        if array < 3:
            r.wide[array, parity, at, :] = value
        else:
            r.mass_wide[0, parity, at, :] = value

    def apply(turn, carry):
        begins, ends = turn == 0, turn == 1
        mine = r.mine.at[turn]
        slaves_out, slaves_in = r.slaves_out.at[turn], r.slaves_in.at[turn]
        masters_out, masters_in = r.masters_out.at[turn], r.masters_in.at[turn]
        table = table_of(r.vectors[turn])
        gather_slaves(table, r.segments, mine, slaves_out, r.places, group)
        send_blocks(slaves_out, slaves_in, "slaves", turn)

        @pl.when(begins)
        def _segments():
            receive("packed")

        half = group // 2

        def masters(k, carry):
            first = half * k
            gather_masters(table_of(r.vectors[turn]), r.bundle, masters_out, group, gy + first, half)

            @pl.when(k > 0)
            def _middle():
                send_block(masters_out, masters_in, "masters", first, turn)

            for j in range(1, half):
                send_block(masters_out, masters_in, "masters", first + j, turn)
            return carry

        lax.fori_loop(0, 2, masters, 0)
        masters_in[gy] = masters_out[gy]

        @pl.when(begins)
        def _first():
            receive("halo")
            unpack_halo(FIRST_PLAN, extents, r.halo_in, store)
            for i in range(3):
                for parity in range(4):
                    wide_mass = r.mass_wide[0, parity]
                    entry = r.out[i, parity] + wide_mass
                    inverse = jnp.where(wide_mass > 0.0, 1.0 / entry, 0.0)
                    r.wide[i, parity] = r.wide[i, parity] * inverse

        @pl.when(ends)
        def _next():
            r.wide[...] = jnp.zeros_like(r.wide)
            for i in range(3):
                widen_own(r.vectors.at[1], i, r.wide, i)
            receive("halo_next")
            unpack_halo(NEXT_PLAN, extents, r.halo_in_next, store)

        lift(r.wide, r.wide_up, r.wide_mid)
        stiffness_into(r.out, r.wide, r.wide_up, r.wide_mid, r.wide_mod, r.wide_mod_up)
        applied = r.applied.at[turn]
        for i in range(3):
            narrow(r.out, i, applied, i)
        mass = r.own[192:256, :]
        applied[...] += jnp.concatenate([mass, mass, mass], axis=0) * r.vectors[turn]
        receive("slaves", turn)

        @pl.when(ends)
        def _sums():
            scaled = r.vectors[1]
            r.tile[0:1, :] = inner(r.own[0:192, :], r.vectors[0])
            r.tile[1:2, :] = inner(r.vectors[0], r.applied[0])
            r.tile[2:3, :] = inner(scaled, r.applied[0])
            r.tile[4:8, :] = jnp.zeros((4, 128), F32)
            pressed = jnp.zeros((3, CAP), F32)
            for source in range(group):
                gap = r.masters_out[1, source, 0:3, :] - r.slaves_in[1, source, 0:3, :]
                pressed = pressed + r.bundle[source, 4:5, :] * gap * gap
            pressed = jnp.sum(pressed, axis=0, keepdims=True)
            energy = inner(scaled, r.applied[1])
            for k in range(CAP // 128):
                energy = energy + pressed[:, 128 * k : 128 * (k + 1)]
            r.tile[3:4, :] = energy
            for k in range(1, wide):
                copy_of("across", r.tile, r.across.at[gx], beside(k, 0)).start()
            r.across[gx] = r.tile[...]

        r.total[...] = jnp.zeros_like(r.total)

        def pushes(k, carry):
            scatter_masters(r.total, r.bundle, masters_out, slaves_in, half * k, half)

            @pl.when(jnp.logical_and(ends, k == 0))
            def _along():
                receive("across")
                part = jnp.sum(r.across[...], axis=0)
                r.middle[...] = part
                for j in range(1, group):
                    copy_of("along", r.middle, r.along.at[gy], beside(0, j)).start()
                r.along[gy] = part

            return carry

        lax.fori_loop(0, 2, pushes, 0)
        receive("masters", turn)
        pull_slaves(r.segments, mine, masters_in, r.places, r.pulls, group)
        scatter_slaves(r.total, r.segments, r.pulls)
        applied[...] += total_rows(r.total)

        @pl.when(begins)
        def _scaled():
            r.vectors[1] = r.applied[0] * r.inverse[...]
            pack_halo(NEXT_PLAN, r.vectors.at[1], r.halo_out_next)
            send_halo(NEXT_PLAN, r.halo_out_next, r.halo_in_next, "halo_next")

        return carry

    lax.fori_loop(0, 2, apply, 0)
    seed, direction, scaled = r.own[0:192, :], r.vectors[0], r.vectors[1]
    applied, again = r.applied[0], r.applied[1]
    receive("along")
    totals = jnp.sum(jnp.sum(r.along[...], axis=0), axis=1, keepdims=True)
    first, second, third, fourth = (totals[k : k + 1] for k in range(4))
    step = first / second
    later = step * step * third - first
    grown = 1.0 + later / first
    curved = grown * grown * second - 2.0 * step * grown * third + step * step * fourth
    step_next = later / curved
    forward = step + step_next * grown
    aside = step_next * step
    adjoint[...] = forward * direction - aside * scaled
    residual[...] = seed - forward * applied + aside * again
    for kind in KINDS:
        for turn in range(2 if kind in ("slaves", "masters") else 1):
            all_of(kind, turn).wait_send()


def finish_kernel(found, left, adjoint, residual):
    for source, ref in ((found, adjoint), (left, residual)):
        value = reorder(source[...], False)
        for i in range(3):
            for x in range(8):
                for py in range(2):
                    row = i * 64 + (x % 2 * 2 + py) * 16 + x // 2 * 4
                    ref[i, x, pl.ds(py, 4, stride=2), :] = value[row : row + 4]


def shards(
    seed_grad,
    modulus,
    lumped_mass,
    pair_dest,
    slave_nodes,
    slave_weights,
    master_nodes,
    master_weights,
    penalty,
):
    extents = (lax.axis_size("gx"), lax.axis_size("gy"))
    count = penalty.shape[0]
    args = (
        seed_grad,
        modulus,
        lumped_mass,
        pair_dest.reshape(1, count),
        slave_nodes,
        slave_weights,
        master_nodes,
        master_weights,
        penalty.reshape(1, count),
    )
    scratch = scratch_of(extents, args)
    own = jax.ShapeDtypeStruct((192, 128), F32)
    found, left = pl.pallas_call(
        functools.partial(whole_kernel, extents, tuple(scratch)),
        out_shape=[own, own],
        in_specs=[pl.BlockSpec(memory_space=pl.ANY)] * len(args),
        out_specs=[VMEM, VMEM],
        scratch_shapes=list(scratch.values()),
        compiler_params=pltpu.CompilerParams(
            collective_id=1, has_side_effects=True, vmem_limit_bytes=LIMIT
        ),
        name="conjugate_gradients",
    )(*args)
    field = jax.ShapeDtypeStruct(seed_grad.shape, F32)
    return tuple(
        pl.pallas_call(
            finish_kernel,
            out_shape=[field, field],
            in_specs=[VMEM, VMEM],
            out_specs=[VMEM, VMEM],
            compiler_params=pltpu.CompilerParams(vmem_limit_bytes=LIMIT),
            name="finish",
        )(found, left)
    )


def solution(mesh):
    placed = (
        P(None, "gx", "gy", None),
        P("gx", "gy", None),
        P("gx", "gy", None),
        P(("gx", "gy"), None),
        P(None, ("gx", "gy")),
        P(None, ("gx", "gy")),
        P(None, ("gx", "gy")),
        P(None, ("gx", "gy")),
        P(("gx", "gy")),
    )
    return jax.shard_map(
        shards,
        mesh=mesh,
        in_specs=placed,
        out_specs=(P(None, "gx", "gy", None), P(None, "gx", "gy", None)),
        check_vma=False,
    )
```

```python
import functools
import math

import jax
import jax.numpy as jnp
import numpy as np
from jax import lax
from jax.experimental import pallas as pl
from jax.experimental.pallas import tpu as pltpu
from jax.sharding import PartitionSpec as P

CAP = 256
SHEAR = 1.0 / 2.6
LAME = 0.3 / 0.52
MESH = pl.DeviceIdType.MESH
F32 = jnp.float32
BF16 = jnp.bfloat16
VMEM = pl.BlockSpec(memory_space=pltpu.VMEM)
LIMIT = 64 * 1024 * 1024

WIDE = 72


def shape_tables():
    abscissa = 1.0 / math.sqrt(3.0)
    points = [
        (a, b, c)
        for a in (-abscissa, abscissa)
        for b in (-abscissa, abscissa)
        for c in (-abscissa, abscissa)
    ]
    offsets = [
        (i, j, k)
        for i in range(3)
        for j in range(3)
        for k in range(3)
        if (i == 1) + (j == 1) + (k == 1) <= 1
    ]
    derivative = np.zeros((8, 3, 20))
    for g, location in enumerate(points):
        for n, offset in enumerate(offsets):
            natural = [offset[d] - 1 for d in range(3)]
            factors = [
                1.0 - location[d] ** 2 if natural[d] == 0 else 1.0 + location[d] * natural[d]
                for d in range(3)
            ]
            slopes = [
                -2.0 * location[d] if natural[d] == 0 else float(natural[d]) for d in range(3)
            ]
            linear = sum(location[d] * natural[d] for d in range(3)) - 2.0
            for d in range(3):
                others = factors[(d + 1) % 3] * factors[(d + 2) % 3]
                if 0 in natural:
                    derivative[g, d, n] = slopes[d] * others / 4.0
                else:
                    derivative[g, d, n] = natural[d] * others * (linear + factors[d]) / 8.0
    return derivative, offsets


def signs(count, dims):
    table = np.ones((count, count))
    for t in range(count):
        for c in range(count):
            for d in range(dims):
                if t >> d & 1 and not c >> d & 1:
                    table[t, c] = -table[t, c]
    return table


def element_tables():
    derivative, offsets = shape_tables()
    eight, four = signs(8, 3), signs(4, 2)
    modal = np.einsum("sg,gan->asn", eight, derivative) / 8.0
    corner_at = [offsets.index((c >> 2 << 1, (c >> 1 & 1) << 1, (c & 1) << 1)) for c in range(8)]
    edge_at = []
    for d in range(3):
        row = []
        for c in range(4):
            offset = [(c >> 1) << 1, (c & 1) << 1]
            offset.insert(d, 1)
            row.append(offsets.index(tuple(offset)))
        edge_at.append(row)
    corner_terms = np.einsum("tn,asn->ast", eight, modal[:, :, corner_at]) / 8.0
    edge_terms = [np.einsum("tn,asn->ast", four, modal[:, :, edge_at[d]]) / 4.0 for d in range(3)]
    trilinear = np.array([(1.0 / math.sqrt(3.0)) ** bin(t).count("1") / 8.0 for t in range(8)])
    at_points = np.einsum("t,tg->gt", trilinear, eight)
    squares = derivative * derivative
    weight = np.einsum(
        "gt,gni->tni",
        at_points,
        SHEAR * squares.sum(axis=1)[:, :, None] + (LAME + SHEAR) * np.swapaxes(squares, 1, 2),
    )
    corner_diag = np.einsum("un,tni->uti", eight, weight[:, corner_at]) / 8.0
    edge_diag = [np.einsum("un,tni->uti", four, weight[:, edge_at[d]]) / 4.0 for d in range(3)]
    return corner_terms, edge_terms, trilinear, corner_diag, edge_diag


def split_sums(values):
    values = list(values)
    step = 1
    while step < len(values):
        for low in range(len(values)):
            if not low & step:
                a, b = values[low], values[low | step]
                values[low], values[low | step] = b + a, b - a
        step *= 2
    return values


def join_sums(values):
    values = list(values)
    step = 1
    while step < len(values):
        for low in range(len(values)):
            if not low & step:
                a, b = values[low], values[low | step]
                values[low], values[low | step] = a - b, a + b
        step *= 2
    return values


def combine(terms):
    total = None
    for factor, value in terms:
        if abs(factor) < 1e-12:
            continue
        term = value * np.float32(factor)
        total = term if total is None else total + term
    return total


def rows_at(group, shift):
    return pl.ds(pl.multiple_of(8 * group, 8) + shift, 8)


def lanes(rows):
    return lax.broadcasted_iota(jnp.int32, (rows, 128), 1)


def shift_down(value):
    return jnp.where(lanes(value.shape[0]) == 63, 0.0, pltpu.roll(value, 127, 1))


def collect(low, middle, high):
    total = low + jnp.where(lanes(8) < 64, pltpu.roll(high, 1, 1), 0.0)
    if middle is not None:
        total = total + pltpu.roll(middle, 64, 1)
    return total


def corner_moduli(wide_mod, wide_mod_up, group):
    values = []
    for c in range(8):
        ref = wide_mod_up if c & 1 else wide_mod
        values.append(ref[rows_at(group + (c >> 2), c >> 1 & 1), :])
    inside = lanes(8) < 64
    return split_sums([jnp.where(inside, value, 0.0) for value in values])


def edge_corner(d, c):
    where = [c >> 1, c & 1]
    where.insert(d, None)
    return where


def add_rows(ref, index, row, value):
    ref[index + (row, slice(None))] += value


def scatter_forces(out, i, corner, edges, group):
    for xy in range(4):
        row = rows_at(group + (xy >> 1), xy & 1)
        add_rows(out, (i, 0), row, collect(corner[2 * xy], edges[2][xy], corner[2 * xy + 1]))
    for y in range(2):
        add_rows(
            out, (i, 2), rows_at(group, y), collect(edges[0][2 * y], None, edges[0][2 * y + 1])
        )
    for x in range(2):
        add_rows(
            out, (i, 1), rows_at(group + x, 0), collect(edges[1][2 * x], None, edges[1][2 * x + 1])
        )


def diagonal_into(out, wide_mod, wide_mod_up):
    corner_diag, edge_diag = element_tables()[3:]
    out[...] = jnp.zeros_like(out)

    def step(group, carry):
        moduli = corner_moduli(wide_mod, wide_mod_up, group)
        for i in range(3):
            corner = join_sums(
                [
                    combine([(corner_diag[u, t, i], moduli[t]) for t in range(8)])
                    for u in range(8)
                ]
            )
            edges = [
                join_sums(
                    [
                        combine([(edge_diag[d][u, t, i], moduli[t]) for t in range(8)])
                        for u in range(4)
                    ]
                )
                for d in range(3)
            ]
            scatter_forces(out, i, corner, edges, group)
        return carry

    lax.fori_loop(0, 7, step, 0, unroll=7)


def stiffness_into(out, wide, wide_up, wide_mid, wide_mod, wide_mod_up):
    corner_terms, edge_terms, trilinear = element_tables()[:3]
    out[...] = jnp.zeros_like(out)

    def step(group, carry):
        moduli = corner_moduli(wide_mod, wide_mod_up, group)
        points = join_sums([moduli[t] * np.float32(trilinear[t]) for t in range(8)])
        slopes = []
        for i in range(3):
            corner = []
            for c in range(8):
                ref = wide_up if c & 1 else wide
                corner.append(ref[i, 0, rows_at(group + (c >> 2), c >> 1 & 1), :])
            corner = split_sums(corner)
            edges = []
            for d in range(3):
                values = []
                for c in range(4):
                    x, y, z = edge_corner(d, c)
                    row = rows_at(group + (x or 0), y or 0)
                    parity = (2, 1, 0)[d]
                    if d == 2:
                        values.append(wide_mid[i, row, :])
                    else:
                        values.append((wide_up if z else wide)[i, parity, row, :])
                edges.append(split_sums(values))
            slopes.append(
                [
                    [
                        combine(
                            [(corner_terms[a, s, t], corner[t]) for t in range(8)]
                            + [
                                (edge_terms[d][a, s, t], edges[d][t])
                                for d in range(3)
                                for t in range(4)
                            ]
                        )
                        for s in range(8)
                    ]
                    for a in range(3)
                ]
            )

        def plus(a, b):
            return a if b is None else b if a is None else a + b

        zero = jnp.zeros((8, 128), F32)
        strain = {}
        for a in range(3):
            strain[a, a] = slopes[a][a]
            for b in range(a):
                strain[b, a] = [plus(p, q) for p, q in zip(slopes[a][b], slopes[b][a])]
        strain = {
            key: join_sums([zero if v is None else v for v in value])
            for key, value in strain.items()
        }
        stress = {key: [] for key in strain}
        for g in range(8):
            volume = (strain[0, 0][g] + strain[1, 1][g] + strain[2, 2][g]) * np.float32(LAME)
            for a in range(3):
                stress[a, a].append(
                    points[g] * (volume + strain[a, a][g] * np.float32(2.0 * SHEAR))
                )
            scaled = points[g] * np.float32(SHEAR)
            for key in ((0, 1), (0, 2), (1, 2)):
                stress[key].append(scaled * strain[key][g])
        stress = {key: split_sums(value) for key, value in stress.items()}
        for i in range(3):
            pairs = [
                (a, s, stress[min(a, i), max(a, i)][s]) for a in range(3) for s in range(8)
            ]
            corner = join_sums(
                [combine([(corner_terms[a, s, t], v) for a, s, v in pairs]) for t in range(8)]
            )
            edges = [
                join_sums(
                    [combine([(edge_terms[d][a, s, t], v) for a, s, v in pairs]) for t in range(4)]
                )
                for d in range(3)
            ]
            scatter_forces(out, i, corner, edges, group)
        return carry

    lax.fori_loop(1, 6, step, 0, unroll=5)


def lift(wide, wide_up, wide_mid):
    for i in range(3):
        for parity in range(3):
            wide_up[i, parity] = shift_down(wide[i, parity])
        wide_mid[i] = pltpu.roll(wide[i, 0], 64, 1)


def halo_plan(fields, modulus=None):
    plan, first = [], 0
    for dx in (-1, 0, 1):
        for dy in (-1, 0, 1):
            if dx == 0 and dy == 0:
                continue
            pieces = []

            def places(step, both):
                if step == 1:
                    return [(p, 3, 1) for p in ((0, 1) if both else (0,))]
                return [(0, 0, 6)]

            def strips(array, xs, ys):
                for px, ox, wx in xs:
                    for py, oy, wy in ys:
                        if ox is None:
                            pieces.append((array, px * 2 + py, oy, 4, 4, 8 * 2 + wy, 8))
                        elif oy is None:
                            pieces.append((array, px * 2 + py, 4 * ox, 4, 1, 8 * wx + 2, 1))
                        else:
                            pieces.append((array, px * 2 + py, 4 * ox + oy, 1, 1, 8 * wx + wy, 1))

            every = [(0, None, None), (1, None, None)]
            for array in range(fields):
                strips(
                    array,
                    every if dx == 0 else places(dx, True),
                    every if dy == 0 else places(dy, True),
                )
            if modulus is not None:
                deep = {1: [(0, 3, 1), (0, 2, 0)], -1: [(0, 0, 6), (0, 1, 7)], 0: every[:1]}
                strips(modulus, deep[dx], deep[dy])
            rows = sum(piece[3] for piece in pieces)
            plan.append((dx, dy, first, -(-rows // 8) * 8, pieces))
            first += plan[-1][3]
    return plan, first


MODULUS_PLAN, MODULUS_ROWS = halo_plan(0, 4)
FIRST_PLAN, FIRST_ROWS = halo_plan(4)
NEXT_PLAN, NEXT_ROWS = halo_plan(3)


def rows_of(start, count, stride):
    return pl.ds(start, count) if stride == 1 else pl.ds(start, count, stride=stride)


def pack_halo(plan, own, message):
    message[...] = jnp.zeros_like(message)
    for _, _, first, _, pieces in plan:
        at = first
        for array, parity, start, count, stride, _, _ in pieces:
            source = own[rows_of(array * 64 + parity * 16 + start, count, stride), :]
            message[pl.ds(at, count), :] = source
            at += count


def unpack_halo(plan, extents, message, store):
    gx, gy = lax.axis_index("gx"), lax.axis_index("gy")
    for dx, dy, first, _, pieces in plan:
        inside = None
        for step, at, extent in ((dx, gx, extents[0]), (dy, gy, extents[1])):
            if step:
                here = at > 0 if step == 1 else at < extent - 1
                inside = here if inside is None else jnp.logical_and(inside, here)
        keep = jnp.where(inside, 1.0, 0.0).astype(F32)
        at = first
        for array, parity, _, count, _, start, stride in pieces:
            store(array, parity, start, count, stride, message[pl.ds(at, count), :] * keep)
            at += count


def widen_own(own, array, wide, i):
    for parity in range(4):
        for x in range(4):
            wide[i, parity, pl.ds(8 * (x + 2) + 2, 4), :] = own[
                pl.ds(array * 64 + parity * 16 + 4 * x, 4), :
            ]


def narrow(wide, i, own, array):
    for parity in range(4):
        for x in range(4):
            own[pl.ds(array * 64 + parity * 16 + 4 * x, 4), :] = wide[
                i, parity, pl.ds(8 * (x + 2) + 2, 4), :
            ]


def in_two(value):
    head = value.astype(BF16)
    return head, (value - head.astype(F32)).astype(BF16)


def down_iota(rows, columns):
    return lax.broadcasted_iota(jnp.int32, (rows, columns), 0).astype(F32).astype(BF16)


def ones_where(rows, labels):
    columns = labels.shape[1]
    return jnp.where(
        down_iota(rows, columns) == labels.astype(BF16), jnp.ones((), BF16), jnp.zeros((), BF16)
    )


def dot(a, b, transposed=False):
    return lax.dot_general(
        a, b, (((1,), (1 if transposed else 0,)), ((), ())), preferred_element_type=F32
    )


BLOCK = CAP
GATHER_UNROLL = 8
SCATTER_UNROLL = 4


def picks_of(lane, extent):
    return jnp.concatenate([ones_where(extent, lane[j : j + 1]) for j in range(4)], axis=1)


def gather_block(table, block):
    count = block.shape[1]
    picks = picks_of(block[12:16], 128)
    found = dot(table, jnp.concatenate([picks, picks], axis=0))
    down = lax.broadcasted_iota(jnp.int32, (64, count), 0).astype(F32)
    factors = [
        jnp.where(down == block[8 + j : 9 + j], block[j : j + 1], 0.0) for j in range(4)
    ]
    result = []
    for i in range(3):
        total = sum(
            factors[j] * found[64 * i : 64 * (i + 1), count * j : count * (j + 1)]
            for j in range(4)
        )
        result.append(jnp.sum(total, axis=0, keepdims=True))
    return jnp.concatenate(result, axis=0)


def scatter_block(block, traction):
    upper = jnp.where(block[8:12] >= 32.0, 1.0, 0.0)
    row, lane = block[8:12] - 32.0 * upper, block[12:16] + 128.0 * upper
    rows = [ones_where(32, row[j : j + 1]) for j in range(4)]
    parts = [
        [in_two(block[j : j + 1] * traction[i : i + 1]) for j in range(4)] for i in range(3)
    ]
    left = [
        jnp.concatenate([rows[j] * parts[i][j][part] for j in range(4)], axis=1)
        for part in range(2)
        for i in range(3)
    ]
    return dot(jnp.concatenate(left, axis=0), picks_of(lane, 256), True)


def total_rows(total):
    value = total[0:96, :] + total[96:192, :]
    return jnp.concatenate(
        [
            value[32 * i : 32 * (i + 1), 128 * half : 128 * (half + 1)]
            for i in range(3)
            for half in range(2)
        ],
        axis=0,
    )


def table_of(value):
    head, tail = in_two(value)
    return jnp.concatenate([head, tail], axis=1)


def each(first, last, body, unroll):
    def step(k, carry):
        body(k)
        return carry

    lax.fori_loop(first, last, step, 0, unroll=unroll)


def gather_slaves(table, segments, mine, theirs, places, group):
    mine[...] = jnp.zeros_like(mine)

    def slave(k):
        at = pl.ds(pl.multiple_of(k * BLOCK, BLOCK), BLOCK)
        mine[0:3, at] = gather_block(table, segments[:, at])

    each(0, segments.shape[1] // BLOCK, slave, 4)
    head, tail = in_two(mine[...])
    both = jnp.concatenate([head, tail], axis=0)
    target = segments[5:6, :]
    left = jnp.concatenate(
        [jnp.where(target == t, 1.0, 0.0).astype(BF16) * both for t in range(group)], axis=0
    )
    placed = dot(left, places[...], True).reshape(group, 16, CAP)
    theirs[...] = placed[:, 0:4] + placed[:, 8:12]


def gather_masters(table, bundle, theirs, place, first, count):
    def master(k):
        source = place(first + k)
        theirs[source, 0:3, :] = gather_block(table, bundle[source])

    each(0, count, master, GATHER_UNROLL)


def pull_slaves(segments, mine, returned, places, pulls, group):
    nothing = jnp.zeros((4, CAP), F32)
    slots = jnp.concatenate([v for t in range(group) for v in (returned[t], nothing)], axis=0)
    head, tail = in_two(slots)
    found = dot(
        jnp.concatenate([head, tail], axis=1),
        jnp.concatenate([places[...], places[...]], axis=0),
    )
    target = segments[5:6, :]
    back = sum(jnp.where(target == t, 1.0, 0.0) * found[8 * t : 8 * (t + 1)] for t in range(group))
    pulls[0:3, :] = segments[4:5, :] * (mine[0:3, :] - back[0:3, :])


def scatter_slaves(total, segments, pulls):
    def slave(k):
        at = pl.ds(pl.multiple_of(k * 2 * BLOCK, 2 * BLOCK), 2 * BLOCK)
        total[...] += scatter_block(segments[:, at], pulls[0:3, at])

    each(0, segments.shape[1] // (2 * BLOCK), slave, 2)


def scatter_masters(total, bundle, sent, arrived, first, count):
    def master(k):
        pair = [first + 2 * k, first + 2 * k + 1]
        block = jnp.concatenate([bundle[source] for source in pair], axis=1)
        gap = [sent[source, 0:3, :] - arrived[source, 0:3, :] for source in pair]
        total[...] += scatter_block(block, block[4:5] * jnp.concatenate(gap, axis=1))

    each(0, count // 2, master, SCATTER_UNROLL)


def swap_lanes(forth):
    a = lax.broadcasted_iota(jnp.int32, (128, 128), 0 if forth else 1)
    b = lax.broadcasted_iota(jnp.int32, (128, 128), 1 if forth else 0)
    return jnp.where(b == (a % 2) * 64 + a // 2, 1.0, 0.0).astype(F32)


def reorder(value, forth):
    head = value.astype(BF16)
    rest = value - head.astype(F32)
    middle = rest.astype(BF16)
    tail = (rest - middle.astype(F32)).astype(BF16)
    swap = swap_lanes(forth).astype(BF16)
    return dot(
        jnp.concatenate([head, middle, tail], axis=1), jnp.concatenate([swap, swap, swap], axis=0)
    )


def lay_out(fields, first, own, swapped):
    values = [field[...].reshape(-1, 128) for field in fields]
    value = reorder(values[0] if len(values) == 1 else jnp.concatenate(values, axis=0), True)
    count = value.shape[0] // 64
    swapped[pl.ds(first, count)] = value.reshape(count, 8, 8, 128)
    for array in range(first, first + count):
        for x in range(8):
            for py in range(2):
                row = array * 64 + (x % 2 * 2 + py) * 16 + x // 2 * 4
                own[pl.ds(row, 4), :] = swapped[array, x, pl.ds(py, 4, stride=2), :]


def place_of(node):
    x, y, z = node // 1024, node // 128 % 8, node % 128
    row = (x % 2 * 2 + y % 2) * 16 + x // 2 * 4 + y // 2
    return row.astype(F32), (z % 2 * 64 + z // 2).astype(F32)


def place_segments(
    group,
    pair,
    slave_nodes,
    slave_weights,
    master_nodes,
    master_weights,
    penalty,
    packed,
    segments,
    places,
):
    slave_row, slave_lane = place_of(slave_nodes[...])
    master_row, master_lane = place_of(master_nodes[...])
    target = pair[...].astype(F32)
    count = target.shape[1]
    chosen = ones_where(group, target)
    a = lax.broadcasted_iota(jnp.int32, (128, 128), 0)
    b = lax.broadcasted_iota(jnp.int32, (128, 128), 1)
    before = jnp.where(a < b, 1.0, 0.0).astype(BF16)
    ranks, base = [], jnp.zeros((group, 1), F32)
    for k in range(count // 128):
        part = chosen[:, 128 * k : 128 * (k + 1)]
        wide = part.astype(F32)
        rank = dot(part, before) + base
        ranks.append(jnp.sum(rank * wide, axis=0, keepdims=True))
        base = base + jnp.sum(wide, axis=1, keepdims=True)
    position = jnp.concatenate(ranks, axis=1)
    segments[0:4, :] = slave_weights[...]
    segments[4:5, :] = penalty[...]
    segments[5:6, :] = target
    segments[6:7, :] = position
    segments[7:8, :] = jnp.zeros_like(position)
    segments[8:12, :] = slave_row
    segments[12:16, :] = slave_lane
    spots = ones_where(CAP, position)
    places[...] = spots
    nothing = jnp.zeros((3, count), F32)
    values = jnp.concatenate([master_weights[...], penalty[...], nothing], axis=0)
    head, tail = in_two(values)
    nodes = jnp.concatenate([master_row, master_lane], axis=0)
    sent = jnp.concatenate([head, tail, nodes.astype(BF16), jnp.zeros((8, count), BF16)], axis=0)
    left = jnp.concatenate(
        [jnp.where(target == t, 1.0, 0.0).astype(BF16) * sent for t in range(group)], axis=0
    )
    placed = dot(left, spots, True).reshape(group, 32, CAP)
    packed[:, 0:8] = placed[:, 0:8] + placed[:, 8:16]
    packed[:, 8:16] = placed[:, 16:24]


def inner(a, b):
    return jnp.sum(a * b, axis=0, keepdims=True)


INPUTS = (
    "seed",
    "modulus",
    "mass",
    "pair",
    "slave_nodes",
    "slave_weights",
    "master_nodes",
    "master_weights",
    "penalty",
)


KINDS = {
    "modulus": 0,
    "halo": 1,
    "packed": 2,
    "slaves": 3,
    "masters": 5,
    "halo_next": 7,
    "across": 8,
    "along": 9,
}


def scratch_of(extents, args):
    group, count = extents[1], args[-1].shape[-1]
    dma, parts, field = pltpu.SemaphoreType.DMA, (group, 4, CAP), (3, 4, WIDE, 128)
    room = {name: pltpu.VMEM(arg.shape, arg.dtype) for name, arg in zip(INPUTS, args)}
    shapes = {
        "own": (320, 128),
        "swapped": (5, 8, 8, 128),
        "segments": (16, count),
        "packed": (group, 16, CAP),
        "bundle": (group, 16, CAP),
        "modulus_out": (MODULUS_ROWS, 128),
        "modulus_in": (MODULUS_ROWS, 128),
        "halo_out": (FIRST_ROWS, 128),
        "halo_in": (FIRST_ROWS, 128),
        "halo_out_next": (NEXT_ROWS, 128),
        "halo_in_next": (NEXT_ROWS, 128),
        "mine": (2, 8, count),
        "slaves_out": (2,) + parts,
        "slaves_in": (2,) + parts,
        "masters_out": (2,) + parts,
        "masters_in": (2,) + parts,
        "vectors": (2, 192, 128),
        "applied": (2, 192, 128),
        "inverse": (192, 128),
        "wide_mod": (WIDE, 128),
        "wide_mod_up": (WIDE, 128),
        "mass_wide": (1, 4, WIDE, 128),
        "wide": field,
        "wide_up": (3, 3, WIDE, 128),
        "wide_mid": (3, WIDE, 128),
        "out": field,
        "total": (192, 256),
        "pulls": (8, count),
        "tile": (8, 128),
        "middle": (8, 128),
        "across": (extents[0], 8, 128),
        "along": (group, 8, 128),
    }
    room.update({name: pltpu.VMEM(shape, F32) for name, shape in shapes.items()})
    room["places"] = pltpu.VMEM((CAP, count), BF16)
    room["loads"] = dma((len(INPUTS),))
    room["sends"] = dma((10,))
    room["receives"] = dma((10,))
    return room


class Refs:
    def __init__(self, names, refs):
        self.__dict__.update(zip(names, refs))


def whole_kernel(extents, names, *refs):
    inputs, results = refs[: len(INPUTS)], refs[len(INPUTS)]
    r = Refs(names, refs[len(INPUTS) + 1 :])
    wide, group = extents
    gx, gy = lax.axis_index("gx"), lax.axis_index("gy")
    loads = {
        name: pltpu.make_async_copy(ref, getattr(r, name), r.loads.at[k])
        for k, (name, ref) in enumerate(zip(INPUTS, inputs))
    }
    for name in sorted(loads, key=lambda name: name != "modulus"):
        loads[name].start()

    def beside(dx, dy):
        return lax.rem(gx + dx + wide, wide), lax.rem(gy + dy + group, group)

    barrier = pltpu.get_barrier_semaphore()
    peers = [(dx, dy) for dx, dy, _, _, _ in FIRST_PLAN]
    peers += [(k, 0) for k in range(2, wide - 1)] + [(0, k) for k in range(2, group - 1)]
    for dx, dy in peers:
        pl.semaphore_signal(barrier, inc=1, device_id=beside(dx, dy), device_id_type=MESH)

    def copy_of(kind, source, target, device, turn=0):
        k = KINDS[kind] + turn
        return pltpu.make_async_remote_copy(
            src_ref=source,
            dst_ref=target,
            send_sem=r.sends.at[k],
            recv_sem=r.receives.at[k],
            device_id=device,
            device_id_type=MESH,
        )

    def all_of(kind, turn=0):
        buffers = {"modulus": r.modulus_in, "halo": r.halo_in, "halo_next": r.halo_in_next}
        if kind in buffers:
            part = buffers[kind]
        elif kind in ("slaves", "masters"):
            part = (r.slaves_in if kind == "slaves" else r.masters_in).at[turn]
            part = part.at[pl.ds(0, group - 1)]
        elif kind == "across":
            part = r.across.at[pl.ds(0, wide - 1)]
        else:
            part = (r.bundle if kind == "packed" else r.along).at[pl.ds(0, group - 1)]
        return copy_of(kind, part, part, beside(0, 1), turn)

    def receive(kind, turn=0):
        all_of(kind, turn).wait_recv()

    def send_halo(plan, source, target, kind):
        for dx, dy, at, rows, _ in plan:
            part = pl.ds(at, rows)
            copy_of(kind, source.at[part], target.at[part], beside(dx, dy)).start()

    side = math.isqrt(group)
    offsets = [(dy, dx) for dy in range(side) for dx in range(side) if dy or dx]
    offsets.sort(key=lambda offset: -sum(min(d, side - d) for d in offset))

    def across_square(dy, dx):
        row, column = lax.rem(gy // side + dy, side), lax.rem(lax.rem(gy, side) + dx, side)
        return row * side + column

    def send_block(source, target, kind, to, turn):
        copy_of(kind, source.at[to], target.at[gy], (gx, to), turn).start()

    def send_blocks(source, target, kind, turn=0):
        for offset in offsets:
            send_block(source, target, kind, across_square(*offset), turn)
        target[gy] = source[gy]

    def in_turn(n):
        return across_square(side // 2 + side - n // side, lax.rem(n, side))

    r.wide[...] = jnp.zeros_like(r.wide)
    r.mass_wide[...] = jnp.zeros_like(r.mass_wide)
    r.wide_mod[...] = jnp.zeros_like(r.wide_mod)
    r.masters_out[...] = jnp.zeros_like(r.masters_out)
    loads["modulus"].wait()
    lay_out([r.modulus], 4, r.own, r.swapped)
    pack_halo(MODULUS_PLAN, r.own, r.modulus_out)
    pl.semaphore_wait(barrier, len(peers))
    send_halo(MODULUS_PLAN, r.modulus_out, r.modulus_in, "modulus")
    loads["seed"].wait()
    loads["mass"].wait()
    lay_out([r.seed, r.mass], 0, r.own, r.swapped)
    pack_halo(FIRST_PLAN, r.own, r.halo_out)
    send_halo(FIRST_PLAN, r.halo_out, r.halo_in, "halo")
    for name in INPUTS[3:]:
        loads[name].wait()
    place_segments(
        group,
        r.pair,
        r.slave_nodes,
        r.slave_weights,
        r.master_nodes,
        r.master_weights,
        r.penalty,
        r.packed,
        r.segments,
        r.places,
    )
    send_blocks(r.packed, r.bundle, "packed")

    for i in range(3):
        widen_own(r.own, i, r.wide, i)
    widen_own(r.own, 3, r.mass_wide, 0)
    for x in range(4):
        r.wide_mod[pl.ds(8 * (x + 2) + 2, 4), :] = r.own[pl.ds(4 * 64 + 4 * x, 4), :]

    def store_modulus(array, parity, start, count, stride, value):
        r.wide_mod[rows_of(start, count, stride), :] = value

    receive("modulus")
    unpack_halo(MODULUS_PLAN, extents, r.modulus_in, store_modulus)
    r.wide_mod_up[...] = shift_down(r.wide_mod[...])
    diagonal_into(r.out, r.wide_mod, r.wide_mod_up)
    for i in range(3):
        narrow(r.out, i, r.inverse, i)
    mass = r.own[192:256, :]
    r.inverse[...] = 1.0 / (r.inverse[...] + jnp.concatenate([mass, mass, mass], axis=0))
    r.vectors[0] = r.own[0:192, :] * r.inverse[...]

    def store(array, parity, start, count, stride, value):
        at = rows_of(start, count, stride)
        if array < 3:
            r.wide[array, parity, at, :] = value
        else:
            r.mass_wide[0, parity, at, :] = value

    def apply(turn, carry):
        begins, ends = turn == 0, turn == 1
        mine = r.mine.at[turn]
        slaves_out, slaves_in = r.slaves_out.at[turn], r.slaves_in.at[turn]
        masters_out, masters_in = r.masters_out.at[turn], r.masters_in.at[turn]
        table = table_of(r.vectors[turn])
        gather_slaves(table, r.segments, mine, slaves_out, r.places, group)
        send_blocks(slaves_out, slaves_in, "slaves", turn)

        @pl.when(begins)
        def _segments():
            receive("packed")

        half = group // 2

        def masters(k, carry):
            first = half * k
            gather_masters(table_of(r.vectors[turn]), r.bundle, masters_out, in_turn, first, half)

            @pl.when(k == 0)
            def _other():
                send_block(masters_out, masters_in, "masters", in_turn(first), turn)

            for j in range(1, half):
                send_block(masters_out, masters_in, "masters", in_turn(first + j), turn)
            return carry

        lax.fori_loop(0, 2, masters, 0)
        masters_in[gy] = masters_out[gy]

        @pl.when(begins)
        def _first():
            receive("halo")
            unpack_halo(FIRST_PLAN, extents, r.halo_in, store)
            for i in range(3):
                for parity in range(4):
                    wide_mass = r.mass_wide[0, parity]
                    entry = r.out[i, parity] + wide_mass
                    inverse = jnp.where(wide_mass > 0.0, 1.0 / entry, 0.0)
                    r.wide[i, parity] = r.wide[i, parity] * inverse

        @pl.when(ends)
        def _next():
            for i in range(3):
                widen_own(r.vectors.at[1], i, r.wide, i)
            receive("halo_next")
            unpack_halo(NEXT_PLAN, extents, r.halo_in_next, store)

        lift(r.wide, r.wide_up, r.wide_mid)
        stiffness_into(r.out, r.wide, r.wide_up, r.wide_mid, r.wide_mod, r.wide_mod_up)
        applied = r.applied.at[turn]
        for i in range(3):
            narrow(r.out, i, applied, i)
        mass = r.own[192:256, :]
        applied[...] += jnp.concatenate([mass, mass, mass], axis=0) * r.vectors[turn]
        receive("slaves", turn)

        @pl.when(ends)
        def _sums():
            scaled = r.vectors[1]
            r.tile[0:1, :] = inner(r.own[0:192, :], r.vectors[0])
            r.tile[1:2, :] = inner(r.vectors[0], r.applied[0])
            r.tile[2:3, :] = inner(scaled, r.applied[0])
            r.tile[4:8, :] = jnp.zeros((4, 128), F32)
            pressed = jnp.zeros((3, CAP), F32)
            for source in range(group):
                gap = r.masters_out[1, source, 0:3, :] - r.slaves_in[1, source, 0:3, :]
                pressed = pressed + r.bundle[source, 4:5, :] * gap * gap
            pressed = jnp.sum(pressed, axis=0, keepdims=True)
            energy = inner(scaled, r.applied[1])
            for k in range(CAP // 128):
                energy = energy + pressed[:, 128 * k : 128 * (k + 1)]
            r.tile[3:4, :] = energy
            for k in range(1, wide):
                copy_of("across", r.tile, r.across.at[gx], beside(k, 0)).start()
            r.across[gx] = r.tile[...]

        r.total[...] = jnp.zeros_like(r.total)

        def pushes(k, carry):
            scatter_masters(r.total, r.bundle, masters_out, slaves_in, half * k, half)

            @pl.when(jnp.logical_and(ends, k == 0))
            def _along():
                receive("across")
                part = jnp.sum(r.across[...], axis=0)
                r.middle[...] = part
                for offset in offsets:
                    device = (gx, across_square(*offset))
                    copy_of("along", r.middle, r.along.at[gy], device).start()
                r.along[gy] = part

            return carry

        lax.fori_loop(0, 2, pushes, 0)
        receive("masters", turn)
        pull_slaves(r.segments, mine, masters_in, r.places, r.pulls, group)
        scatter_slaves(r.total, r.segments, r.pulls)
        applied[...] += total_rows(r.total)

        @pl.when(begins)
        def _scaled():
            r.vectors[1] = r.applied[0] * r.inverse[...]
            pack_halo(NEXT_PLAN, r.vectors.at[1], r.halo_out_next)
            send_halo(NEXT_PLAN, r.halo_out_next, r.halo_in_next, "halo_next")

        return carry

    lax.fori_loop(0, 2, apply, 0)
    seed, direction, scaled = r.own[0:192, :], r.vectors[0], r.vectors[1]
    applied, again = r.applied[0], r.applied[1]
    receive("along")
    totals = jnp.sum(jnp.sum(r.along[...], axis=0), axis=1, keepdims=True)
    first, second, third, fourth = (totals[k : k + 1] for k in range(4))
    step = first / second
    later = step * step * third - first
    grown = 1.0 + later / first
    curved = grown * grown * second - 2.0 * step * grown * third + step * step * fourth
    step_next = later / curved
    forward = step + step_next * grown
    aside = step_next * step
    results[0:192, :] = forward * direction - aside * scaled
    results[192:384, :] = seed - forward * applied + aside * again
    for kind in KINDS:
        for turn in range(2 if kind in ("slaves", "masters") else 1):
            all_of(kind, turn).wait_send()


def finish_kernel(results, adjoint, residual):
    values = reorder(results[...], False)
    for value, ref in ((values[0:192], adjoint), (values[192:384], residual)):
        for i in range(3):
            for x in range(8):
                for py in range(2):
                    row = i * 64 + (x % 2 * 2 + py) * 16 + x // 2 * 4
                    ref[i, x, pl.ds(py, 4, stride=2), :] = value[row : row + 4]


def shards(
    seed_grad,
    modulus,
    lumped_mass,
    pair_dest,
    slave_nodes,
    slave_weights,
    master_nodes,
    master_weights,
    penalty,
):
    extents = (lax.axis_size("gx"), lax.axis_size("gy"))
    count = penalty.shape[0]
    args = (
        seed_grad,
        modulus,
        lumped_mass,
        pair_dest.reshape(1, count),
        slave_nodes,
        slave_weights,
        master_nodes,
        master_weights,
        penalty.reshape(1, count),
    )
    scratch = scratch_of(extents, args)
    results = pl.pallas_call(
        functools.partial(whole_kernel, extents, tuple(scratch)),
        out_shape=jax.ShapeDtypeStruct((384, 128), F32),
        in_specs=[pl.BlockSpec(memory_space=pl.ANY)] * len(args),
        out_specs=VMEM,
        scratch_shapes=list(scratch.values()),
        compiler_params=pltpu.CompilerParams(
            collective_id=1, has_side_effects=True, vmem_limit_bytes=LIMIT
        ),
        name="conjugate_gradients",
    )(*args)
    field = jax.ShapeDtypeStruct(seed_grad.shape, F32)
    return tuple(
        pl.pallas_call(
            finish_kernel,
            out_shape=[field, field],
            in_specs=[VMEM],
            out_specs=[VMEM, VMEM],
            compiler_params=pltpu.CompilerParams(vmem_limit_bytes=LIMIT),
            name="finish",
        )(results)
    )


def solution(mesh):
    placed = (
        P(None, "gx", "gy", None),
        P("gx", "gy", None),
        P("gx", "gy", None),
        P(("gx", "gy"), None),
        P(None, ("gx", "gy")),
        P(None, ("gx", "gy")),
        P(None, ("gx", "gy")),
        P(None, ("gx", "gy")),
        P(("gx", "gy")),
    )
    return jax.shard_map(
        shards,
        mesh=mesh,
        in_specs=placed,
        out_specs=(P(None, "gx", "gy", None), P(None, "gx", "gy", None)),
        check_vma=False,
    )
```

```python
import functools
import math

import jax
import jax.numpy as jnp
import numpy as np
from jax import lax
from jax.experimental import pallas as pl
from jax.experimental.pallas import tpu as pltpu
from jax.sharding import PartitionSpec as P

CAP = 256
SHEAR = 1.0 / 2.6
LAME = 0.3 / 0.52
MESH = pl.DeviceIdType.MESH
F32 = jnp.float32
BF16 = jnp.bfloat16
VMEM = pl.BlockSpec(memory_space=pltpu.VMEM)
LIMIT = 64 * 1024 * 1024

WIDE = 72


def shape_tables():
    abscissa = 1.0 / math.sqrt(3.0)
    points = [
        (a, b, c)
        for a in (-abscissa, abscissa)
        for b in (-abscissa, abscissa)
        for c in (-abscissa, abscissa)
    ]
    offsets = [
        (i, j, k)
        for i in range(3)
        for j in range(3)
        for k in range(3)
        if (i == 1) + (j == 1) + (k == 1) <= 1
    ]
    derivative = np.zeros((8, 3, 20))
    for g, location in enumerate(points):
        for n, offset in enumerate(offsets):
            natural = [offset[d] - 1 for d in range(3)]
            factors = [
                1.0 - location[d] ** 2 if natural[d] == 0 else 1.0 + location[d] * natural[d]
                for d in range(3)
            ]
            slopes = [
                -2.0 * location[d] if natural[d] == 0 else float(natural[d]) for d in range(3)
            ]
            linear = sum(location[d] * natural[d] for d in range(3)) - 2.0
            for d in range(3):
                others = factors[(d + 1) % 3] * factors[(d + 2) % 3]
                if 0 in natural:
                    derivative[g, d, n] = slopes[d] * others / 4.0
                else:
                    derivative[g, d, n] = natural[d] * others * (linear + factors[d]) / 8.0
    return derivative, offsets


def signs(count, dims):
    table = np.ones((count, count))
    for t in range(count):
        for c in range(count):
            for d in range(dims):
                if t >> d & 1 and not c >> d & 1:
                    table[t, c] = -table[t, c]
    return table


def element_tables():
    derivative, offsets = shape_tables()
    eight, four = signs(8, 3), signs(4, 2)
    modal = np.einsum("sg,gan->asn", eight, derivative) / 8.0
    corner_at = [offsets.index((c >> 2 << 1, (c >> 1 & 1) << 1, (c & 1) << 1)) for c in range(8)]
    edge_at = []
    for d in range(3):
        row = []
        for c in range(4):
            offset = [(c >> 1) << 1, (c & 1) << 1]
            offset.insert(d, 1)
            row.append(offsets.index(tuple(offset)))
        edge_at.append(row)
    corner_terms = np.einsum("tn,asn->ast", eight, modal[:, :, corner_at]) / 8.0
    edge_terms = [np.einsum("tn,asn->ast", four, modal[:, :, edge_at[d]]) / 4.0 for d in range(3)]
    trilinear = np.array([(1.0 / math.sqrt(3.0)) ** bin(t).count("1") / 8.0 for t in range(8)])
    at_points = np.einsum("t,tg->gt", trilinear, eight)
    squares = derivative * derivative
    weight = np.einsum(
        "gt,gni->tni",
        at_points,
        SHEAR * squares.sum(axis=1)[:, :, None] + (LAME + SHEAR) * np.swapaxes(squares, 1, 2),
    )
    corner_diag = np.einsum("un,tni->uti", eight, weight[:, corner_at]) / 8.0
    edge_diag = [np.einsum("un,tni->uti", four, weight[:, edge_at[d]]) / 4.0 for d in range(3)]
    return corner_terms, edge_terms, trilinear, corner_diag, edge_diag


def split_sums(values):
    values = list(values)
    step = 1
    while step < len(values):
        for low in range(len(values)):
            if not low & step:
                a, b = values[low], values[low | step]
                values[low], values[low | step] = b + a, b - a
        step *= 2
    return values


def join_sums(values):
    values = list(values)
    step = 1
    while step < len(values):
        for low in range(len(values)):
            if not low & step:
                a, b = values[low], values[low | step]
                values[low], values[low | step] = a - b, a + b
        step *= 2
    return values


def combine(terms):
    total = None
    for factor, value in terms:
        if abs(factor) < 1e-12:
            continue
        term = value * np.float32(factor)
        total = term if total is None else total + term
    return total


def rows_at(group, shift):
    return pl.ds(pl.multiple_of(8 * group, 8) + shift, 8)


def lanes(rows):
    return lax.broadcasted_iota(jnp.int32, (rows, 128), 1)


def shift_down(value):
    return jnp.where(lanes(value.shape[0]) == 63, 0.0, pltpu.roll(value, 127, 1))


def collect(low, middle, high):
    total = low + jnp.where(lanes(8) < 64, pltpu.roll(high, 1, 1), 0.0)
    if middle is not None:
        total = total + pltpu.roll(middle, 64, 1)
    return total


def corner_moduli(wide_mod, wide_mod_up, group):
    values = []
    for c in range(8):
        ref = wide_mod_up if c & 1 else wide_mod
        values.append(ref[rows_at(group + (c >> 2), c >> 1 & 1), :])
    inside = lanes(8) < 64
    return split_sums([jnp.where(inside, value, 0.0) for value in values])


def edge_corner(d, c):
    where = [c >> 1, c & 1]
    where.insert(d, None)
    return where


def add_rows(ref, index, row, value):
    ref[index + (row, slice(None))] += value


def scatter_forces(out, i, corner, edges, group):
    for xy in range(4):
        row = rows_at(group + (xy >> 1), xy & 1)
        add_rows(out, (i, 0), row, collect(corner[2 * xy], edges[2][xy], corner[2 * xy + 1]))
    for y in range(2):
        add_rows(
            out, (i, 2), rows_at(group, y), collect(edges[0][2 * y], None, edges[0][2 * y + 1])
        )
    for x in range(2):
        add_rows(
            out, (i, 1), rows_at(group + x, 0), collect(edges[1][2 * x], None, edges[1][2 * x + 1])
        )


def diagonal_into(out, wide_mod, wide_mod_up):
    corner_diag, edge_diag = element_tables()[3:]
    out[...] = jnp.zeros_like(out)

    def step(group, carry):
        moduli = corner_moduli(wide_mod, wide_mod_up, group)
        for i in range(3):
            corner = join_sums(
                [
                    combine([(corner_diag[u, t, i], moduli[t]) for t in range(8)])
                    for u in range(8)
                ]
            )
            edges = [
                join_sums(
                    [
                        combine([(edge_diag[d][u, t, i], moduli[t]) for t in range(8)])
                        for u in range(4)
                    ]
                )
                for d in range(3)
            ]
            scatter_forces(out, i, corner, edges, group)
        return carry

    lax.fori_loop(0, 7, step, 0, unroll=7)


def stiffness_into(out, wide, wide_up, wide_mid, wide_mod, wide_mod_up):
    corner_terms, edge_terms, trilinear = element_tables()[:3]
    out[...] = jnp.zeros_like(out)

    def step(group, carry):
        moduli = corner_moduli(wide_mod, wide_mod_up, group)
        points = join_sums([moduli[t] * np.float32(trilinear[t]) for t in range(8)])
        slopes = []
        for i in range(3):
            corner = []
            for c in range(8):
                ref = wide_up if c & 1 else wide
                corner.append(ref[i, 0, rows_at(group + (c >> 2), c >> 1 & 1), :])
            corner = split_sums(corner)
            edges = []
            for d in range(3):
                values = []
                for c in range(4):
                    x, y, z = edge_corner(d, c)
                    row = rows_at(group + (x or 0), y or 0)
                    parity = (2, 1, 0)[d]
                    if d == 2:
                        values.append(wide_mid[i, row, :])
                    else:
                        values.append((wide_up if z else wide)[i, parity, row, :])
                edges.append(split_sums(values))
            slopes.append(
                [
                    [
                        combine(
                            [(corner_terms[a, s, t], corner[t]) for t in range(8)]
                            + [
                                (edge_terms[d][a, s, t], edges[d][t])
                                for d in range(3)
                                for t in range(4)
                            ]
                        )
                        for s in range(8)
                    ]
                    for a in range(3)
                ]
            )

        def plus(a, b):
            return a if b is None else b if a is None else a + b

        zero = jnp.zeros((8, 128), F32)
        strain = {}
        for a in range(3):
            strain[a, a] = slopes[a][a]
            for b in range(a):
                strain[b, a] = [plus(p, q) for p, q in zip(slopes[a][b], slopes[b][a])]
        strain = {
            key: join_sums([zero if v is None else v for v in value])
            for key, value in strain.items()
        }
        stress = {key: [] for key in strain}
        for g in range(8):
            volume = (strain[0, 0][g] + strain[1, 1][g] + strain[2, 2][g]) * np.float32(LAME)
            for a in range(3):
                stress[a, a].append(
                    points[g] * (volume + strain[a, a][g] * np.float32(2.0 * SHEAR))
                )
            scaled = points[g] * np.float32(SHEAR)
            for key in ((0, 1), (0, 2), (1, 2)):
                stress[key].append(scaled * strain[key][g])
        stress = {key: split_sums(value) for key, value in stress.items()}
        for i in range(3):
            pairs = [
                (a, s, stress[min(a, i), max(a, i)][s]) for a in range(3) for s in range(8)
            ]
            corner = join_sums(
                [combine([(corner_terms[a, s, t], v) for a, s, v in pairs]) for t in range(8)]
            )
            edges = [
                join_sums(
                    [combine([(edge_terms[d][a, s, t], v) for a, s, v in pairs]) for t in range(4)]
                )
                for d in range(3)
            ]
            scatter_forces(out, i, corner, edges, group)
        return carry

    lax.fori_loop(1, 6, step, 0, unroll=5)


def lift(wide, wide_up, wide_mid):
    for i in range(3):
        for parity in range(3):
            wide_up[i, parity] = shift_down(wide[i, parity])
        wide_mid[i] = pltpu.roll(wide[i, 0], 64, 1)


def halo_plan(fields, modulus=None):
    plan, first = [], 0
    for dx in (-1, 0, 1):
        for dy in (-1, 0, 1):
            if dx == 0 and dy == 0:
                continue
            pieces = []

            def places(step, both):
                if step == 1:
                    return [(p, 3, 1) for p in ((0, 1) if both else (0,))]
                return [(0, 0, 6)]

            def strips(array, xs, ys):
                for px, ox, wx in xs:
                    for py, oy, wy in ys:
                        if ox is None:
                            pieces.append((array, px * 2 + py, oy, 4, 4, 8 * 2 + wy, 8))
                        elif oy is None:
                            pieces.append((array, px * 2 + py, 4 * ox, 4, 1, 8 * wx + 2, 1))
                        else:
                            pieces.append((array, px * 2 + py, 4 * ox + oy, 1, 1, 8 * wx + wy, 1))

            every = [(0, None, None), (1, None, None)]
            for array in range(fields):
                strips(
                    array,
                    every if dx == 0 else places(dx, True),
                    every if dy == 0 else places(dy, True),
                )
            if modulus is not None:
                deep = {1: [(0, 3, 1), (0, 2, 0)], -1: [(0, 0, 6), (0, 1, 7)], 0: every[:1]}
                strips(modulus, deep[dx], deep[dy])
            rows = sum(piece[3] for piece in pieces)
            plan.append((dx, dy, first, -(-rows // 8) * 8, pieces))
            first += plan[-1][3]
    return plan, first


MODULUS_PLAN, MODULUS_ROWS = halo_plan(0, 4)
FIRST_PLAN, FIRST_ROWS = halo_plan(4)
NEXT_PLAN, NEXT_ROWS = halo_plan(3)


def rows_of(start, count, stride):
    return pl.ds(start, count) if stride == 1 else pl.ds(start, count, stride=stride)


def pack_halo(plan, own, message):
    message[...] = jnp.zeros_like(message)
    for _, _, first, _, pieces in plan:
        at = first
        for array, parity, start, count, stride, _, _ in pieces:
            source = own[rows_of(array * 64 + parity * 16 + start, count, stride), :]
            message[pl.ds(at, count), :] = source
            at += count


def unpack_halo(plan, extents, message, store):
    gx, gy = lax.axis_index("gx"), lax.axis_index("gy")
    for dx, dy, first, _, pieces in plan:
        inside = None
        for step, at, extent in ((dx, gx, extents[0]), (dy, gy, extents[1])):
            if step:
                here = at > 0 if step == 1 else at < extent - 1
                inside = here if inside is None else jnp.logical_and(inside, here)
        keep = jnp.where(inside, 1.0, 0.0).astype(F32)
        at = first
        for array, parity, _, count, _, start, stride in pieces:
            store(array, parity, start, count, stride, message[pl.ds(at, count), :] * keep)
            at += count


def widen_own(own, array, wide, i):
    for parity in range(4):
        for x in range(4):
            wide[i, parity, pl.ds(8 * (x + 2) + 2, 4), :] = own[
                pl.ds(array * 64 + parity * 16 + 4 * x, 4), :
            ]


def narrow(wide, i, own, array):
    for parity in range(4):
        for x in range(4):
            own[pl.ds(array * 64 + parity * 16 + 4 * x, 4), :] = wide[
                i, parity, pl.ds(8 * (x + 2) + 2, 4), :
            ]


def in_two(value):
    head = value.astype(BF16)
    return head, (value - head.astype(F32)).astype(BF16)


def down_iota(rows, columns):
    return lax.broadcasted_iota(jnp.int32, (rows, columns), 0).astype(F32).astype(BF16)


def ones_where(rows, labels):
    columns = labels.shape[1]
    return jnp.where(
        down_iota(rows, columns) == labels.astype(BF16), jnp.ones((), BF16), jnp.zeros((), BF16)
    )


def dot(a, b, transposed=False):
    return lax.dot_general(
        a, b, (((1,), (1 if transposed else 0,)), ((), ())), preferred_element_type=F32
    )


BLOCK = CAP
GATHER_UNROLL = 8
SCATTER_UNROLL = 4


def picks_of(lane, extent):
    return jnp.concatenate([ones_where(extent, lane[j : j + 1]) for j in range(4)], axis=1)


def gather_block(table, block):
    count = block.shape[1]
    picks = picks_of(block[12:16], 128)
    found = dot(table, jnp.concatenate([picks, picks], axis=0))
    down = lax.broadcasted_iota(jnp.int32, (64, count), 0).astype(F32)
    factors = [
        jnp.where(down == block[8 + j : 9 + j], block[j : j + 1], 0.0) for j in range(4)
    ]
    result = []
    for i in range(3):
        total = sum(
            factors[j] * found[64 * i : 64 * (i + 1), count * j : count * (j + 1)]
            for j in range(4)
        )
        result.append(jnp.sum(total, axis=0, keepdims=True))
    return jnp.concatenate(result, axis=0)


def scatter_block(block, traction):
    upper = jnp.where(block[8:12] >= 32.0, 1.0, 0.0)
    row, lane = block[8:12] - 32.0 * upper, block[12:16] + 128.0 * upper
    rows = [ones_where(32, row[j : j + 1]) for j in range(4)]
    parts = [
        [in_two(block[j : j + 1] * traction[i : i + 1]) for j in range(4)] for i in range(3)
    ]
    left = [
        jnp.concatenate([rows[j] * parts[i][j][part] for j in range(4)], axis=1)
        for part in range(2)
        for i in range(3)
    ]
    return dot(jnp.concatenate(left, axis=0), picks_of(lane, 256), True)


def total_rows(total):
    value = total[0:96, :] + total[96:192, :]
    return jnp.concatenate(
        [
            value[32 * i : 32 * (i + 1), 128 * half : 128 * (half + 1)]
            for i in range(3)
            for half in range(2)
        ],
        axis=0,
    )


def table_of(value):
    head, tail = in_two(value)
    return jnp.concatenate([head, tail], axis=1)


def each(first, last, body, unroll):
    def step(k, carry):
        body(k)
        return carry

    lax.fori_loop(first, last, step, 0, unroll=unroll)


def gather_slaves(table, segments, mine, theirs, places, group):
    mine[...] = jnp.zeros_like(mine)

    def slave(k):
        at = pl.ds(pl.multiple_of(k * BLOCK, BLOCK), BLOCK)
        mine[0:3, at] = gather_block(table, segments[:, at])

    each(0, segments.shape[1] // BLOCK, slave, 4)
    head, tail = in_two(mine[...])
    both = jnp.concatenate([head, tail], axis=0)
    target = segments[5:6, :]
    left = jnp.concatenate(
        [jnp.where(target == t, 1.0, 0.0).astype(BF16) * both for t in range(group)], axis=0
    )
    placed = dot(left, places[...], True).reshape(group, 16, CAP)
    theirs[...] = placed[:, 0:4] + placed[:, 8:12]


def gather_masters(table, bundle, theirs, place, first, count):
    def master(k):
        source = place(first + k)
        theirs[source, 0:3, :] = gather_block(table, bundle[source])

    each(0, count, master, GATHER_UNROLL)


def pull_slaves(segments, mine, returned, places, pulls, group):
    nothing = jnp.zeros((4, CAP), F32)
    slots = jnp.concatenate([v for t in range(group) for v in (returned[t], nothing)], axis=0)
    head, tail = in_two(slots)
    found = dot(
        jnp.concatenate([head, tail], axis=1),
        jnp.concatenate([places[...], places[...]], axis=0),
    )
    target = segments[5:6, :]
    back = sum(jnp.where(target == t, 1.0, 0.0) * found[8 * t : 8 * (t + 1)] for t in range(group))
    pulls[0:3, :] = segments[4:5, :] * (mine[0:3, :] - back[0:3, :])


def scatter_slaves(total, segments, pulls):
    def slave(k):
        at = pl.ds(pl.multiple_of(k * 2 * BLOCK, 2 * BLOCK), 2 * BLOCK)
        total[...] += scatter_block(segments[:, at], pulls[0:3, at])

    each(0, segments.shape[1] // (2 * BLOCK), slave, 2)


def scatter_masters(total, bundle, sent, arrived, first, count):
    def master(k):
        pair = [first + 2 * k, first + 2 * k + 1]
        block = jnp.concatenate([bundle[source] for source in pair], axis=1)
        gap = [sent[source, 0:3, :] - arrived[source, 0:3, :] for source in pair]
        total[...] += scatter_block(block, block[4:5] * jnp.concatenate(gap, axis=1))

    each(0, count // 2, master, SCATTER_UNROLL)


def swap_lanes(forth):
    a = lax.broadcasted_iota(jnp.int32, (128, 128), 0 if forth else 1)
    b = lax.broadcasted_iota(jnp.int32, (128, 128), 1 if forth else 0)
    return jnp.where(b == (a % 2) * 64 + a // 2, 1.0, 0.0).astype(F32)


def reorder(value, forth):
    head = value.astype(BF16)
    rest = value - head.astype(F32)
    middle = rest.astype(BF16)
    tail = (rest - middle.astype(F32)).astype(BF16)
    swap = swap_lanes(forth).astype(BF16)
    return dot(
        jnp.concatenate([head, middle, tail], axis=1), jnp.concatenate([swap, swap, swap], axis=0)
    )


def lay_out(fields, first, own, swapped):
    values = [field[...].reshape(-1, 128) for field in fields]
    value = reorder(values[0] if len(values) == 1 else jnp.concatenate(values, axis=0), True)
    count = value.shape[0] // 64
    swapped[pl.ds(first, count)] = value.reshape(count, 8, 8, 128)
    for array in range(first, first + count):
        for x in range(8):
            for py in range(2):
                row = array * 64 + (x % 2 * 2 + py) * 16 + x // 2 * 4
                own[pl.ds(row, 4), :] = swapped[array, x, pl.ds(py, 4, stride=2), :]


def place_of(node):
    x, y, z = node // 1024, node // 128 % 8, node % 128
    row = (x % 2 * 2 + y % 2) * 16 + x // 2 * 4 + y // 2
    return row.astype(F32), (z % 2 * 64 + z // 2).astype(F32)


def place_segments(
    group,
    pair,
    slave_nodes,
    slave_weights,
    master_nodes,
    master_weights,
    penalty,
    packed,
    segments,
    places,
):
    slave_row, slave_lane = place_of(slave_nodes[...])
    master_row, master_lane = place_of(master_nodes[...])
    target = pair[...].astype(F32)
    count = target.shape[1]
    chosen = ones_where(group, target)
    a = lax.broadcasted_iota(jnp.int32, (128, 128), 0)
    b = lax.broadcasted_iota(jnp.int32, (128, 128), 1)
    before = jnp.where(a < b, 1.0, 0.0).astype(BF16)
    ranks, base = [], jnp.zeros((group, 1), F32)
    for k in range(count // 128):
        part = chosen[:, 128 * k : 128 * (k + 1)]
        wide = part.astype(F32)
        rank = dot(part, before) + base
        ranks.append(jnp.sum(rank * wide, axis=0, keepdims=True))
        base = base + jnp.sum(wide, axis=1, keepdims=True)
    position = jnp.concatenate(ranks, axis=1)
    segments[0:4, :] = slave_weights[...]
    segments[4:5, :] = penalty[...]
    segments[5:6, :] = target
    segments[6:7, :] = position
    segments[7:8, :] = jnp.zeros_like(position)
    segments[8:12, :] = slave_row
    segments[12:16, :] = slave_lane
    spots = ones_where(CAP, position)
    places[...] = spots
    nothing = jnp.zeros((3, count), F32)
    values = jnp.concatenate([master_weights[...], penalty[...], nothing], axis=0)
    head, tail = in_two(values)
    nodes = jnp.concatenate([master_row, master_lane], axis=0)
    sent = jnp.concatenate([head, tail, nodes.astype(BF16), jnp.zeros((8, count), BF16)], axis=0)
    left = jnp.concatenate(
        [jnp.where(target == t, 1.0, 0.0).astype(BF16) * sent for t in range(group)], axis=0
    )
    placed = dot(left, spots, True).reshape(group, 32, CAP)
    packed[:, 0:8] = placed[:, 0:8] + placed[:, 8:16]
    packed[:, 8:16] = placed[:, 16:24]


def inner(a, b):
    return jnp.sum(a * b, axis=0, keepdims=True)


INPUTS = (
    "seed",
    "modulus",
    "mass",
    "pair",
    "slave_nodes",
    "slave_weights",
    "master_nodes",
    "master_weights",
    "penalty",
)


KINDS = {
    "modulus": 0,
    "halo": 1,
    "packed": 2,
    "slaves": 3,
    "masters": 5,
    "halo_next": 7,
    "across": 8,
    "along": 9,
}


def scratch_of(extents, args):
    group, count = extents[1], args[-1].shape[-1]
    dma, parts, field = pltpu.SemaphoreType.DMA, (group, 4, CAP), (3, 4, WIDE, 128)
    room = {name: pltpu.VMEM(arg.shape, arg.dtype) for name, arg in zip(INPUTS, args)}
    shapes = {
        "own": (320, 128),
        "swapped": (5, 8, 8, 128),
        "segments": (16, count),
        "packed": (group, 16, CAP),
        "bundle": (group, 16, CAP),
        "modulus_out": (MODULUS_ROWS, 128),
        "modulus_in": (MODULUS_ROWS, 128),
        "halo_out": (FIRST_ROWS, 128),
        "halo_in": (FIRST_ROWS, 128),
        "halo_out_next": (NEXT_ROWS, 128),
        "halo_in_next": (NEXT_ROWS, 128),
        "mine": (2, 8, count),
        "slaves_out": (2,) + parts,
        "slaves_in": (2,) + parts,
        "masters_out": (2,) + parts,
        "masters_in": (2,) + parts,
        "vectors": (2, 192, 128),
        "applied": (2, 192, 128),
        "inverse": (192, 128),
        "wide_mod": (WIDE, 128),
        "wide_mod_up": (WIDE, 128),
        "mass_wide": (1, 4, WIDE, 128),
        "wide": field,
        "wide_up": (3, 3, WIDE, 128),
        "wide_mid": (3, WIDE, 128),
        "out": field,
        "total": (192, 256),
        "pulls": (8, count),
        "tile": (8, 128),
        "middle": (8, 128),
        "across": (extents[0], 8, 128),
        "along": (group, 8, 128),
    }
    room.update({name: pltpu.VMEM(shape, F32) for name, shape in shapes.items()})
    room["places"] = pltpu.VMEM((CAP, count), BF16)
    room["loads"] = dma((len(INPUTS),))
    room["sends"] = dma((10,))
    room["receives"] = dma((10,))
    return room


class Refs:
    def __init__(self, names, refs):
        self.__dict__.update(zip(names, refs))


def whole_kernel(extents, names, *refs):
    inputs, results = refs[: len(INPUTS)], refs[len(INPUTS)]
    r = Refs(names, refs[len(INPUTS) + 1 :])
    wide, group = extents
    gx, gy = lax.axis_index("gx"), lax.axis_index("gy")
    loads = {
        name: pltpu.make_async_copy(ref, getattr(r, name), r.loads.at[k])
        for k, (name, ref) in enumerate(zip(INPUTS, inputs))
    }
    for name in sorted(loads, key=lambda name: name != "modulus"):
        loads[name].start()

    def beside(dx, dy):
        return lax.rem(gx + dx + wide, wide), lax.rem(gy + dy + group, group)

    barrier = pltpu.get_barrier_semaphore()
    peers = [(dx, dy) for dx, dy, _, _, _ in FIRST_PLAN]
    peers += [(k, 0) for k in range(2, wide - 1)] + [(0, k) for k in range(2, group - 1)]
    for dx, dy in peers:
        pl.semaphore_signal(barrier, inc=1, device_id=beside(dx, dy), device_id_type=MESH)

    def copy_of(kind, source, target, device, turn=0):
        k = KINDS[kind] + turn
        return pltpu.make_async_remote_copy(
            src_ref=source,
            dst_ref=target,
            send_sem=r.sends.at[k],
            recv_sem=r.receives.at[k],
            device_id=device,
            device_id_type=MESH,
        )

    def all_of(kind, turn=0):
        buffers = {"modulus": r.modulus_in, "halo": r.halo_in, "halo_next": r.halo_in_next}
        if kind in buffers:
            part = buffers[kind]
        elif kind in ("slaves", "masters"):
            part = (r.slaves_in if kind == "slaves" else r.masters_in).at[turn]
            part = part.at[pl.ds(0, group - 1)]
        elif kind == "across":
            part = r.across.at[pl.ds(0, wide - 1)]
        else:
            part = (r.bundle if kind == "packed" else r.along).at[pl.ds(0, group - 1)]
        return copy_of(kind, part, part, beside(0, 1), turn)

    def receive(kind, turn=0):
        all_of(kind, turn).wait_recv()

    def send_halo(plan, source, target, kind):
        for dx, dy, at, rows, _ in plan:
            part = pl.ds(at, rows)
            copy_of(kind, source.at[part], target.at[part], beside(dx, dy)).start()

    side = math.isqrt(group)
    offsets = [(dy, dx) for dy in range(side) for dx in range(side) if dy or dx]
    offsets.sort(key=lambda offset: -sum(min(d, side - d) for d in offset))

    def across_square(dy, dx):
        row, column = lax.rem(gy // side + dy, side), lax.rem(lax.rem(gy, side) + dx, side)
        return row * side + column

    def send_block(source, target, kind, to, turn):
        copy_of(kind, source.at[to], target.at[gy], (gx, to), turn).start()

    def send_blocks(source, target, kind, turn=0):
        for offset in offsets:
            send_block(source, target, kind, across_square(*offset), turn)
        target[gy] = source[gy]

    def in_turn(n):
        return across_square(side // 2 + side - n // side, lax.rem(n, side))

    r.wide[...] = jnp.zeros_like(r.wide)
    r.mass_wide[...] = jnp.zeros_like(r.mass_wide)
    r.wide_mod[...] = jnp.zeros_like(r.wide_mod)
    r.masters_out[...] = jnp.zeros_like(r.masters_out)
    loads["modulus"].wait()
    lay_out([r.modulus], 4, r.own, r.swapped)
    pack_halo(MODULUS_PLAN, r.own, r.modulus_out)
    pl.semaphore_wait(barrier, len(peers))
    send_halo(MODULUS_PLAN, r.modulus_out, r.modulus_in, "modulus")
    loads["seed"].wait()
    loads["mass"].wait()
    lay_out([r.seed, r.mass], 0, r.own, r.swapped)
    pack_halo(FIRST_PLAN, r.own, r.halo_out)
    send_halo(FIRST_PLAN, r.halo_out, r.halo_in, "halo")
    for name in INPUTS[3:]:
        loads[name].wait()
    place_segments(
        group,
        r.pair,
        r.slave_nodes,
        r.slave_weights,
        r.master_nodes,
        r.master_weights,
        r.penalty,
        r.packed,
        r.segments,
        r.places,
    )
    send_blocks(r.packed, r.bundle, "packed")

    for i in range(3):
        widen_own(r.own, i, r.wide, i)
    widen_own(r.own, 3, r.mass_wide, 0)
    for x in range(4):
        r.wide_mod[pl.ds(8 * (x + 2) + 2, 4), :] = r.own[pl.ds(4 * 64 + 4 * x, 4), :]

    def store_modulus(array, parity, start, count, stride, value):
        r.wide_mod[rows_of(start, count, stride), :] = value

    receive("modulus")
    unpack_halo(MODULUS_PLAN, extents, r.modulus_in, store_modulus)
    r.wide_mod_up[...] = shift_down(r.wide_mod[...])
    diagonal_into(r.out, r.wide_mod, r.wide_mod_up)
    for i in range(3):
        narrow(r.out, i, r.inverse, i)
    mass = r.own[192:256, :]
    r.inverse[...] = 1.0 / (r.inverse[...] + jnp.concatenate([mass, mass, mass], axis=0))
    r.vectors[0] = r.own[0:192, :] * r.inverse[...]

    def store(array, parity, start, count, stride, value):
        at = rows_of(start, count, stride)
        if array < 3:
            r.wide[array, parity, at, :] = value
        else:
            r.mass_wide[0, parity, at, :] = value

    def apply(turn, carry):
        begins, ends = turn == 0, turn == 1
        mine = r.mine.at[turn]
        slaves_out, slaves_in = r.slaves_out.at[turn], r.slaves_in.at[turn]
        masters_out, masters_in = r.masters_out.at[turn], r.masters_in.at[turn]
        table = table_of(r.vectors[turn])
        gather_slaves(table, r.segments, mine, slaves_out, r.places, group)
        send_blocks(slaves_out, slaves_in, "slaves", turn)

        @pl.when(begins)
        def _segments():
            receive("packed")

        half = group // 2

        def masters(k, carry):
            first = half * k
            gather_masters(table_of(r.vectors[turn]), r.bundle, masters_out, in_turn, first, half)

            @pl.when(k == 0)
            def _other():
                send_block(masters_out, masters_in, "masters", in_turn(first), turn)

            for j in range(1, half):
                send_block(masters_out, masters_in, "masters", in_turn(first + j), turn)
            return carry

        lax.fori_loop(0, 2, masters, 0)
        masters_in[gy] = masters_out[gy]

        @pl.when(begins)
        def _first():
            receive("halo")
            unpack_halo(FIRST_PLAN, extents, r.halo_in, store)
            for i in range(3):
                for parity in range(4):
                    wide_mass = r.mass_wide[0, parity]
                    entry = r.out[i, parity] + wide_mass
                    inverse = jnp.where(wide_mass > 0.0, 1.0 / entry, 0.0)
                    r.wide[i, parity] = r.wide[i, parity] * inverse

        @pl.when(ends)
        def _next():
            for i in range(3):
                widen_own(r.vectors.at[1], i, r.wide, i)
            receive("halo_next")
            unpack_halo(NEXT_PLAN, extents, r.halo_in_next, store)

        lift(r.wide, r.wide_up, r.wide_mid)
        stiffness_into(r.out, r.wide, r.wide_up, r.wide_mid, r.wide_mod, r.wide_mod_up)
        applied = r.applied.at[turn]
        for i in range(3):
            narrow(r.out, i, applied, i)
        mass = r.own[192:256, :]
        applied[...] += jnp.concatenate([mass, mass, mass], axis=0) * r.vectors[turn]

        @pl.when(ends)
        def _early():
            scaled = r.vectors[1]
            r.tile[0:1, :] = inner(r.own[0:192, :], r.vectors[0])
            r.tile[1:2, :] = inner(r.vectors[0], r.applied[0])
            r.tile[2:3, :] = inner(scaled, r.applied[0])
            r.tile[4:8, :] = jnp.zeros((4, 128), F32)
            r.tile[3:4, :] = inner(scaled, r.applied[1])

        receive("slaves", turn)

        @pl.when(ends)
        def _sums():
            pressed = jnp.zeros((3, CAP), F32)
            for source in range(group):
                gap = r.masters_out[1, source, 0:3, :] - r.slaves_in[1, source, 0:3, :]
                pressed = pressed + r.bundle[source, 4:5, :] * gap * gap
            pressed = jnp.sum(pressed, axis=0, keepdims=True)
            energy = r.tile[3:4, :]
            for k in range(CAP // 128):
                energy = energy + pressed[:, 128 * k : 128 * (k + 1)]
            r.tile[3:4, :] = energy
            for k in sorted(range(1, wide), key=lambda k: -min(k, wide - k)):
                copy_of("across", r.tile, r.across.at[gx], beside(k, 0)).start()
            r.across[gx] = r.tile[...]

        r.total[...] = jnp.zeros_like(r.total)

        def pushes(k, carry):
            scatter_masters(r.total, r.bundle, masters_out, slaves_in, half * k, half)

            @pl.when(jnp.logical_and(ends, k == 0))
            def _along():
                receive("across")
                part = jnp.sum(r.across[...], axis=0)
                r.middle[...] = part
                for offset in offsets:
                    device = (gx, across_square(*offset))
                    copy_of("along", r.middle, r.along.at[gy], device).start()
                r.along[gy] = part

            return carry

        lax.fori_loop(0, 2, pushes, 0)
        receive("masters", turn)
        pull_slaves(r.segments, mine, masters_in, r.places, r.pulls, group)
        scatter_slaves(r.total, r.segments, r.pulls)
        applied[...] += total_rows(r.total)

        @pl.when(begins)
        def _scaled():
            r.vectors[1] = r.applied[0] * r.inverse[...]
            pack_halo(NEXT_PLAN, r.vectors.at[1], r.halo_out_next)
            send_halo(NEXT_PLAN, r.halo_out_next, r.halo_in_next, "halo_next")

        return carry

    lax.fori_loop(0, 2, apply, 0)
    seed, direction, scaled = r.own[0:192, :], r.vectors[0], r.vectors[1]
    applied, again = r.applied[0], r.applied[1]
    receive("along")
    totals = jnp.sum(jnp.sum(r.along[...], axis=0), axis=1, keepdims=True)
    first, second, third, fourth = (totals[k : k + 1] for k in range(4))
    step = first / second
    later = step * step * third - first
    grown = 1.0 + later / first
    curved = grown * grown * second - 2.0 * step * grown * third + step * step * fourth
    step_next = later / curved
    forward = step + step_next * grown
    aside = step_next * step
    results[0:192, :] = forward * direction - aside * scaled
    results[192:384, :] = seed - forward * applied + aside * again
    for kind in KINDS:
        for turn in range(2 if kind in ("slaves", "masters") else 1):
            all_of(kind, turn).wait_send()


def finish_kernel(results, adjoint, residual):
    values = reorder(results[...], False)
    for value, ref in ((values[0:192], adjoint), (values[192:384], residual)):
        for i in range(3):
            for x in range(8):
                for py in range(2):
                    row = i * 64 + (x % 2 * 2 + py) * 16 + x // 2 * 4
                    ref[i, x, pl.ds(py, 4, stride=2), :] = value[row : row + 4]


def shards(
    seed_grad,
    modulus,
    lumped_mass,
    pair_dest,
    slave_nodes,
    slave_weights,
    master_nodes,
    master_weights,
    penalty,
):
    extents = (lax.axis_size("gx"), lax.axis_size("gy"))
    count = penalty.shape[0]
    args = (
        seed_grad,
        modulus,
        lumped_mass,
        pair_dest.reshape(1, count),
        slave_nodes,
        slave_weights,
        master_nodes,
        master_weights,
        penalty.reshape(1, count),
    )
    scratch = scratch_of(extents, args)
    results = pl.pallas_call(
        functools.partial(whole_kernel, extents, tuple(scratch)),
        out_shape=jax.ShapeDtypeStruct((384, 128), F32),
        in_specs=[pl.BlockSpec(memory_space=pl.ANY)] * len(args),
        out_specs=VMEM,
        scratch_shapes=list(scratch.values()),
        compiler_params=pltpu.CompilerParams(
            collective_id=1, has_side_effects=True, vmem_limit_bytes=LIMIT
        ),
        name="conjugate_gradients",
    )(*args)
    field = jax.ShapeDtypeStruct(seed_grad.shape, F32)
    return tuple(
        pl.pallas_call(
            finish_kernel,
            out_shape=[field, field],
            in_specs=[VMEM],
            out_specs=[VMEM, VMEM],
            compiler_params=pltpu.CompilerParams(vmem_limit_bytes=LIMIT),
            name="finish",
        )(results)
    )


def solution(mesh):
    placed = (
        P(None, "gx", "gy", None),
        P("gx", "gy", None),
        P("gx", "gy", None),
        P(("gx", "gy"), None),
        P(None, ("gx", "gy")),
        P(None, ("gx", "gy")),
        P(None, ("gx", "gy")),
        P(None, ("gx", "gy")),
        P(("gx", "gy")),
    )
    return jax.shard_map(
        shards,
        mesh=mesh,
        in_specs=placed,
        out_specs=(P(None, "gx", "gy", None), P(None, "gx", "gy", None)),
        check_vma=False,
    )
```
